32 devices in a mesh: dp: 2 (over x), row: 4 (over y, core), col: 4 (over z).
Axes of the slice: x: 2, y: 2, z: 4, core: 2. Of those that a mesh axis runs over, the one named last changes fastest.
Arguments:
- tokens: bfloat16 [4096, 2048], P(('dp', 'col'), 'row'), may hold values from -60 to 60
- segments: int32 [4096], P('dp'), may hold values from 0 to 2047, as said below
- mix_gain: float32 [2048], P('row'), may hold values from 0.5 to 1.5
- w_mix: bfloat16 [2048, 4, 2048], P('row', None, 'col'), may hold values from -0.125 to 0.125
- lower_bound: float32 [2048], P('col'), may hold values from 0.25 to 1
- group_gain: float32 [128], replicated, may hold values from 0.5 to 1.5
- w_out: bfloat16 [2048, 2048], P('col', 'row'), may hold values from -0.21875 to 0.21875
- ffn_gain: float32 [2048], P('row'), may hold values from 0.5 to 1.5
- w_ffn_in: bfloat16 [2048, 2, 5632], P('row', None, 'col'), may hold values from -0.125 to 0.125
- w_down: bfloat16 [5632, 2048], P('col', 'row'), may hold values from -0.125 to 0.125
- cotangent: bfloat16 [4096, 2048], P(('dp', 'col'), 'row'), may hold values from -6 to 6
Outputs:
- output: bfloat16 [4096, 2048], P(('dp', 'col'), 'row')
- grad_tokens: float32 [4096, 2048], P(('dp', 'col'), 'row')
- grad_mix_gain: float32 [2048], P('row')
- grad_w_mix: float32 [2048, 4, 2048], P('row', None, 'col')
- grad_lower_bound: float32 [2048], P('col')
- grad_group_gain: float32 [128], replicated
- grad_w_out: float32 [2048, 2048], P('col', 'row')
- grad_ffn_gain: float32 [2048], P('row')
- grad_w_ffn_in: float32 [2048, 2, 5632], P('row', None, 'col')
- grad_w_down: float32 [5632, 2048], P('col', 'row')
The draws below stay inside these ranges and needn't reach their ends.
Inputs may be any that keep to these rules, and one draw needn't show every extreme that they name: `segments`: within each packed sequence of 2048 tokens the ids start at 0 and never fall; a document is a run of equal ids, and the last document of every sequence has the id 2048 - 1. In every sequence one document starts within the sequence's first 512 tokens, after its first token, and ends within its last 512 tokens.
All inputs are finite; a program needn't handle non-finite values.
Results may differ from the reference program's by a relative error of at most 0.013.
Values may be sent and summed in bfloat16 or wider, within the bound.
No kernel may reach another device: no remote copies, remote signals or barrier semaphores. Data moves between devices by JAX's collectives and lax.ppermute only.
A program may use at most 256 MiB of HBM per device.

```python
import math
import jax
import jax.numpy as jnp
from jax import lax

D = 2048
HEADS = 16
FF = 5632
TOK_DEV = 512
HD = 128
SPAN = 2048
TOKENS = 4096


def draw_tokens(key, part):
    key = jax.random.fold_in(key, 11)
    base_key, col_key, row_key = jax.random.split(key, 3)
    spread = math.log(10.0)
    base = jax.random.normal(base_key, (TOKENS, D), jnp.float32)
    rise = 0.55
    col_level = jax.random.uniform(col_key, (1, D), jnp.float32, 0.0, spread)
    row_level = jax.random.uniform(row_key, (TOKENS, 1), jnp.float32, 0.0, spread)
    slope = rise * jnp.arange(D, dtype=jnp.float32)[None, :] / D
    scaled = base * jnp.exp(col_level + row_level + slope - 0.5 * rise) / 21.5
    return jnp.clip(scaled, -60.0, 60.0).astype(jnp.bfloat16)


def draw_lower_bound(key, part):
    key = jax.random.fold_in(key, 23)
    level_key, jitter_key = jax.random.split(key, 2)
    lowest = math.log(0.0001)
    highest = math.log(0.5)
    head_level = jax.random.uniform(level_key, (HEADS, 1), jnp.float32, lowest, highest)
    jitter = jax.random.uniform(jitter_key, (HEADS, D // HEADS), jnp.float32, -0.35, 0.35)
    return (1.0 - jnp.exp(head_level + jitter)).reshape(D)


def draw_segments(key, part):
    key = jax.random.fold_in(key, 37)
    first_key, last_key, chance_key = jax.random.split(key, 3)
    groups = TOKENS // SPAN
    first = jax.random.randint(first_key, (groups, 1), 1, TOK_DEV)
    last = jax.random.randint(last_key, (groups, 1), SPAN - TOK_DEV + 1, SPAN)
    spots = jnp.arange(SPAN, dtype=jnp.int32)[None, :]
    chance = jax.random.randint(chance_key, (groups, SPAN), 0, 48) == 0
    outside = (spots < first) | (spots > last)
    starts = (spots == 0) | (spots == first) | (spots == last) | chance & outside
    labels = jnp.cumsum(starts.astype(jnp.int32), axis=1) - 1
    closing = labels[:, -1:]
    labels = jnp.where(labels == closing, SPAN - 1, labels)
    return labels.reshape(TOKENS).astype(jnp.int32)


def levels(rng, extent, cuts, least, largest):
    level, own = 1.0, jax.random.fold_in(rng, 6)
    for axis_at, shards_of in cuts:
        steps = jnp.exp(jax.random.uniform(jax.random.fold_in(own, axis_at), (shards_of,), jnp.float32, least / len(cuts), largest / len(cuts)))
        level = level * jnp.repeat(steps, extent[axis_at] // shards_of).reshape([-1 if axis == axis_at else 1 for axis in range(len(extent))])
    return level


def normal_values(key, dims, scale, reach, pieces=(), kind=jnp.bfloat16):
    drawn = scale * jax.random.normal(key, dims, jnp.float32)
    if pieces:
        drawn = drawn * levels(key, dims, pieces, -0.22, 0.18)
    return jnp.clip(drawn, -reach, reach).astype(kind)


def setup_inputs(seed: int = 0) -> dict:
    seeds = jax.random.split(jax.random.key(seed), 12)
    return {
        "tokens": draw_tokens(jax.random.fold_in(seeds[11], 71), 0),
        "segments": draw_segments(jax.random.fold_in(seeds[11], 71), 0),
        "mix_gain": jnp.clip(1.0 + 0.1 * jax.random.normal(seeds[2], (D,), jnp.float32), 0.5, 1.5),
        "w_mix": normal_values(seeds[3], (D, 4, D), D ** -0.5, 0.125, ((0, 4), (2, 4))),
        "lower_bound": draw_lower_bound(jax.random.fold_in(seeds[11], 71), 0),
        "group_gain": jnp.clip(1.0 + 0.1 * jax.random.normal(seeds[5], (HD,), jnp.float32), 0.5, 1.5),
        "w_out": normal_values(seeds[6], (D, D), (D // 3) ** -0.5, 0.21875, ((0, 4), (1, 4))),
        "ffn_gain": jnp.clip(1.0 + 0.1 * jax.random.normal(seeds[7], (D,), jnp.float32), 0.5, 1.5),
        "w_ffn_in": normal_values(seeds[8], (D, 2, FF), D ** -0.5, 0.125, ((0, 4), (2, 4))),
        "w_down": normal_values(seeds[9], (FF, D), (FF // 3) ** -0.5, 0.125, ((0, 4), (1, 4))),
        "cotangent": normal_values(seeds[10], (TOKENS, D), 1.0, 6.0, ((0, 8), (1, 4))),
    }


@jax.custom_vjp
def low(v):
    return lax.optimization_barrier(v.astype(jnp.bfloat16)).astype(jnp.float32)

@jax.custom_vjp
def low_back(v):
    return v

def low_keep(v):
    return (low(v), None)

def low_pass(kept, grad):
    return (grad,)

def back_keep(v):
    return (v, None)

def back_low(kept, grad):
    return (low(grad),)
low.defvjp(low_keep, low_pass)
low_back.defvjp(back_keep, back_low)
norm_eps = 1e-06
exact_result = lax.Precision.HIGHEST

def product(left, right):
    return jnp.dot(left, right, precision=exact_result, preferred_element_type=jnp.float32)

def silu(value):
    return value * jax.nn.sigmoid(value)

def rms_scale(value):
    return lax.rsqrt(lax.optimization_barrier(jnp.mean(value * value, axis=-1, keepdims=True)) + norm_eps)

def recurrence(queries, keys, values, decays):
    length = queries.shape[0]
    block = math.gcd(length, 64)
    size = D // HEADS

    def shaped(array):
        return array.reshape(length // block, block, HEADS, size)

    def steps(state, item):

        def one(carried_state, entry):
            query_vector, key_row, value_row, decay = entry
            carried_state = decay[:, :, None] * carried_state + key_row[:, :, None] * value_row[:, None, :]
            return (carried_state, jnp.einsum('mg,mgs->ms', query_vector, carried_state, precision=exact_result))
        return lax.scan(one, state, item)
    start = jnp.zeros((HEADS, size, size), queries.dtype)
    _, outs = lax.scan(jax.checkpoint(steps), start, (shaped(queries), shaped(keys), shaped(values), shaped(decays)))
    return outs.reshape(length, D)

def block_forward(inputs, fresh, mix_gain, w_mix, lower_bound, group_gain, w_out, ffn_gain, w_ffn_in, w_down):
    length = inputs.shape[0]
    mixed_in = low(inputs * rms_scale(inputs) * mix_gain)
    projected = low_back(product(mixed_in, w_mix.reshape(D, 4 * D))).reshape(length, 4, D)
    query_raw = projected[:, 0]
    forget_raw = projected[:, 1]
    input_raw = projected[:, 2]
    gate_raw = projected[:, 3]
    keys = (1.0 - lower_bound) * jax.nn.sigmoid(-forget_raw)
    decays = (1.0 - keys) * (1.0 - fresh)[:, None]
    recurrence_output = recurrence(silu(query_raw), keys, input_raw, decays).reshape(length, HEADS, D // HEADS)
    normed = recurrence_output * rms_scale(recurrence_output) * group_gain
    gated = low(normed.reshape(length, D) * silu(gate_raw))
    mixer_out = low_back(product(gated, w_out))
    hidden = inputs + mixer_out
    ffn_in = low(hidden * rms_scale(hidden) * ffn_gain)
    both = low_back(product(ffn_in, w_ffn_in.reshape(D, 2 * FF))).reshape(length, 2, FF)
    units = low(silu(both[:, 0]) * both[:, 1])
    return hidden + low_back(product(units, w_down))

def reference(tokens, segments, mix_gain, w_mix, lower_bound, group_gain, w_out, ffn_gain, w_ffn_in, w_down, cotangent):
    groups = TOKENS // SPAN
    params = (mix_gain.astype(jnp.float32), w_mix.astype(jnp.float32), lower_bound.astype(jnp.float32), group_gain.astype(jnp.float32), w_out.astype(jnp.float32), ffn_gain.astype(jnp.float32), w_ffn_in.astype(jnp.float32), w_down.astype(jnp.float32))
    inputs = tokens.astype(jnp.float32).reshape(groups, SPAN, D)
    upstreams = cotangent.astype(jnp.float32).reshape(groups, SPAN, D)
    labels = segments.reshape(groups, SPAN)

    def one_group(totals, item):
        rows_in, upstream, label = item
        changed = jnp.concatenate([jnp.ones((1,), jnp.int32), (label[1:] != label[:-1]).astype(jnp.int32)])
        fresh = changed.astype(rows_in.dtype)

        def forward(values, weights):
            return block_forward(values, fresh, *weights)
        result, pull = jax.vjp(forward, rows_in, params)
        grad_rows, grads = pull(upstream)
        totals = jax.tree.map(jnp.add, totals, grads)
        return (totals, (result.astype(jnp.bfloat16), grad_rows))
    zeros = jax.tree.map(jnp.zeros_like, params)
    totals, (results, grad_rows) = lax.scan(one_group, zeros, (inputs, upstreams, labels))
    return (results.reshape(TOKENS, D), grad_rows.reshape(TOKENS, D), totals[0], totals[1], totals[2], totals[3], totals[4], totals[5], totals[6], totals[7])
```

```python
from functools import partial

import jax
import jax.numpy as jnp
from jax import lax
from jax.experimental import pallas as pl
from jax.experimental.pallas import tpu as pltpu
from jax.sharding import PartitionSpec as P

D = 2048
HD = 128
BLOCK = 64
norm_eps = 1e-06
bf16 = jnp.bfloat16
f32 = jnp.float32

CORE = [(0, 1), (1, 0), (2, 3), (3, 2)]
CHIP = [(0, 2), (2, 0), (1, 3), (3, 1)]
UP = [(0, 1), (1, 2), (2, 3), (3, 0)]
DOWN = [(1, 0), (2, 1), (3, 2), (0, 3)]


def swap_core(x):
    return lax.ppermute(x, "row", CORE)


def swap_chip(x):
    return lax.ppermute(x, "row", CHIP)


def tie(x, *others):
    return lax.optimization_barrier((x, *others))[0]


def mm(left, right):
    return lax.dot_general(left, right, (((1,), (0,)), ((), ())), preferred_element_type=f32)


def mm_nt(left, right):
    return lax.dot_general(left, right, (((1,), (1,)), ((), ())), preferred_element_type=f32)


def mm_tn(left, right):
    return lax.dot_general(left, right, (((0,), (0,)), ((), ())), preferred_element_type=f32)


def silu_slope(value, sigma):
    return sigma * (1.0 + value * (1.0 - sigma))


def split_mm(left, value):
    high = value.astype(bf16)
    low = (value - high.astype(f32)).astype(bf16)
    return mm(left, high) + mm(left, low)


def run_masks(i, idc_ref, idr_ref, prev_ref):
    s = slice(i * BLOCK, (i + 1) * BLOCK)
    idc = idc_ref[s, :]
    idr = idr_ref[0, :, s]
    prev = prev_ref[s, :]
    before = prev[0:1, :]
    last = idc[BLOCK - 1 : BLOCK, :]
    t = lax.broadcasted_iota(jnp.int32, (BLOCK, BLOCK), 0)
    u = lax.broadcasted_iota(jnp.int32, (BLOCK, BLOCK), 1)
    same = idc == idr
    heads = (idc == before).astype(f32)
    tails = (idc == last).astype(f32)
    through = (last == before).astype(f32)
    old = (idc == prev).astype(f32)
    return t, u, same, heads, tails, through, old


def run_decays(f_raw, lb, t, u):
    closed = jax.nn.sigmoid(-f_raw)
    keys = (1.0 - lb) * closed
    total = split_mm((t >= u).astype(bf16), jnp.log1p(-keys))
    middle = total[BLOCK // 2 - 1 : BLOCK // 2, :]
    final = total[BLOCK - 1 : BLOCK, :]
    return closed, keys, total, middle, final


def local_kernel(
    kq, rq, kf, rf, ki, ri, lb_ref, idc_ref, idr_ref, prev_ref,
    inner_ref, qh_ref, kh_ref, vb_ref, keep_ref, seg_ref, segd_ref,
):
    lb = lb_ref[...]
    state = jnp.zeros((HD, HD), f32)
    passing = jnp.ones((1, HD), f32)
    for i in range(kq.shape[0] // BLOCK):
        s = slice(i * BLOCK, (i + 1) * BLOCK)
        t, u, same, heads, tails, through, _ = run_masks(i, idc_ref, idr_ref, prev_ref)
        q_raw = kq[s, :] + rq[s, :].astype(f32)
        f_raw = kf[s, :] + rf[s, :].astype(f32)
        vb = (ki[s, :] + ri[s, :].astype(f32)).astype(bf16)
        q = q_raw * jax.nn.sigmoid(q_raw)
        _, keys, total, middle, final = run_decays(f_raw, lb, t, u)
        qt = (q * jnp.exp(total - middle)).astype(bf16)
        kt = (keys * jnp.exp(middle - total)).astype(bf16)
        scores = jnp.where(same & (t >= u), mm_nt(qt, kt), 0.0).astype(bf16)
        inner_ref[s, :] = mm(scores, vb)
        qh_ref[s, :] = (q * jnp.exp(total) * heads).astype(bf16)
        kh = (keys * jnp.exp(final - total) * tails).astype(bf16)
        kh_ref[s, :] = kh
        vb_ref[s, :] = vb
        keep = jnp.exp(final) * through
        keep_ref[0, 0, i : i + 1, :] = keep
        state = keep * state + mm_tn(vb, kh)
        passing = passing * keep
    seg_ref[0, 0] = state.astype(bf16)
    segd_ref[0, 0] = passing


def finish_kernel(
    y_ref, inner_ref, qh_ref, kh_ref, vb_ref, keep_ref, pseg_ref, psegd_ref, kg, rg, gain_ref,
    gated_ref, rec_ref, st_ref, state_ref,
):
    j = pl.program_id(1)
    y = y_ref[0]

    @pl.when(j == 0)
    def _():
        state_ref[...] = jnp.zeros_like(state_ref)

    @pl.when(y == 1)
    def _():
        state_ref[...] = psegd_ref[0, 0] * state_ref[...] + pseg_ref[0, 0].astype(f32)

    state = state_ref[...]
    for i in range(qh_ref.shape[0] // BLOCK):
        s = slice(i * BLOCK, (i + 1) * BLOCK)
        low = state.astype(bf16)
        st_ref[0, i] = low
        rec = inner_ref[s, :] + mm_nt(qh_ref[s, :], low)
        rec_ref[s, :] = rec
        scale = lax.rsqrt(jnp.mean(rec * rec, axis=1, keepdims=True) + norm_eps)
        g_raw = kg[s, :] + rg[s, :].astype(f32)
        gate = g_raw * jax.nn.sigmoid(g_raw)
        gated_ref[s, :] = (rec * scale * gain_ref[...] * gate).astype(bf16)
        state = keep_ref[0, 0, i : i + 1, :] * state + mm_tn(vb_ref[s, :], kh_ref[s, :])
    state_ref[...] = state

    @pl.when(y == 0)
    def _():
        state_ref[...] = psegd_ref[0, 0] * state_ref[...] + pseg_ref[0, 0].astype(f32)


def back_local_kernel(
    kd, rd, rec_ref, kg, rg, gain_ref, qh_ref, keep_ref,
    do_ref, dg_ref, group_ref, seg_ref,
):
    @pl.when((pl.program_id(0) == 0) & (pl.program_id(1) == 0))
    def _():
        group_ref[...] = jnp.zeros_like(group_ref)

    gain = gain_ref[...]
    adjoint = jnp.zeros((HD, HD), f32)
    group = jnp.zeros((1, HD), f32)
    for i in reversed(range(qh_ref.shape[0] // BLOCK)):
        s = slice(i * BLOCK, (i + 1) * BLOCK)
        grad = kd[s, :] + rd[s, :].astype(f32)
        rec = rec_ref[s, :]
        scale = lax.rsqrt(jnp.mean(rec * rec, axis=1, keepdims=True) + norm_eps)
        normed = rec * scale
        g_raw = kg[s, :] + rg[s, :].astype(f32)
        sigma = jax.nn.sigmoid(g_raw)
        act = g_raw * sigma
        both = grad * normed
        group = group + jnp.sum(both * act, axis=0, keepdims=True)
        dg_ref[s, :] = (both * gain * silu_slope(g_raw, sigma)).astype(bf16)
        dn = grad * gain * act
        do = (scale * (dn - normed * jnp.mean(dn * normed, axis=1, keepdims=True))).astype(bf16)
        do_ref[s, :] = do
        adjoint = keep_ref[0, 0, i : i + 1, :] * adjoint + mm_tn(do, qh_ref[s, :])
    group_ref[...] += group
    seg_ref[0, 0] = adjoint.astype(bf16)


def back_finish_kernel(
    y_ref, kq, rq, kf, rf, lb_ref, idc_ref, idr_ref, prev_ref,
    qh_ref, kh_ref, vb_ref, keep_ref, st_ref, do_ref, pseg_ref, psegd_ref,
    dq_ref, df_ref, dv_ref, bound_ref, adj_ref,
):
    j = pl.program_id(1)
    y = y_ref[0]

    @pl.when(j == 0)
    def _():
        adj_ref[...] = jnp.zeros_like(adj_ref)
        bound_ref[...] = jnp.zeros_like(bound_ref)

    @pl.when(y == 0)
    def _():
        adj_ref[...] = psegd_ref[0, 0] * adj_ref[...] + pseg_ref[0, 0].astype(f32)

    lb = lb_ref[...]
    adjoint = adj_ref[...]
    bound = jnp.zeros((1, HD), f32)
    for i in reversed(range(kq.shape[0] // BLOCK)):
        s = slice(i * BLOCK, (i + 1) * BLOCK)
        t, u, same, heads, tails, through, old = run_masks(i, idc_ref, idr_ref, prev_ref)
        causal = same & (t >= u)
        q_raw = kq[s, :] + rq[s, :].astype(f32)
        f_raw = kf[s, :] + rf[s, :].astype(f32)
        sigma = jax.nn.sigmoid(q_raw)
        q = q_raw * sigma
        closed, keys, total, middle, final = run_decays(f_raw, lb, t, u)
        out = jnp.exp(total - middle)
        back = jnp.exp(middle - total)
        qt = (q * out).astype(bf16)
        kt = (keys * back).astype(bf16)
        scores = jnp.where(causal, mm_nt(qt, kt), 0.0).astype(bf16)
        vb = vb_ref[s, :]
        kh = kh_ref[s, :]
        qh = qh_ref[s, :]
        do = do_ref[s, :]
        st = st_ref[0, i]
        low = adjoint.astype(bf16)
        keep = keep_ref[0, 0, i : i + 1, :]
        ds = jnp.where(causal, mm_nt(do, vb), 0.0).astype(bf16)
        dq = mm(ds, kt) * out + mm(do, st) * (jnp.exp(total) * heads)
        dkh = mm(vb, low)
        dk = mm_tn(ds, qt) * back + dkh * (jnp.exp(final - total) * tails)
        dv_ref[s, :] = (mm_tn(scores, do) + mm_nt(kh, low)).astype(bf16)
        ends = keep * jnp.sum(adjoint * st.astype(f32), axis=0, keepdims=True) + jnp.sum(
            kh.astype(f32) * dkh, axis=0, keepdims=True
        )
        later = (same & (u >= t)).astype(bf16)
        dlog = split_mm(later, q * dq - keys * dk) + tails * ends
        key_total = dk - old * dlog / (1.0 - keys)
        bound = bound - jnp.sum(key_total * closed, axis=0, keepdims=True)
        df_ref[s, :] = (-key_total * keys * (1.0 - closed)).astype(bf16)
        dq_ref[s, :] = (dq * silu_slope(q_raw, sigma)).astype(bf16)
        adjoint = keep * adjoint + mm_tn(do, qh)
    bound_ref[...] += bound
    adj_ref[...] = adjoint

    @pl.when(y == 1)
    def _():
        adj_ref[...] = psegd_ref[0, 0] * adj_ref[...] + pseg_ref[0, 0].astype(f32)


def shape(dims, kind):
    return jax.ShapeDtypeStruct(dims, kind)


def cost(flops, moved):
    return pl.CostEstimate(flops=flops, bytes_accessed=moved, transcendentals=0)


def column(run, heads, part, turn):
    return pl.BlockSpec((run, HD), lambda h, j: (turn(j), part * heads + h))


def forward_turn(j):
    return j


def recurrence_local(keep, recv, bound, ids):
    idc, idr, prev = ids
    runs, _, run = idr.shape
    heads = keep.shape[1] // (4 * HD)
    chunks = run // BLOCK
    tokens = runs * run
    col = partial(column, run, heads, turn=forward_turn)
    one = pl.BlockSpec((run, 1), lambda h, j: (j, 0))
    seg = lambda *dims: pl.BlockSpec((1, 1, *dims), lambda h, j: (h, j, 0, 0))
    return pl.pallas_call(
        local_kernel,
        grid=(heads, runs),
        in_specs=[
            col(part=0), col(part=0), col(part=1), col(part=1), col(part=2), col(part=2),
            pl.BlockSpec((1, HD), lambda h, j: (0, h)),
            one,
            pl.BlockSpec((1, 1, run), lambda h, j: (j, 0, 0)),
            one,
        ],
        out_specs=[col(part=0)] * 4 + [seg(chunks, HD), seg(HD, HD), seg(1, HD)],
        out_shape=[
            shape((tokens, heads * HD), f32),
            shape((tokens, heads * HD), bf16),
            shape((tokens, heads * HD), bf16),
            shape((tokens, heads * HD), bf16),
            shape((heads, runs, chunks, HD), f32),
            shape((heads, runs, HD, HD), bf16),
            shape((heads, runs, 1, HD), f32),
        ],
        cost_estimate=cost(int(4e9), int(2e7)),
        name="recurrence_local",
    )(keep, recv, keep, recv, keep, recv, bound, idc, idr, prev)


def recurrence_finish(y, local, peer, keep, recv, gain):
    inner, qh, kh, vb, decay = local
    heads, runs, chunks, _ = decay.shape
    run = chunks * BLOCK
    tokens = runs * run
    col = partial(column, run, heads, turn=forward_turn)
    seg = lambda *dims: pl.BlockSpec((1, 1, *dims), lambda h, j: (h, j, 0, 0))
    return pl.pallas_call(
        finish_kernel,
        grid=(heads, runs),
        in_specs=[
            pl.BlockSpec(memory_space=pltpu.SMEM),
            col(part=0), col(part=0), col(part=0), col(part=0),
            seg(chunks, HD), seg(HD, HD), seg(1, HD),
            col(part=3), col(part=3),
            pl.BlockSpec((1, HD), lambda h, j: (0, 0)),
        ],
        out_specs=[
            col(part=0), col(part=0),
            pl.BlockSpec((1, chunks, HD, HD), lambda h, j: (h, j, 0, 0)),
        ],
        out_shape=[
            shape((tokens, heads * HD), bf16),
            shape((tokens, heads * HD), f32),
            shape((heads, runs * chunks, HD, HD), bf16),
        ],
        scratch_shapes=[pltpu.VMEM((HD, HD), f32)],
        cost_estimate=cost(int(3e9), int(1e7)),
        name="recurrence_finish",
    )(y, inner, qh, kh, vb, decay, *peer, keep, recv, gain)


def recurrence_back_local(kd, rd, rec, keep, recv, gain, qh, decay):
    heads, runs, chunks, _ = decay.shape
    run = chunks * BLOCK
    tokens = runs * run
    col = partial(column, run, heads, turn=forward_turn)
    seg = lambda *dims: pl.BlockSpec((1, 1, *dims), lambda h, j: (h, j, 0, 0))
    return pl.pallas_call(
        back_local_kernel,
        grid=(heads, runs),
        in_specs=[
            col(part=0), col(part=0), col(part=0), col(part=3), col(part=3),
            pl.BlockSpec((1, HD), lambda h, j: (0, 0)),
            col(part=0), seg(chunks, HD),
        ],
        out_specs=[
            col(part=0), col(part=0),
            pl.BlockSpec((1, HD), lambda h, j: (0, 0)),
            seg(HD, HD),
        ],
        out_shape=[
            shape((tokens, heads * HD), bf16),
            shape((tokens, heads * HD), bf16),
            shape((1, HD), f32),
            shape((heads, runs, HD, HD), bf16),
        ],
        cost_estimate=cost(int(3e9), int(1e7)),
        name="recurrence_back_local",
    )(kd, rd, rec, keep, recv, gain, qh, decay)


def recurrence_back_finish(y, keep, recv, bound, ids, local, states, do, peer):
    idc, idr, prev = ids
    _, qh, kh, vb, decay = local
    heads, runs, chunks, _ = decay.shape
    run = chunks * BLOCK
    tokens = runs * run
    turn = lambda j: runs - 1 - j
    col = partial(column, run, heads, turn=turn)
    one = pl.BlockSpec((run, 1), lambda h, j: (turn(j), 0))
    seg = lambda *dims: pl.BlockSpec((1, 1, *dims), lambda h, j: (h, turn(j), 0, 0))
    return pl.pallas_call(
        back_finish_kernel,
        grid=(heads, runs),
        in_specs=[
            pl.BlockSpec(memory_space=pltpu.SMEM),
            col(part=0), col(part=0), col(part=1), col(part=1),
            pl.BlockSpec((1, HD), lambda h, j: (0, h)),
            one,
            pl.BlockSpec((1, 1, run), lambda h, j: (turn(j), 0, 0)),
            one,
            col(part=0), col(part=0), col(part=0),
            seg(chunks, HD),
            pl.BlockSpec((1, chunks, HD, HD), lambda h, j: (h, turn(j), 0, 0)),
            col(part=0),
            seg(HD, HD), seg(1, HD),
        ],
        out_specs=[
            col(part=0), col(part=0), col(part=0),
            pl.BlockSpec((1, HD), lambda h, j: (0, h)),
        ],
        out_shape=[
            shape((tokens, heads * HD), bf16),
            shape((tokens, heads * HD), bf16),
            shape((tokens, heads * HD), bf16),
            shape((1, heads * HD), f32),
        ],
        scratch_shapes=[pltpu.VMEM((HD, HD), f32)],
        cost_estimate=cost(int(8e9), int(2e7)),
        name="recurrence_back_finish",
    )(y, keep, recv, keep, recv, bound, idc, idr, prev, qh, kh, vb, decay, states, do, *peer)


def gather_pair(own, other, z):
    count = lax.axis_size("col")
    rows, width = own.shape

    def put(whole, part, at):
        return lax.dynamic_update_slice(whole, part[None], (at % count, 0, 0))

    first = put(jnp.zeros((count, rows, width), own.dtype), own, z)
    second = put(jnp.zeros((count, rows, width), other.dtype), other, z)
    for k in range(1, count):
        own = lax.ppermute(own, "col", UP)
        other = lax.ppermute(other, "col", DOWN)
        first = put(first, own, z - k + count)
        second = put(second, other, z + k)
    return first.reshape(count * rows, width), second.reshape(count * rows, width)


def scatter_pair(own, other, z, offset):
    count = lax.axis_size("col")
    own = own.reshape(count, -1, own.shape[1])
    other = other.reshape(count, -1, other.shape[1])

    def block(whole, at):
        return lax.dynamic_index_in_dim(whole, (at + offset) % count, 0, keepdims=False)

    first = block(own, z - 1 + count)
    second = block(other, z + 1)
    for k in range(2, count + 1):
        moved = lax.ppermute(first.astype(bf16), "col", UP)
        first = moved.astype(f32) + block(own, z - k + count)
        moved = lax.ppermute(second.astype(bf16), "col", DOWN)
        second = moved.astype(f32) + block(other, z + k)
    return first, second


def sum_over(value, axis):
    count = lax.axis_size(axis)
    if count == 2:
        return value + lax.ppermute(value, axis, [(0, 1), (1, 0)])
    if count == 4:
        value = value + lax.ppermute(value, axis, [(0, 1), (1, 0), (2, 3), (3, 2)])
        return value + lax.ppermute(value, axis, [(0, 2), (2, 0), (1, 3), (3, 1)])
    return lax.psum(value, axis)


def sum_groups(grad):
    sent = grad.astype(bf16)
    if lax.axis_size("dp") == 2:
        return sent.astype(f32) + lax.ppermute(sent, "dp", [(0, 1), (1, 0)]).astype(f32)
    return lax.psum(sent, "dp").astype(f32)


def weight_grad(left_own, left_other, right):
    sent = swap_chip(mm_tn(left_other, right).astype(bf16))
    return sum_groups(mm_tn(left_own, right) + sent.astype(f32))


def shards(
    tokens,
    segments,
    mix_gain,
    w_mix,
    lower_bound,
    group_gain,
    w_out,
    ffn_gain,
    w_ffn_in,
    w_down,
    cotangent,
):
    row = lax.axis_index("row")
    core = row % 2
    y = row // 2
    z = lax.axis_index("col")
    count = lax.axis_size("col")
    span = segments.shape[0]
    half = tokens.shape[0] // 2
    width = tokens.shape[1]
    cols = w_mix.shape[2]
    hc = cols // 2
    units_col = w_down.shape[0]
    here = count * half
    hb = here // 2

    def mine(x, at, size, axis):
        return lax.dynamic_slice_in_dim(x, at * size, size, axis)

    def joined(first_if_zero, second_if_zero, flag, axis):
        return jnp.where(
            flag == 0,
            jnp.concatenate([first_if_zero, second_if_zero], axis),
            jnp.concatenate([second_if_zero, first_if_zero], axis),
        )

    tok_own = mine(tokens, y, half, 0)
    tok_other = swap_chip(mine(tokens, 1 - y, half, 0))
    x_own, x_other = gather_pair(tok_own, tok_other, z)

    gains = jnp.stack([mix_gain, ffn_gain])
    gains_other = swap_chip(gains)
    wm_keep = mine(w_mix, core, hc, 2).reshape(width, 4 * hc)
    wm_send = mine(w_mix, 1 - core, hc, 2).reshape(width, 4 * hc)
    wm_send_o = swap_chip(wm_send)
    wm_keep_o = swap_chip(wm_keep)
    wo_keep = mine(w_out, core, hc, 0)
    wo_send = mine(w_out, 1 - core, hc, 0)
    wo = tie(jnp.concatenate([wo_keep, wo_send], 0), wm_keep_o, wm_send_o)
    wo_o = swap_chip(wo)
    wo_keep_o, wo_send_o = wo_o[:hc], wo_o[hc:]
    wf = w_ffn_in.reshape(width, 2 * units_col)
    wf_o = swap_chip(tie(wf, wo_o))
    wd = w_down
    wd_o = swap_chip(tie(wd, wf_o))

    ids = segments.astype(f32)
    before = jnp.concatenate([jnp.full((1,), -1.0, f32), ids[:-1]])
    pick = lambda a: lax.dynamic_index_in_dim(a.reshape(count, 2, half), y, 1, keepdims=False)
    ids, before = pick(ids), pick(before)
    ids = (ids.reshape(here, 1), ids.reshape(count, 1, half), before.reshape(here, 1))

    xo = x_own.astype(f32)
    xp = x_other.astype(f32)
    squares = jnp.sum(xo * xo, axis=1) + jnp.sum(xp * xp, axis=1)
    squares = squares + swap_core(squares)
    mix_scale = lax.rsqrt(squares / D + norm_eps)[:, None]
    m_own = (xo * mix_scale * mix_gain).astype(bf16)
    m_other = (xp * mix_scale * gains_other[0]).astype(bf16)

    send = (mm(m_own, wm_send) + mm(m_other, wm_send_o)).astype(bf16)
    recv = swap_core(send)
    keep = mm(m_own, wm_keep) + mm(m_other, wm_keep_o)

    cot = tie(cotangent, m_own)
    cot_own = mine(cot, y, half, 0)
    cot_other = swap_chip(mine(cot, 1 - y, half, 0))
    c_own, c_other = gather_pair(cot_own, cot_other, z)

    y_here = y.astype(jnp.int32).reshape(1)
    bound = mine(lower_bound, core, hc, 0).reshape(1, hc)
    gain_row = group_gain.reshape(1, HD)
    *local, seg_state, seg_decay = recurrence_local(keep, recv, bound, ids)
    peer_state = swap_chip(seg_state)
    peer_decay = swap_chip(seg_decay)
    gated, rec, states = recurrence_finish(
        y_here, local, (peer_state, peer_decay), keep, recv, gain_row
    )
    gated_p = swap_core(gated)
    gated_all = jnp.concatenate([gated, gated_p], 1)
    mixed_own, mixed_other = scatter_pair(mm(gated_all, wo), mm(gated_all, wo_o), z, 0)
    h_own = tok_own.astype(f32) + mixed_own
    h_other = tok_other.astype(f32) + mixed_other

    squares = jnp.sum(h_own * h_own, axis=1) + jnp.sum(h_other * h_other, axis=1)
    squares = squares + swap_core(squares)
    ffn_scale = lax.rsqrt(squares / D + norm_eps)[:, None]
    n_own = (h_own * ffn_scale * ffn_gain).astype(bf16)
    n_other = (h_other * ffn_scale * gains_other[1]).astype(bf16)
    f_own, f_other = gather_pair(n_own, n_other, z)

    def rows(x, at):
        return mine(x, at, hb, 0)

    gu_send = (mm_nt(rows(c_own, 1 - core), wd) + mm_nt(rows(c_other, 1 - core), wd_o)).astype(bf16)
    gu_recv = swap_core(gu_send)
    gu = mm_nt(rows(c_own, core), wd) + mm_nt(rows(c_other, core), wd_o) + gu_recv.astype(f32)

    fk_own, fs_own = rows(f_own, core), rows(f_own, 1 - core)
    fk_other, fs_other = rows(f_other, core), rows(f_other, 1 - core)
    b_send = (mm(fs_own, wf) + mm(fs_other, wf_o)).astype(bf16)
    b_recv = swap_core(b_send)
    both = mm(fk_own, wf) + mm(fk_other, wf_o) + b_recv.astype(f32)
    gate, up = both[:, :units_col], both[:, units_col:]
    sigma = jax.nn.sigmoid(gate)
    act = gate * sigma
    units = (act * up).astype(bf16)
    grad_both = jnp.concatenate(
        [(gu * up * silu_slope(gate, sigma)).astype(bf16), (gu * act).astype(bf16)], 1
    )
    grad_both_p = swap_core(grad_both)
    gb = jnp.concatenate([grad_both, grad_both_p], 0)
    units_p = swap_core(tie(units, grad_both_p))
    un = jnp.concatenate([units, units_p], 0)
    shift = 2 * core

    df_own, df_other = scatter_pair(mm_nt(gb, wf), mm_nt(gb, wf_o), z, shift)

    gain_f, gain_fo = ffn_gain, gains_other[1]
    w_o, w_p = df_own * gain_f, df_other * gain_fo
    along = jnp.sum(w_o * h_own, axis=1) + jnp.sum(w_p * h_other, axis=1)
    along = along + swap_core(along)
    factor = ffn_scale**3 * along[:, None] / D
    cot_f_own = cot_own.astype(f32)
    cot_f_other = cot_other.astype(f32)
    gh_own = cot_f_own + ffn_scale * w_o - h_own * factor
    gh_other = cot_f_other + ffn_scale * w_p - h_other * factor
    ffn_part = jnp.sum(df_own * h_own * ffn_scale, axis=0)
    ffn_part_o = jnp.sum(df_other * h_other * ffn_scale, axis=0)
    g_own, g_other = gather_pair(gh_own.astype(bf16), gh_other.astype(bf16), z)

    gg_send = (mm_nt(g_own, wo_send) + mm_nt(g_other, wo_send_o)).astype(bf16)
    gg_recv = swap_core(gg_send)
    gg_keep = mm_nt(g_own, wo_keep) + mm_nt(g_other, wo_keep_o)
    do, d_gate, group_part, adj = recurrence_back_local(
        gg_keep, gg_recv, rec, keep, recv, gain_row, local[1], local[4]
    )
    peer_adj = swap_chip(adj)
    d_gate_p = swap_core(d_gate)
    d_query, d_forget, d_input, bound_part = recurrence_back_finish(
        y_here, keep, recv, bound, ids, local, states, do, (peer_adj, peer_decay)
    )
    d_three = jnp.concatenate([d_query, d_forget, d_input], 1)
    d_three_p = swap_core(d_three)
    dp_keep = jnp.concatenate([d_three, d_gate], 1)
    dp_send = jnp.concatenate([d_three_p, d_gate_p], 1)
    dx_own, dx_other = scatter_pair(
        mm_nt(dp_keep, wm_keep) + mm_nt(dp_send, wm_send),
        mm_nt(dp_keep, wm_keep_o) + mm_nt(dp_send, wm_send_o),
        z,
        0,
    )

    un = tie(un, g_own, g_other)
    out_own, out_other = scatter_pair(mm(un, wd), mm(un, wd_o), z, shift)
    out_own = (h_own + out_own).astype(bf16)
    out_other = (h_other + out_other).astype(bf16)
    output = joined(out_own, swap_chip(out_other), y, 0)

    ck = jnp.concatenate([rows(c_own, core), rows(c_own, 1 - core)], 0)
    ck_o = jnp.concatenate([rows(c_other, core), rows(c_other, 1 - core)], 0)
    sent = swap_chip(mm_tn(un, ck_o).astype(bf16))
    grad_w_down = sum_groups(mm_tn(un, ck) + sent.astype(f32))
    grad_w_ffn = weight_grad(
        jnp.concatenate([fk_own, fs_own], 0), jnp.concatenate([fk_other, fs_other], 0), gb
    ).reshape(width, 2, units_col)
    sent = swap_chip(mm_tn(gated_all, g_other).astype(bf16))
    grad_wo = sum_groups(mm_tn(gated_all, g_own) + sent.astype(f32))
    grad_w_out = joined(grad_wo[:hc], grad_wo[hc:], core, 0)
    gm_keep = weight_grad(m_own, m_other, dp_keep).reshape(width, 4, hc)
    gm_send = weight_grad(m_own, m_other, dp_send).reshape(width, 4, hc)
    grad_w_mix = joined(gm_keep, gm_send, core, 2)

    scale = lax.dynamic_slice_in_dim(mix_scale, z * half, half, 0)
    t_own, t_other = tok_own.astype(f32), tok_other.astype(f32)
    w_o, w_p = dx_own * mix_gain, dx_other * gains_other[0]
    along = jnp.sum(w_o * t_own, axis=1) + jnp.sum(w_p * t_other, axis=1)
    along = along + swap_core(along)
    factor = scale**3 * along[:, None] / D
    gt_own = gh_own + scale * w_o - t_own * factor
    gt_other = gh_other + scale * w_p - t_other * factor
    mix_part = jnp.sum(dx_own * t_own * scale, axis=0)
    mix_part_o = jnp.sum(dx_other * t_other * scale, axis=0)
    grad_tokens = joined(gt_own, swap_chip(gt_other), y, 0)

    small = jnp.stack([mix_part, ffn_part])
    small_o = jnp.stack([mix_part_o, ffn_part_o])
    small = small + swap_chip(small_o)
    small = sum_over(sum_over(small, "col"), "dp")
    bound_part = bound_part[0]
    bound_part = bound_part + swap_chip(bound_part)
    bound_part = sum_over(bound_part, "dp")
    bound_p = swap_core(bound_part)
    grad_bound = joined(bound_part, bound_p, core, 0)
    group = group_part[0]
    group = group + swap_core(group)
    group = group + swap_chip(group)
    group = sum_over(sum_over(group, "col"), "dp")
    return (
        output,
        grad_tokens,
        small[0],
        grad_w_mix,
        grad_bound,
        group,
        grad_w_out,
        small[1],
        grad_w_ffn,
        grad_w_down,
    )


def solution(mesh):
    return jax.shard_map(
        shards,
        mesh=mesh,
        in_specs=(
            P(("dp", "col"), "row"),
            P("dp"),
            P("row"),
            P("row", None, "col"),
            P("col"),
            P(),
            P("col", "row"),
            P("row"),
            P("row", None, "col"),
            P("col", "row"),
            P(("dp", "col"), "row"),
        ),
        out_specs=(
            P(("dp", "col"), "row"),
            P(("dp", "col"), "row"),
            P("row"),
            P("row", None, "col"),
            P("col"),
            P(),
            P("col", "row"),
            P("row"),
            P("row", None, "col"),
            P("col", "row"),
        ),
        check_vma=False,
    )
```

```python
from functools import partial

import jax
import jax.numpy as jnp
from jax import lax
from jax.experimental import pallas as pl
from jax.experimental.pallas import tpu as pltpu
from jax.sharding import PartitionSpec as P

D = 2048
HD = 128
BLOCK = 64
norm_eps = 1e-06
bf16 = jnp.bfloat16
f32 = jnp.float32

CORE = [(0, 1), (1, 0), (2, 3), (3, 2)]
CHIP = [(0, 2), (2, 0), (1, 3), (3, 1)]
UP = [(0, 1), (1, 2), (2, 3), (3, 0)]
DOWN = [(1, 0), (2, 1), (3, 2), (0, 3)]


def swap_core(x):
    return lax.ppermute(x, "row", CORE)


def swap_chip(x):
    return lax.ppermute(x, "row", CHIP)


def tie(x, *others):
    return lax.optimization_barrier((x, *others))[0]


def mm(left, right):
    return lax.dot_general(left, right, (((1,), (0,)), ((), ())), preferred_element_type=f32)


def mm_nt(left, right):
    return lax.dot_general(left, right, (((1,), (1,)), ((), ())), preferred_element_type=f32)


def mm_tn(left, right):
    return lax.dot_general(left, right, (((0,), (0,)), ((), ())), preferred_element_type=f32)


def silu_slope(value, sigma):
    return sigma * (1.0 + value * (1.0 - sigma))


def split_mm(left, value):
    high = value.astype(bf16)
    low = (value - high.astype(f32)).astype(bf16)
    return mm(left, high) + mm(left, low)


def run_masks(i, idc_ref, idr_ref, prev_ref):
    s = slice(i * BLOCK, (i + 1) * BLOCK)
    idc = idc_ref[s, :]
    idr = idr_ref[0, :, s]
    prev = prev_ref[s, :]
    before = prev[0:1, :]
    last = idc[BLOCK - 1 : BLOCK, :]
    t = lax.broadcasted_iota(jnp.int32, (BLOCK, BLOCK), 0)
    u = lax.broadcasted_iota(jnp.int32, (BLOCK, BLOCK), 1)
    same = idc == idr
    heads = (idc == before).astype(f32)
    tails = (idc == last).astype(f32)
    through = (last == before).astype(f32)
    old = (idc == prev).astype(f32)
    return t, u, same, heads, tails, through, old


def run_decays(f_raw, lb, t, u):
    closed = jax.nn.sigmoid(-f_raw)
    keys = (1.0 - lb) * closed
    total = split_mm((t >= u).astype(bf16), jnp.log1p(-keys))
    middle = total[BLOCK // 2 - 1 : BLOCK // 2, :]
    final = total[BLOCK - 1 : BLOCK, :]
    return closed, keys, total, middle, final


def col(h, part=0, heads=1):
    start = (part * heads + h) * HD
    return slice(start, start + HD)


def local_kernel(
    keep_ref, recv_ref, lb_ref, idc_ref, idr_ref, prev_ref,
    inner_ref, qh_ref, kh_ref, vb_ref, decay_ref, seg_ref, low_ref, segd_ref,
):
    heads = lb_ref.shape[1] // HD
    state = [jnp.zeros((HD, HD), f32)] * heads
    passing = [jnp.ones((1, HD), f32)] * heads
    for i in range(keep_ref.shape[0] // BLOCK):
        s = slice(i * BLOCK, (i + 1) * BLOCK)
        t, u, same, head, tails, through, _ = run_masks(i, idc_ref, idr_ref, prev_ref)
        for h in range(heads):
            c = col(h)

            def raw(part):
                p = col(h, part, heads)
                return keep_ref[s, p] + recv_ref[s, p].astype(f32)

            q_raw = raw(0)
            vb = raw(2).astype(bf16)
            q = q_raw * jax.nn.sigmoid(q_raw)
            _, keys, total, middle, final = run_decays(raw(1), lb_ref[:, c], t, u)
            qt = (q * jnp.exp(total - middle)).astype(bf16)
            kt = (keys * jnp.exp(middle - total)).astype(bf16)
            scores = jnp.where(same & (t >= u), mm_nt(qt, kt), 0.0).astype(bf16)
            inner_ref[s, c] = mm(scores, vb)
            qh_ref[s, c] = (q * jnp.exp(total) * head).astype(bf16)
            kh = (keys * jnp.exp(final - total) * tails).astype(bf16)
            kh_ref[s, c] = kh
            vb_ref[s, c] = vb
            keep = jnp.exp(final) * through
            decay_ref[0, i : i + 1, c] = keep
            state[h] = keep * state[h] + mm_tn(vb, kh)
            passing[h] = passing[h] * keep
    for h in range(heads):
        seg_ref[0, h] = state[h]
        low_ref[0, h] = state[h].astype(bf16)
        segd_ref[0, :, col(h)] = passing[h]


def enter_kernel(reverse, place_ref, seg_ref, segd_ref, peer_ref, peerd_ref, out_ref):
    z, y = place_ref[0], place_ref[1]
    count, heads = seg_ref.shape[:2]
    peer_first = (y == 0) if reverse else (y == 1)
    state = [jnp.zeros((HD, HD), f32)] * heads
    for place in reversed(range(count)) if reverse else range(count):
        k = lax.rem(z - place + count, count)
        for h in range(heads):
            add = peer_ref[k, h].astype(f32)
            scale = peerd_ref[k, :, col(h)]
            s = jnp.where(peer_first, scale, 1.0) * state[h] + jnp.where(peer_first, add, 0.0)
            out_ref[k, h] = s
            s = segd_ref[k, :, col(h)] * s + seg_ref[k, h]
            state[h] = jnp.where(peer_first, 1.0, scale) * s + jnp.where(peer_first, 0.0, add)


def finish_kernel(
    inner_ref, qh_ref, kh_ref, vb_ref, decay_ref, enter_ref, keep_ref, recv_ref, gain_ref,
    gated_ref, rec_ref, st_ref,
):
    heads = enter_ref.shape[1]
    state = [enter_ref[0, h] for h in range(heads)]
    for i in range(qh_ref.shape[0] // BLOCK):
        s = slice(i * BLOCK, (i + 1) * BLOCK)
        for h in range(heads):
            c = col(h)
            low = state[h].astype(bf16)
            st_ref[0, i, h] = low
            rec = inner_ref[s, c] + mm_nt(qh_ref[s, c], low)
            rec_ref[s, c] = rec
            scale = lax.rsqrt(jnp.mean(rec * rec, axis=1, keepdims=True) + norm_eps)
            g_raw = keep_ref[s, c] + recv_ref[s, c].astype(f32)
            gate = g_raw * jax.nn.sigmoid(g_raw)
            gated_ref[s, c] = (rec * scale * gain_ref[...] * gate).astype(bf16)
            state[h] = decay_ref[0, i : i + 1, c] * state[h] + mm_tn(vb_ref[s, c], kh_ref[s, c])


def back_local_kernel(
    kd, rd, rec_ref, keep_ref, recv_ref, gain_ref, qh_ref, decay_ref,
    do_ref, dg_ref, group_ref, seg_ref, low_ref,
):
    @pl.when(pl.program_id(0) == 0)
    def _():
        group_ref[...] = jnp.zeros_like(group_ref)

    gain = gain_ref[...]
    heads = seg_ref.shape[1]
    adjoint = [jnp.zeros((HD, HD), f32)] * heads
    group = jnp.zeros((1, HD), f32)
    for i in reversed(range(qh_ref.shape[0] // BLOCK)):
        s = slice(i * BLOCK, (i + 1) * BLOCK)
        for h in range(heads):
            c = col(h)
            grad = kd[s, c] + rd[s, c].astype(f32)
            rec = rec_ref[s, c]
            scale = lax.rsqrt(jnp.mean(rec * rec, axis=1, keepdims=True) + norm_eps)
            normed = rec * scale
            g_raw = keep_ref[s, c] + recv_ref[s, c].astype(f32)
            sigma = jax.nn.sigmoid(g_raw)
            act = g_raw * sigma
            both = grad * normed
            group = group + jnp.sum(both * act, axis=0, keepdims=True)
            dg_ref[s, c] = (both * gain * silu_slope(g_raw, sigma)).astype(bf16)
            dn = grad * gain * act
            do = (scale * (dn - normed * jnp.mean(dn * normed, axis=1, keepdims=True))).astype(bf16)
            do_ref[s, c] = do
            adjoint[h] = decay_ref[0, i : i + 1, c] * adjoint[h] + mm_tn(do, qh_ref[s, c])
    group_ref[...] += group
    for h in range(heads):
        seg_ref[0, h] = adjoint[h]
        low_ref[0, h] = adjoint[h].astype(bf16)


def back_finish_kernel(
    keep_ref, recv_ref, lb_ref, idc_ref, idr_ref, prev_ref,
    qh_ref, kh_ref, vb_ref, decay_ref, st_ref, do_ref, enter_ref,
    grad_ref, bound_ref,
):
    @pl.when(pl.program_id(0) == 0)
    def _():
        bound_ref[...] = jnp.zeros_like(bound_ref)

    heads = enter_ref.shape[1]
    adjoint = [enter_ref[0, h] for h in range(heads)]
    bound = [jnp.zeros((1, HD), f32)] * heads
    for i in reversed(range(keep_ref.shape[0] // BLOCK)):
        s = slice(i * BLOCK, (i + 1) * BLOCK)
        t, u, same, head, tails, through, old = run_masks(i, idc_ref, idr_ref, prev_ref)
        causal = same & (t >= u)
        later = (same & (u >= t)).astype(bf16)
        for h in range(heads):
            c = col(h)

            def raw(part):
                p = col(h, part, heads)
                return keep_ref[s, p] + recv_ref[s, p].astype(f32)

            q_raw = raw(0)
            sigma = jax.nn.sigmoid(q_raw)
            q = q_raw * sigma
            closed, keys, total, middle, final = run_decays(raw(1), lb_ref[:, c], t, u)
            out = jnp.exp(total - middle)
            back = jnp.exp(middle - total)
            qt = (q * out).astype(bf16)
            kt = (keys * back).astype(bf16)
            scores = jnp.where(causal, mm_nt(qt, kt), 0.0).astype(bf16)
            vb = vb_ref[s, c]
            kh = kh_ref[s, c]
            do = do_ref[s, c]
            st = st_ref[0, i, h]
            low = adjoint[h].astype(bf16)
            keep = decay_ref[0, i : i + 1, c]
            ds = jnp.where(causal, mm_nt(do, vb), 0.0).astype(bf16)
            dq = mm(ds, kt) * out + mm(do, st) * (jnp.exp(total) * head)
            dkh = mm(vb, low)
            dk = mm_tn(ds, qt) * back + dkh * (jnp.exp(final - total) * tails)
            grad_ref[s, col(h, 2, heads)] = (mm_tn(scores, do) + mm_nt(kh, low)).astype(bf16)
            ends = keep * jnp.sum(adjoint[h] * st.astype(f32), axis=0, keepdims=True) + jnp.sum(
                kh.astype(f32) * dkh, axis=0, keepdims=True
            )
            dlog = split_mm(later, q * dq - keys * dk) + tails * ends
            key_total = dk - old * dlog / (1.0 - keys)
            bound[h] = bound[h] - jnp.sum(key_total * closed, axis=0, keepdims=True)
            grad_ref[s, col(h, 1, heads)] = (-key_total * keys * (1.0 - closed)).astype(bf16)
            grad_ref[s, col(h, 0, heads)] = (dq * silu_slope(q_raw, sigma)).astype(bf16)
            adjoint[h] = keep * adjoint[h] + mm_tn(do, qh_ref[s, c])
    for h in range(heads):
        bound_ref[:, col(h)] += bound[h]


def shape(dims, kind):
    return jax.ShapeDtypeStruct(dims, kind)


COST = pl.CostEstimate(flops=0, bytes_accessed=0, transcendentals=0)
SMEM = pl.BlockSpec(memory_space=pltpu.SMEM)
VMEM = pl.BlockSpec(memory_space=pltpu.VMEM)


def run_block(*dims, at=0):
    return pl.BlockSpec(dims, lambda j: (j, *([0] * (len(dims) - 2)), at))


def whole(*dims):
    return pl.BlockSpec(dims, lambda j: (0,) * len(dims))


def recurrence_local(keep, recv, bound, ids):
    runs, _, run = ids[1].shape
    width = bound.shape[1]
    heads = width // HD
    chunks = run // BLOCK
    tokens = runs * run
    return pl.pallas_call(
        local_kernel,
        grid=(runs,),
        in_specs=[
            run_block(run, 4 * width), run_block(run, 4 * width), whole(1, width),
            run_block(run, 1), run_block(1, 1, run), run_block(run, 1),
        ],
        out_specs=[run_block(run, width)] * 4
        + [run_block(1, chunks, width)]
        + [run_block(1, heads, HD, HD)] * 2
        + [run_block(1, 1, width)],
        out_shape=[
            shape((tokens, width), f32),
            shape((tokens, width), bf16),
            shape((tokens, width), bf16),
            shape((tokens, width), bf16),
            shape((runs, chunks, width), f32),
            shape((runs, heads, HD, HD), f32),
            shape((runs, heads, HD, HD), bf16),
            shape((runs, 1, width), f32),
        ],
        cost_estimate=COST,
        name="recurrence_local",
    )(keep, recv, bound, *ids)


def recurrence_enter(place, seg, segd, peer, peerd, reverse):
    return pl.pallas_call(
        partial(enter_kernel, reverse),
        in_specs=[SMEM] + [VMEM] * 4,
        out_specs=VMEM,
        out_shape=shape(seg.shape, f32),
        cost_estimate=COST,
        name="recurrence_enter_back" if reverse else "recurrence_enter",
    )(place, seg, segd, peer, peerd)


def recurrence_finish(local, enter, keep, recv, gain):
    inner, qh, kh, vb, decay = local
    runs, chunks, width = decay.shape
    heads = width // HD
    run = chunks * BLOCK
    tokens = runs * run
    cols = run_block(run, width)
    gate = run_block(run, width, at=3)
    return pl.pallas_call(
        finish_kernel,
        grid=(runs,),
        in_specs=[
            cols, cols, cols, cols, run_block(1, chunks, width), run_block(1, heads, HD, HD),
            gate, gate, whole(1, HD),
        ],
        out_specs=[cols, cols, run_block(1, chunks, heads, HD, HD)],
        out_shape=[
            shape((tokens, width), bf16),
            shape((tokens, width), f32),
            shape((runs, chunks, heads, HD, HD), bf16),
        ],
        cost_estimate=COST,
        name="recurrence_finish",
    )(inner, qh, kh, vb, decay, enter, keep, recv, gain)


def recurrence_back_local(kd, rd, rec, keep, recv, gain, qh, decay):
    runs, chunks, width = decay.shape
    heads = width // HD
    run = chunks * BLOCK
    tokens = runs * run
    cols = run_block(run, width)
    gate = run_block(run, width, at=3)
    return pl.pallas_call(
        back_local_kernel,
        grid=(runs,),
        in_specs=[
            cols, cols, cols, gate, gate, whole(1, HD), cols, run_block(1, chunks, width),
        ],
        out_specs=[cols, cols, whole(1, HD)] + [run_block(1, heads, HD, HD)] * 2,
        out_shape=[
            shape((tokens, width), bf16),
            shape((tokens, width), bf16),
            shape((1, HD), f32),
            shape((runs, heads, HD, HD), f32),
            shape((runs, heads, HD, HD), bf16),
        ],
        cost_estimate=COST,
        name="recurrence_back_local",
    )(kd, rd, rec, keep, recv, gain, qh, decay)


def recurrence_back_finish(keep, recv, bound, ids, local, states, do, enter):
    _, qh, kh, vb, decay = local
    runs, chunks, width = decay.shape
    heads = width // HD
    run = chunks * BLOCK
    tokens = runs * run
    cols = run_block(run, width)
    return pl.pallas_call(
        back_finish_kernel,
        grid=(runs,),
        in_specs=[
            run_block(run, 4 * width), run_block(run, 4 * width), whole(1, width),
            run_block(run, 1), run_block(1, 1, run), run_block(run, 1),
            cols, cols, cols, run_block(1, chunks, width),
            run_block(1, chunks, heads, HD, HD), cols, run_block(1, heads, HD, HD),
        ],
        out_specs=[run_block(run, 3 * width), whole(1, width)],
        out_shape=[shape((tokens, 3 * width), bf16), shape((1, width), f32)],
        cost_estimate=COST,
        name="recurrence_back_finish",
    )(keep, recv, bound, *ids, qh, kh, vb, decay, states, do, enter)


def swap_group(x):
    return lax.ppermute(x, "dp", [(0, 1), (1, 0)])


def up(x):
    return lax.ppermute(x, "col", UP)


def down(x):
    return lax.ppermute(x, "col", DOWN)


def step(sends, work=None, given=(), join=()):
    n = len(sends)
    arrays = lax.optimization_barrier((*(array for _, array in sends), *given))
    moved = [mover(array) for (mover, _), array in zip(sends, arrays)]
    made = tuple(work(*arrays[n:])) if work else ()
    ends = made[:1] if getattr(work, "marked", False) else made
    done = lax.optimization_barrier((*moved, *ends, *join))
    made = made[1:] if getattr(work, "marked", False) else done[n : n + len(made)]
    return list(done[:n]), list(made), list(done[n + len(ends) :])


def aside(ready, work):
    def marked(*given):
        return (jnp.ones((), f32), *work(*given))

    def run(*given):
        shapes = jax.eval_shape(marked, *given)
        return lax.cond(
            ready, marked, lambda *a: tuple(jnp.zeros(s.shape, s.dtype) for s in shapes), *given
        )

    run.marked = True
    return run


def ordered(own, other):
    return jnp.concatenate(own, 0), jnp.concatenate([other[0], *other[:0:-1]], 0)


def cut(array, count):
    each = -(-array.shape[0] // count)
    each = -(-each // 16) * 16
    return [array[at : at + each] for at in range(0, array.shape[0], each)]


def shards(
    tokens,
    segments,
    mix_gain,
    w_mix,
    lower_bound,
    group_gain,
    w_out,
    ffn_gain,
    w_ffn_in,
    w_down,
    cotangent,
):
    row = lax.axis_index("row")
    core = row % 2
    y = row // 2
    z = lax.axis_index("col")
    count = lax.axis_size("col")
    pairs = lax.axis_size("dp") == 2
    half = tokens.shape[0] // 2
    width = tokens.shape[1]
    hc = w_mix.shape[2] // 2
    units_col = w_down.shape[0]
    here = count * half
    hb = here // 2
    ready = segments[0] >= 0

    def mine(x, at, size, axis):
        return lax.dynamic_slice_in_dim(x, at * size, size, axis)

    def rows(x, at):
        return mine(x, at, hb, 0)

    def joined(first_if_zero, second_if_zero, flag, axis):
        return jnp.where(
            flag == 0,
            jnp.concatenate([first_if_zero, second_if_zero], axis),
            jnp.concatenate([second_if_zero, first_if_zero], axis),
        )

    def blocks(array):
        return [array[k * half : (k + 1) * half] for k in range(count)]

    tok_own = mine(tokens, y, half, 0)
    (tok_other,), _, _ = step([(swap_chip, mine(tokens, 1 - y, half, 0))])
    cot_own, cot_send = mine(cotangent, y, half, 0), mine(cotangent, 1 - y, half, 0)
    wm_parts = cut(w_mix, 4)
    first = swap_chip(tie(wm_parts[0], tok_other))
    gains_other = swap_chip(tie(jnp.stack([mix_gain, ffn_gain]), tok_other))
    x_own, x_other = tok_own.astype(f32), tok_other.astype(f32)
    squares = jnp.sum(x_own * x_own, axis=1) + jnp.sum(x_other * x_other, axis=1)
    squares = squares + swap_core(squares)
    mix_scale = lax.rsqrt(squares / D + norm_eps)[:, None]
    mo = [(x_own * mix_scale * mix_gain).astype(bf16)]
    mp = [(x_other * mix_scale * gains_other[0]).astype(bf16)]
    wm = [first]
    for k in range(1, count):
        sends = [(up, mo[-1]), (down, mp[-1])]
        sends.append((swap_chip, cot_send if k == 1 else wm_parts[k - 1]))
        (a, b, got), _, late = step(sends, join=wm if k == 1 else [])
        if k == 1:
            wm, cot_other = late, got
        else:
            wm.append(got)
        mo.append(a)
        mp.append(b)
    co, cp = [cot_own], [cot_other]
    (a, b, got, mo[-1], mp[-1]), _, _ = step(
        [(up, cot_own), (down, cot_other), (swap_chip, wm_parts[3])]
        + [(lambda v: v, mo[-1]), (lambda v: v, mp[-1])]
    )
    co.append(a)
    cp.append(b)
    wm_other = jnp.concatenate([*wm, got], 0)
    m_own, m_other = ordered(mo, mp)

    def columns(w, at):
        return mine(w, at, hc, 2).reshape(width, 4 * hc)

    wm_keep, wm_send = columns(w_mix, core), columns(w_mix, 1 - core)
    wm_keep_o, wm_send_o = columns(wm_other, core), columns(wm_other, 1 - core)

    names = segments.astype(f32)
    before = jnp.concatenate([jnp.full((1,), -1.0, f32), names[:-1]])

    def runs_of(array):
        array = lax.dynamic_index_in_dim(array.reshape(count, 2, half), y, 1, keepdims=False)
        places = [(z - k + count) % count for k in range(count)]
        return jnp.stack(
            [lax.dynamic_index_in_dim(array, at, 0, keepdims=False) for at in places]
        )

    names, before = runs_of(names), runs_of(before)
    ids = (names.reshape(here, 1), names.reshape(count, 1, half), before.reshape(here, 1))
    bound = mine(lower_bound, core, hc, 0).reshape(1, hc)
    gain_row = group_gain.reshape(1, HD)
    place = jnp.stack([z, y]).astype(jnp.int32)

    send = (mm(m_own, wm_send) + mm(m_other, wm_send_o)).astype(bf16)
    recv = swap_core(send)
    keep = mm(m_own, wm_keep) + mm(m_other, wm_keep_o)
    wf = w_ffn_in.reshape(width, 2 * units_col)
    pieces = cut(w_down, 2) + cut(wf, 5)
    (a, b, wo_o), local, _ = step(
        [(up, co[-1]), (down, cp[-1]), (swap_chip, w_out)],
        lambda keep, recv: recurrence_local(keep, recv, bound, ids),
        (keep, recv),
    )
    co.append(a)
    cp.append(b)
    *local, seg, low, decay = local
    (peer, peer_decay), _, _ = step([(swap_chip, low), (swap_chip, decay)])

    def finish(seg, decay, peer, peer_decay):
        enter = recurrence_enter(place, seg, decay, peer, peer_decay, False)
        return recurrence_finish(local, enter, keep, recv, gain_row)

    (a, b, got), (gated, rec, states), _ = step(
        [(up, co[-1]), (down, cp[-1]), (swap_chip, pieces[0])],
        finish,
        (seg, decay, peer, peer_decay),
    )
    co.append(a)
    cp.append(b)
    weights = [got]
    c_own, c_other = ordered(co, cp)
    gated = joined(gated, swap_core(gated), core, 1)

    def scatter(own, other, beside):
        a, b = own[1], other[-1]
        for k in range(1, count):
            sends, work, given, take = beside(k)
            moved, made, _ = step([(up, a.astype(bf16)), (down, b.astype(bf16)), *sends], work, given)
            a = moved[0].astype(f32) + own[(k + 1) % count].astype(f32)
            b = moved[1].astype(f32) + other[-(k + 1) % count].astype(f32)
            take(moved[2:], made)
        return a, b

    def gather(own, other, beside):
        own, other = [own], [other]
        for k in range(1, count):
            sends, work, given, take = beside(k)
            moved, made, _ = step([(up, own[-1]), (down, other[-1]), *sends], work, given)
            own.append(moved[0])
            other.append(moved[1])
            take(moved[2:], made)
        return ordered(own, other)

    def weights_step(k):
        return [(swap_chip, pieces[len(weights)])], None, (), lambda moved, made: weights.extend(moved)

    h_own, h_other = scatter(
        blocks(mm(gated, w_out).astype(bf16)), blocks(mm(gated, wo_o).astype(bf16)), weights_step
    )
    h_own, h_other = x_own + h_own, x_other + h_other

    squares = jnp.sum(h_own * h_own, axis=1) + jnp.sum(h_other * h_other, axis=1)
    squares = squares + swap_core(squares)
    ffn_scale = lax.rsqrt(squares / D + norm_eps)[:, None]
    n_own = (h_own * ffn_scale * ffn_gain).astype(bf16)
    n_other = (h_other * ffn_scale * gains_other[1]).astype(bf16)

    wd_o = jnp.concatenate(weights[:2], 0)
    gu_recv = swap_core(
        (mm_nt(rows(c_own, 1 - core), w_down) + mm_nt(rows(c_other, 1 - core), wd_o)).astype(bf16)
    )
    gu = mm_nt(rows(c_own, core), w_down) + mm_nt(rows(c_other, core), wd_o) + gu_recv.astype(f32)
    f_own, f_other = gather(n_own, n_other, weights_step)
    wf_o = jnp.concatenate(weights[2:], 0)
    f_own, gu = lax.optimization_barrier((f_own, gu))
    fk_own, fs_own = rows(f_own, core), rows(f_own, 1 - core)
    fk_other, fs_other = rows(f_other, core), rows(f_other, 1 - core)
    b_recv = swap_core((mm(fs_own, wf) + mm(fs_other, wf_o)).astype(bf16))
    both = mm(fk_own, wf) + mm(fk_other, wf_o) + b_recv.astype(f32)
    gate, up_part = both[:, :units_col], both[:, units_col:]
    sigma = jax.nn.sigmoid(gate)
    act = gate * sigma
    units = (act * up_part).astype(bf16)
    gb = jnp.concatenate(
        [(gu * up_part * silu_slope(gate, sigma)).astype(bf16), (gu * act).astype(bf16)], 1
    )
    gb_p = swap_core(gb)
    units_p = swap_core(tie(units, gb))
    df_kept = [mm_nt(gb, wf).astype(bf16), mm_nt(gb, wf_o).astype(bf16)]
    df_sent = [mm_nt(gb_p, wf).astype(bf16), mm_nt(gb_p, wf_o).astype(bf16)]
    ck_own, cs_own = rows(c_own, core), rows(c_own, 1 - core)
    ck_other, cs_other = rows(c_other, core), rows(c_other, 1 - core)
    down_sent = cut((mm_tn(units, ck_other) + mm_tn(units_p, cs_other)).astype(bf16), 2)

    def by_core(kept, sent):
        each = count // 2
        parts = []
        for k in range(count):
            s = slice(k % each * half, (k % each + 1) * half)
            parts.append(jnp.where(core == k // each, kept[s], sent[s]))
        return parts

    y_queue, x_queue, x_done, own_parts = [], [], [], {}

    def background(take_more=None, work=None, given=(), y_pieces=1, x_pieces=1):
        sends, keys = [], []
        for _ in range(min(y_pieces, len(y_queue))):
            key, array = y_queue.pop(0)
            keys.append(key)
            sends.append((swap_chip, array))
        n = len(sends)
        moving = [x_queue.pop(0) for _ in range(min(x_pieces, len(x_queue)))]
        if pairs:
            sends += [(swap_group, array) for _, array in moving]

        def take(moved, made):
            if take_more is not None:
                take_more(made)
            for key, got in zip(keys, moved[:n]):
                x_queue.append((key, (own_parts[key] + got.astype(f32)).astype(bf16)))
            for n_moved, (key, array) in enumerate(moving):
                if pairs:
                    value = array.astype(f32) + moved[n + n_moved].astype(f32)
                else:
                    value = lax.psum(array, "dp").astype(f32)
                x_done.append((key, value))

        return sends, work, given, take

    def queue(name, parts):
        y_queue.extend((f"{name}{n}", part) for n, part in enumerate(parts))

    def hold(name, parts):
        own_parts.update((f"{name}{n}", part) for n, part in enumerate(parts))

    queue("d", down_sent)

    def ffn_step(k):
        if k == 1:

            def take(made):
                hold("d", made[:2])
                queue("f", made[2:])

            def work(u, v, c, d, f, h, g, p):
                grad = (mm_tn(f, g) + mm_tn(h, p)).astype(bf16)
                return (*cut(mm_tn(u, c) + mm_tn(v, d), 2), *cut(grad, 4))

            given = (units, units_p, ck_own, cs_own, fk_other, fs_other, gb, gb_p)
            return background(take, aside(ready, work), given)
        if k == 2:

            def work(f, h, g, p):
                return cut(mm_tn(f, g) + mm_tn(h, p), 4)

            return background(
                lambda made: hold("f", made), aside(ready, work), (fk_own, fs_own, gb, gb_p)
            )

        def work(u, v, w, o):
            return [mm(a, b).astype(bf16) for b in (w, o) for a in (u, v)]

        return background(kept.extend, aside(ready, work), (units, units_p, w_down, wd_o))

    kept = []
    df_own, df_other = scatter(
        by_core(df_kept[0], df_sent[0]), by_core(df_kept[1], df_sent[1]), ffn_step
    )
    un_own, un_other = by_core(*kept[:2]), by_core(*kept[2:])

    gain_fo = gains_other[1]
    w_o, w_p = df_own * ffn_gain, df_other * gain_fo
    along = jnp.sum(w_o * h_own, axis=1) + jnp.sum(w_p * h_other, axis=1)
    along = along + swap_core(along)
    factor = ffn_scale**3 * along[:, None] / D
    gh_own = cot_own.astype(f32) + ffn_scale * w_o - h_own * factor
    gh_other = cot_other.astype(f32) + ffn_scale * w_p - h_other * factor
    ffn_part = jnp.sum(df_own * h_own * ffn_scale, axis=0)
    ffn_part_o = jnp.sum(df_other * h_other * ffn_scale, axis=0)
    g_own, g_other = gather(
        gh_own.astype(bf16), gh_other.astype(bf16), lambda k: background()
    )

    gg_recv = swap_core(
        (mm_nt(g_own, mine(w_out, 1 - core, hc, 0)) + mm_nt(g_other, mine(wo_o, 1 - core, hc, 0)))
        .astype(bf16)
    )
    gg_keep = mm_nt(g_own, mine(w_out, core, hc, 0)) + mm_nt(g_other, mine(wo_o, core, hc, 0))
    out_sent = mm_tn(gated, g_other).astype(bf16)
    do, d_gate, group_part, seg, low = recurrence_back_local(
        gg_keep, gg_recv, rec, keep, recv, gain_row, local[1], local[4]
    )
    (peer, d_gate_p), _, _ = step([(swap_chip, low), (swap_core, d_gate)])

    def finish_back(seg, peer):
        enter = recurrence_enter(place, seg, decay, peer, peer_decay, True)
        return recurrence_back_finish(keep, recv, bound, ids, local, states, do, enter)

    queue("o", [out_sent])
    out_a, out_b = un_own[1], un_other[-1]
    sends, _, _, take = background(y_pieces=1, x_pieces=1)
    moved, (d_three, bound_part), _ = step(
        [(up, out_a), (down, out_b), *sends], finish_back, (seg, peer)
    )
    out_a = (moved[0].astype(f32) + un_own[2].astype(f32)).astype(bf16)
    out_b = (moved[1].astype(f32) + un_other[2].astype(f32)).astype(bf16)
    hold("o", [mm_tn(gated, g_own)])
    take(moved[2:], [])

    d_three_p = swap_core(d_three)

    def part(p):
        if p == 3:
            return joined(d_gate, d_gate_p, core, 1)
        s = slice(p * hc, (p + 1) * hc)
        return joined(d_three[:, s], d_three_p[:, s], core, 1)

    sums_own = mm_nt(d_three, wm_keep[:, : 3 * hc]) + mm_nt(d_gate, wm_keep[:, 3 * hc :])
    sums_own += mm_nt(d_three_p, wm_send[:, : 3 * hc]) + mm_nt(d_gate_p, wm_send[:, 3 * hc :])
    sums_other = mm_nt(d_three, wm_keep_o[:, : 3 * hc]) + mm_nt(d_gate, wm_keep_o[:, 3 * hc :])
    sums_other += mm_nt(d_three_p, wm_send_o[:, : 3 * hc]) + mm_nt(d_gate_p, wm_send_o[:, 3 * hc :])
    parts = {name: part(p) for p, name in enumerate("qkvg")}

    for name in "gqkv":
        queue(name, [mm_tn(m_other, parts[name]).astype(bf16)])
        hold(name, [mm_tn(m_own, parts[name])])
    dx_own, dx_other = scatter(
        blocks(sums_own.astype(bf16)),
        blocks(sums_other.astype(bf16)),
        lambda k: background(None, None, (), 2 if k == 1 else 1, 2 if k == 3 else 1),
    )
    mix_part = jnp.sum(sums_own * m_own.astype(f32), axis=0) / mix_gain
    mix_part_o = jnp.sum(sums_other * m_other.astype(f32), axis=0) / gains_other[0]
    tail = jnp.concatenate([bound_part[0], group_part[0]])
    small = jnp.concatenate([mix_part, ffn_part, tail])
    small_o = jnp.concatenate([mix_part_o, ffn_part_o, tail])
    sends, _, _, take = background(None, None, (), 1, 1)
    moved, _, _ = step([(up, out_a), (down, out_b), (swap_chip, small_o), *sends])
    out_a = (moved[0].astype(f32) + un_own[3].astype(f32)).astype(bf16)
    out_b = (moved[1].astype(f32) + un_other[1].astype(f32)).astype(bf16)
    small = small + moved[2]
    take(moved[3:], [])

    w_o, w_p = dx_own * mix_gain, dx_other * gains_other[0]
    along = jnp.sum(w_o * x_own, axis=1) + jnp.sum(w_p * x_other, axis=1)
    along = along + swap_core(along)
    factor = mix_scale**3 * along[:, None] / D
    gt_own = gh_own + mix_scale * w_o - x_own * factor
    gt_other = gh_other + mix_scale * w_p - x_other * factor
    sends, _, _, take = background(None, None, (), 1, 2)
    if pairs:
        sends.append((swap_group, small))
    moved, _, _ = step([(up, out_a), (down, out_b), (swap_chip, gt_other.astype(bf16)), *sends])
    out_own = (h_own + moved[0].astype(f32) + un_own[0].astype(f32)).astype(bf16)
    out_other = (h_other + moved[1].astype(f32) + un_other[0].astype(f32)).astype(bf16)
    grad_other = moved[2].astype(f32)
    small = small + moved[-1] if pairs else lax.psum(small, "dp")
    take(moved[3:-1] if pairs else moved[3:], [])
    edge = 2 * width
    bound_sum = small[edge : edge + hc]
    wide = jnp.concatenate([small[:edge], small[edge + hc :]])
    near = lambda a: lax.ppermute(a, "col", [(i, i ^ 1) for i in range(count)])
    far = lambda a: lax.ppermute(a, "col", [(i, i ^ 2) for i in range(count)])
    sends, _, _, take = background(None, None, (), 1, 2)
    moved, _, _ = step([(swap_chip, out_other), (near, wide), *sends])
    out_other = moved[0]
    wide = wide + moved[1]
    take(moved[2:], [])
    while y_queue or x_queue:
        sends, _, _, take = background(None, None, (), 1, 2)
        moved, _, _ = step(sends) if sends else ([], [], [])
        take(moved, [])
    wide = wide + far(wide)
    turned = swap_core(jnp.concatenate([bound_sum, wide[edge:]]))
    grad_bound = joined(bound_sum, turned[:hc], core, 0)
    found = dict(x_done)

    def all_of(name, parts):
        return jnp.concatenate([found[f"{name}{n}"] for n in range(parts)], 0)

    return (
        joined(out_own, out_other, y, 0),
        joined(gt_own, grad_other, y, 0),
        wide[:width],
        jnp.stack([found["q0"], found["k0"], found["v0"], found["g0"]], 1),
        grad_bound,
        wide[edge:] + turned[hc:],
        found["o0"],
        wide[width:edge],
        all_of("f", 4).reshape(width, 2, units_col),
        all_of("d", 2),
    )


def solution(mesh):
    return jax.shard_map(
        shards,
        mesh=mesh,
        in_specs=(
            P(("dp", "col"), "row"),
            P("dp"),
            P("row"),
            P("row", None, "col"),
            P("col"),
            P(),
            P("col", "row"),
            P("row"),
            P("row", None, "col"),
            P("col", "row"),
            P(("dp", "col"), "row"),
        ),
        out_specs=(
            P(("dp", "col"), "row"),
            P(("dp", "col"), "row"),
            P("row"),
            P("row", None, "col"),
            P("col"),
            P(),
            P("col", "row"),
            P("row"),
            P("row", None, "col"),
            P("col", "row"),
        ),
        check_vma=False,
    )
```

```python
from functools import partial

import jax
import jax.numpy as jnp
from jax import lax
from jax.experimental import pallas as pl
from jax.experimental.pallas import tpu as pltpu
from jax.sharding import PartitionSpec as P

D = 2048
HD = 128
BLOCK = 64
norm_eps = 1e-06
bf16 = jnp.bfloat16
f32 = jnp.float32

CORE = [(0, 1), (1, 0), (2, 3), (3, 2)]
CHIP = [(0, 2), (2, 0), (1, 3), (3, 1)]


def swap_core(x):
    return lax.ppermute(x, "row", CORE)


def swap_chip(x):
    return lax.ppermute(x, "row", CHIP)


def tie(x, *others):
    return lax.optimization_barrier((x, *others))[0]


def mm(left, right):
    return lax.dot_general(left, right, (((1,), (0,)), ((), ())), preferred_element_type=f32)


def mm_nt(left, right):
    return lax.dot_general(left, right, (((1,), (1,)), ((), ())), preferred_element_type=f32)


def mm_tn(left, right):
    return lax.dot_general(left, right, (((0,), (0,)), ((), ())), preferred_element_type=f32)


def silu_slope(value, sigma):
    return sigma * (1.0 + value * (1.0 - sigma))


def split_mm(left, value):
    high = value.astype(bf16)
    low = (value - high.astype(f32)).astype(bf16)
    return mm(left, high) + mm(left, low)


def run_masks(i, idc_ref, idr_ref, prev_ref):
    s = slice(i * BLOCK, (i + 1) * BLOCK)
    idc = idc_ref[s, :]
    idr = idr_ref[0, :, s]
    prev = prev_ref[s, :]
    before = prev[0:1, :]
    last = idc[BLOCK - 1 : BLOCK, :]
    t = lax.broadcasted_iota(jnp.int32, (BLOCK, BLOCK), 0)
    u = lax.broadcasted_iota(jnp.int32, (BLOCK, BLOCK), 1)
    same = idc == idr
    heads = (idc == before).astype(f32)
    tails = (idc == last).astype(f32)
    through = (last == before).astype(f32)
    old = (idc == prev).astype(f32)
    return t, u, same, heads, tails, through, old


def run_decays(f_raw, lb, t, u):
    closed = jax.nn.sigmoid(-f_raw)
    keys = (1.0 - lb) * closed
    total = split_mm((t >= u).astype(bf16), jnp.log1p(-keys))
    middle = total[BLOCK // 2 - 1 : BLOCK // 2, :]
    final = total[BLOCK - 1 : BLOCK, :]
    return closed, keys, total, middle, final


def col(h, part=0, heads=1):
    start = (part * heads + h) * HD
    return slice(start, start + HD)


def local_kernel(
    keep_ref, recv_ref, lb_ref, idc_ref, idr_ref, prev_ref,
    inner_ref, qh_ref, kh_ref, vb_ref, decay_ref, seg_ref, low_ref, segd_ref,
):
    heads = lb_ref.shape[1] // HD
    state = [jnp.zeros((HD, HD), f32)] * heads
    passing = [jnp.ones((1, HD), f32)] * heads
    for i in range(keep_ref.shape[0] // BLOCK):
        s = slice(i * BLOCK, (i + 1) * BLOCK)
        t, u, same, head, tails, through, _ = run_masks(i, idc_ref, idr_ref, prev_ref)
        for h in range(heads):
            c = col(h)

            def raw(part):
                p = col(h, part, heads)
                return keep_ref[s, p] + recv_ref[s, p].astype(f32)

            q_raw = raw(0)
            vb = raw(2).astype(bf16)
            q = q_raw * jax.nn.sigmoid(q_raw)
            _, keys, total, middle, final = run_decays(raw(1), lb_ref[:, c], t, u)
            qt = (q * jnp.exp(total - middle)).astype(bf16)
            kt = (keys * jnp.exp(middle - total)).astype(bf16)
            scores = jnp.where(same & (t >= u), mm_nt(qt, kt), 0.0).astype(bf16)
            inner_ref[s, c] = mm(scores, vb)
            qh_ref[s, c] = (q * jnp.exp(total) * head).astype(bf16)
            kh = (keys * jnp.exp(final - total) * tails).astype(bf16)
            kh_ref[s, c] = kh
            vb_ref[s, c] = vb
            keep = jnp.exp(final) * through
            decay_ref[0, i : i + 1, c] = keep
            state[h] = keep * state[h] + mm_tn(vb, kh)
            passing[h] = passing[h] * keep
    for h in range(heads):
        seg_ref[0, h] = state[h]
        low_ref[0, h] = state[h].astype(bf16)
        segd_ref[0, :, col(h)] = passing[h]


def enter_kernel(reverse, place_ref, seg_ref, segd_ref, peer_ref, peerd_ref, out_ref):
    z, y = place_ref[0], place_ref[1]
    count, heads = seg_ref.shape[:2]
    peer_first = (y == 0) if reverse else (y == 1)
    state = [jnp.zeros((HD, HD), f32)] * heads
    for place in reversed(range(count)) if reverse else range(count):
        k = lax.rem((z ^ (z >> 1)) - (place ^ (place >> 1)) + count, count)
        for h in range(heads):
            add = peer_ref[k, h].astype(f32)
            scale = peerd_ref[k, :, col(h)]
            s = jnp.where(peer_first, scale, 1.0) * state[h] + jnp.where(peer_first, add, 0.0)
            out_ref[k, h] = s
            s = segd_ref[k, :, col(h)] * s + seg_ref[k, h]
            state[h] = jnp.where(peer_first, 1.0, scale) * s + jnp.where(peer_first, 0.0, add)


def finish_kernel(
    inner_ref, qh_ref, kh_ref, vb_ref, decay_ref, enter_ref, keep_ref, recv_ref, gain_ref,
    gated_ref, rec_ref, st_ref,
):
    heads = enter_ref.shape[1]
    state = [enter_ref[0, h] for h in range(heads)]
    for i in range(qh_ref.shape[0] // BLOCK):
        s = slice(i * BLOCK, (i + 1) * BLOCK)
        for h in range(heads):
            c = col(h)
            low = state[h].astype(bf16)
            st_ref[0, i, h] = low
            rec = inner_ref[s, c] + mm_nt(qh_ref[s, c], low)
            rec_ref[s, c] = rec
            scale = lax.rsqrt(jnp.mean(rec * rec, axis=1, keepdims=True) + norm_eps)
            g_raw = keep_ref[s, c] + recv_ref[s, c].astype(f32)
            gate = g_raw * jax.nn.sigmoid(g_raw)
            gated_ref[s, c] = (rec * scale * gain_ref[...] * gate).astype(bf16)
            state[h] = decay_ref[0, i : i + 1, c] * state[h] + mm_tn(vb_ref[s, c], kh_ref[s, c])


def back_local_kernel(
    kd, rd, rec_ref, keep_ref, recv_ref, gain_ref, qh_ref, decay_ref,
    do_ref, dg_ref, group_ref, seg_ref, low_ref,
):
    @pl.when(pl.program_id(0) == 0)
    def _():
        group_ref[...] = jnp.zeros_like(group_ref)

    gain = gain_ref[...]
    heads = seg_ref.shape[1]
    adjoint = [jnp.zeros((HD, HD), f32)] * heads
    group = jnp.zeros((1, HD), f32)
    for i in reversed(range(qh_ref.shape[0] // BLOCK)):
        s = slice(i * BLOCK, (i + 1) * BLOCK)
        for h in range(heads):
            c = col(h)
            grad = kd[s, c] + rd[s, c].astype(f32)
            rec = rec_ref[s, c]
            scale = lax.rsqrt(jnp.mean(rec * rec, axis=1, keepdims=True) + norm_eps)
            normed = rec * scale
            g_raw = keep_ref[s, c] + recv_ref[s, c].astype(f32)
            sigma = jax.nn.sigmoid(g_raw)
            act = g_raw * sigma
            both = grad * normed
            group = group + jnp.sum(both * act, axis=0, keepdims=True)
            dg_ref[s, c] = (both * gain * silu_slope(g_raw, sigma)).astype(bf16)
            dn = grad * gain * act
            do = (scale * (dn - normed * jnp.mean(dn * normed, axis=1, keepdims=True))).astype(bf16)
            do_ref[s, c] = do
            adjoint[h] = decay_ref[0, i : i + 1, c] * adjoint[h] + mm_tn(do, qh_ref[s, c])
    group_ref[...] += group
    for h in range(heads):
        seg_ref[0, h] = adjoint[h]
        low_ref[0, h] = adjoint[h].astype(bf16)


def back_finish_kernel(
    keep_ref, recv_ref, lb_ref, idc_ref, idr_ref, prev_ref,
    qh_ref, kh_ref, vb_ref, decay_ref, st_ref, do_ref, enter_ref,
    grad_ref, bound_ref,
):
    @pl.when(pl.program_id(0) == 0)
    def _():
        bound_ref[...] = jnp.zeros_like(bound_ref)

    heads = enter_ref.shape[1]
    adjoint = [enter_ref[0, h] for h in range(heads)]
    bound = [jnp.zeros((1, HD), f32)] * heads
    for i in reversed(range(keep_ref.shape[0] // BLOCK)):
        s = slice(i * BLOCK, (i + 1) * BLOCK)
        t, u, same, head, tails, through, old = run_masks(i, idc_ref, idr_ref, prev_ref)
        causal = same & (t >= u)
        later = (same & (u >= t)).astype(bf16)
        for h in range(heads):
            c = col(h)

            def raw(part):
                p = col(h, part, heads)
                return keep_ref[s, p] + recv_ref[s, p].astype(f32)

            q_raw = raw(0)
            sigma = jax.nn.sigmoid(q_raw)
            q = q_raw * sigma
            closed, keys, total, middle, final = run_decays(raw(1), lb_ref[:, c], t, u)
            out = jnp.exp(total - middle)
            back = jnp.exp(middle - total)
            qt = (q * out).astype(bf16)
            kt = (keys * back).astype(bf16)
            scores = jnp.where(causal, mm_nt(qt, kt), 0.0).astype(bf16)
            vb = vb_ref[s, c]
            kh = kh_ref[s, c]
            do = do_ref[s, c]
            st = st_ref[0, i, h]
            low = adjoint[h].astype(bf16)
            keep = decay_ref[0, i : i + 1, c]
            ds = jnp.where(causal, mm_nt(do, vb), 0.0).astype(bf16)
            dq = mm(ds, kt) * out + mm(do, st) * (jnp.exp(total) * head)
            dkh = mm(vb, low)
            dk = mm_tn(ds, qt) * back + dkh * (jnp.exp(final - total) * tails)
            grad_ref[s, col(h, 2, heads)] = (mm_tn(scores, do) + mm_nt(kh, low)).astype(bf16)
            ends = keep * jnp.sum(adjoint[h] * st.astype(f32), axis=0, keepdims=True) + jnp.sum(
                kh.astype(f32) * dkh, axis=0, keepdims=True
            )
            dlog = split_mm(later, q * dq - keys * dk) + tails * ends
            key_total = dk - old * dlog / (1.0 - keys)
            bound[h] = bound[h] - jnp.sum(key_total * closed, axis=0, keepdims=True)
            grad_ref[s, col(h, 1, heads)] = (-key_total * keys * (1.0 - closed)).astype(bf16)
            grad_ref[s, col(h, 0, heads)] = (dq * silu_slope(q_raw, sigma)).astype(bf16)
            adjoint[h] = keep * adjoint[h] + mm_tn(do, qh_ref[s, c])
    for h in range(heads):
        bound_ref[:, col(h)] += bound[h]


def shape(dims, kind):
    return jax.ShapeDtypeStruct(dims, kind)


COST = pl.CostEstimate(flops=0, bytes_accessed=0, transcendentals=0)
SMEM = pl.BlockSpec(memory_space=pltpu.SMEM)
VMEM = pl.BlockSpec(memory_space=pltpu.VMEM)


def run_block(*dims, at=0):
    return pl.BlockSpec(dims, lambda j: (j, *([0] * (len(dims) - 2)), at))


def whole(*dims):
    return pl.BlockSpec(dims, lambda j: (0,) * len(dims))


def recurrence_local(keep, recv, bound, ids):
    runs, _, run = ids[1].shape
    width = bound.shape[1]
    heads = width // HD
    chunks = run // BLOCK
    tokens = runs * run
    return pl.pallas_call(
        local_kernel,
        grid=(runs,),
        in_specs=[
            run_block(run, 4 * width), run_block(run, 4 * width), whole(1, width),
            run_block(run, 1), run_block(1, 1, run), run_block(run, 1),
        ],
        out_specs=[run_block(run, width)] * 4
        + [run_block(1, chunks, width)]
        + [run_block(1, heads, HD, HD)] * 2
        + [run_block(1, 1, width)],
        out_shape=[
            shape((tokens, width), f32),
            shape((tokens, width), bf16),
            shape((tokens, width), bf16),
            shape((tokens, width), bf16),
            shape((runs, chunks, width), f32),
            shape((runs, heads, HD, HD), f32),
            shape((runs, heads, HD, HD), bf16),
            shape((runs, 1, width), f32),
        ],
        cost_estimate=COST,
        name="recurrence_local",
    )(keep, recv, bound, *ids)


def recurrence_enter(place, seg, segd, peer, peerd, reverse):
    return pl.pallas_call(
        partial(enter_kernel, reverse),
        in_specs=[SMEM] + [VMEM] * 4,
        out_specs=VMEM,
        out_shape=shape(seg.shape, f32),
        cost_estimate=COST,
        name="recurrence_enter_back" if reverse else "recurrence_enter",
    )(place, seg, segd, peer, peerd)


def recurrence_finish(local, enter, keep, recv, gain):
    inner, qh, kh, vb, decay = local
    runs, chunks, width = decay.shape
    heads = width // HD
    run = chunks * BLOCK
    tokens = runs * run
    cols = run_block(run, width)
    gate = run_block(run, width, at=3)
    return pl.pallas_call(
        finish_kernel,
        grid=(runs,),
        in_specs=[
            cols, cols, cols, cols, run_block(1, chunks, width), run_block(1, heads, HD, HD),
            gate, gate, whole(1, HD),
        ],
        out_specs=[cols, cols, run_block(1, chunks, heads, HD, HD)],
        out_shape=[
            shape((tokens, width), bf16),
            shape((tokens, width), f32),
            shape((runs, chunks, heads, HD, HD), bf16),
        ],
        cost_estimate=COST,
        name="recurrence_finish",
    )(inner, qh, kh, vb, decay, enter, keep, recv, gain)


def recurrence_back_local(kd, rd, rec, keep, recv, gain, qh, decay):
    runs, chunks, width = decay.shape
    heads = width // HD
    run = chunks * BLOCK
    tokens = runs * run
    cols = run_block(run, width)
    gate = run_block(run, width, at=3)
    return pl.pallas_call(
        back_local_kernel,
        grid=(runs,),
        in_specs=[
            cols, cols, cols, gate, gate, whole(1, HD), cols, run_block(1, chunks, width),
        ],
        out_specs=[cols, cols, whole(1, HD)] + [run_block(1, heads, HD, HD)] * 2,
        out_shape=[
            shape((tokens, width), bf16),
            shape((tokens, width), bf16),
            shape((1, HD), f32),
            shape((runs, heads, HD, HD), f32),
            shape((runs, heads, HD, HD), bf16),
        ],
        cost_estimate=COST,
        name="recurrence_back_local",
    )(kd, rd, rec, keep, recv, gain, qh, decay)


def recurrence_back_finish(keep, recv, bound, ids, local, states, do, enter):
    _, qh, kh, vb, decay = local
    runs, chunks, width = decay.shape
    heads = width // HD
    run = chunks * BLOCK
    tokens = runs * run
    cols = run_block(run, width)
    return pl.pallas_call(
        back_finish_kernel,
        grid=(runs,),
        in_specs=[
            run_block(run, 4 * width), run_block(run, 4 * width), whole(1, width),
            run_block(run, 1), run_block(1, 1, run), run_block(run, 1),
            cols, cols, cols, run_block(1, chunks, width),
            run_block(1, chunks, heads, HD, HD), cols, run_block(1, heads, HD, HD),
        ],
        out_specs=[run_block(run, 3 * width), whole(1, width)],
        out_shape=[shape((tokens, 3 * width), bf16), shape((1, width), f32)],
        cost_estimate=COST,
        name="recurrence_back_finish",
    )(keep, recv, bound, *ids, qh, kh, vb, decay, states, do, enter)


def weight_kernel(pairs, *refs):
    lefts, rights = refs[:pairs], refs[pairs : 2 * pairs]
    *plus, out = refs[2 * pairs :]
    total = sum(mm_tn(left[...], right[...]) for left, right in zip(lefts, rights))
    out[...] = (total + sum(part[...].astype(f32) for part in plus)).astype(out.dtype)


def weight_gradients(lefts, rights, plus=(), rows=None, columns=None, tile=256):
    at, tall = rows or (0, lefts[0].shape[1])
    first, wide = columns or (0, rights[0].shape[1])
    tiles = wide // tile
    out = pl.BlockSpec((tall, tile), lambda j: (0, j))
    return pl.pallas_call(
        partial(weight_kernel, len(lefts)),
        grid=(tiles,),
        in_specs=[pl.BlockSpec((left.shape[0], tall), lambda j: (0, at)) for left in lefts]
        + [pl.BlockSpec((r.shape[0], tile), lambda j: (0, first * tiles + j)) for r in rights]
        + [out] * len(plus),
        out_specs=out,
        out_shape=shape((tall, wide), bf16),
        cost_estimate=COST,
        name="weight_gradients",
    )(*lefts, *rights, *plus)


def pieces_kernel(pairs, *refs):
    lefts, rights, outs = refs[:pairs], refs[pairs : 2 * pairs], refs[2 * pairs :]
    total = sum(mm_tn(left[...], right[...]) for left, right in zip(lefts, rights))
    each = outs[0].shape[0]
    for n, out in enumerate(outs):
        out[...] = total[n * each : (n + 1) * each].astype(out.dtype)


def weight_gradient_pieces(lefts, rights, kind, pieces, tile=256):
    tall, wide = lefts[0].shape[1] // pieces, rights[0].shape[1]
    return pl.pallas_call(
        partial(pieces_kernel, len(lefts)),
        grid=(wide // tile,),
        in_specs=[whole(*left.shape) for left in lefts]
        + [pl.BlockSpec((right.shape[0], tile), lambda j: (0, j)) for right in rights],
        out_specs=[pl.BlockSpec((tall, tile), lambda j: (0, j))] * pieces,
        out_shape=[shape((tall, wide), kind)] * pieces,
        cost_estimate=COST,
        name="weight_gradient_pieces",
    )(*lefts, *rights)


def sum_kernel(own_ref, got_ref, out_ref):
    out_ref[...] = (own_ref[...] + got_ref[...].astype(f32)).astype(bf16)


def rounded_sum(own, got):
    return pl.pallas_call(
        sum_kernel,
        in_specs=[VMEM] * 2,
        out_specs=VMEM,
        out_shape=shape(own.shape, bf16),
        cost_estimate=COST,
        name="rounded_sum",
    )(own, got)


def halves_kernel(pieces, *refs):
    *given, out_ref = refs
    each = len(given) // pieces
    wide = out_ref.shape[2]
    rows = out_ref.shape[0]
    for n in range(pieces):

        @pl.when(pl.program_id(0) == n)
        def _():
            at = pl.ds(pl.multiple_of(pl.program_id(1) * rows, rows), rows)
            for part in range(out_ref.shape[1]):
                cols = slice(part * wide, (part + 1) * wide)
                value = sum(ref[at, cols].astype(f32) for ref in given[n * each : (n + 1) * each])
                out_ref[:, part, :] = value


def halves_of_rows(pieces, parts, rows=32):
    tall, wide = pieces[0][0].shape
    steps = tall // rows
    given = [array for piece in pieces for array in piece]
    return pl.pallas_call(
        partial(halves_kernel, len(pieces)),
        grid=(len(pieces), steps),
        in_specs=[pl.BlockSpec(a.shape, lambda n, j: (0, 0)) for a in given],
        out_specs=pl.BlockSpec((rows, parts, wide // parts), lambda n, j: (n * steps + j, 0, 0)),
        out_shape=shape((len(pieces) * tall, parts, wide // parts), f32),
        cost_estimate=COST,
        compiler_params=pltpu.CompilerParams(vmem_limit_bytes=40 * 2**20),
        name="halves_of_rows",
    )(*given)


def stack_kernel(parts, *refs):
    *given, out_ref = refs
    each = len(given) // parts
    for part in range(parts):
        out_ref[:, part, :] = sum(
            ref[...].astype(f32) for ref in given[part * each : (part + 1) * each]
        )


def stacked(parts, rows=64):
    tall, wide = parts[0][0].shape
    given = [array for part in parts for array in part]
    return pl.pallas_call(
        partial(stack_kernel, len(parts)),
        grid=(tall // rows,),
        in_specs=[pl.BlockSpec((rows, wide), lambda j: (j, 0))] * len(given),
        out_specs=pl.BlockSpec((rows, len(parts), wide), lambda j: (j, 0, 0)),
        out_shape=shape((tall, len(parts), wide), f32),
        cost_estimate=COST,
        name="stacked",
    )(*given)


def product_kernel(right_ref, *refs):
    lefts, outs = refs[: len(refs) // 2], refs[len(refs) // 2 :]
    for left, out in zip(lefts, outs):
        out[...] = mm(left[...], right_ref[...]).astype(out.dtype)


def products(lefts, right, tile=256):
    wide = right.shape[1]
    return pl.pallas_call(
        product_kernel,
        grid=(wide // tile,),
        in_specs=[pl.BlockSpec((right.shape[0], tile), lambda j: (0, j))]
        + [whole(*left.shape) for left in lefts],
        out_specs=[pl.BlockSpec((left.shape[0], tile), lambda j: (0, j)) for left in lefts],
        out_shape=[shape((left.shape[0], wide), bf16) for left in lefts],
        cost_estimate=COST,
        name="products",
    )(right, *lefts)


def heads_kernel(core_ref, left_ref, own_ref, peer_ref, *refs):
    *plus, out_ref = refs
    half = own_ref.shape[1]
    core = core_ref[0]
    for right_ref, at in ((own_ref, core), (peer_ref, 1 - core)):
        cols = pl.ds(pl.multiple_of(at * half, half), half)
        total = mm_tn(left_ref[...], right_ref[...])
        for part in plus:
            total = total + part[:, cols].astype(f32)
        out_ref[:, cols] = total.astype(out_ref.dtype)


def head_gradients(core, left, own, peer, part, half, kind, plus=()):
    block = pl.BlockSpec((own.shape[0], half), lambda j: (0, part))
    out = whole(left.shape[1], 2 * half)
    return pl.pallas_call(
        heads_kernel,
        grid=(1,),
        in_specs=[SMEM, whole(*left.shape), block, block] + [out] * len(plus),
        out_specs=out,
        out_shape=shape((left.shape[1], 2 * half), kind),
        cost_estimate=COST,
        name="head_gradients",
    )(core, left, own, peer, *plus)


def swap_group(x):
    return lax.ppermute(x, "dp", [(0, 1), (1, 0)])


def folded(place):
    return place ^ (place >> 1)


def up(x):
    count = lax.axis_size("col")
    return lax.ppermute(x, "col", [(folded(n), folded((n + 1) % count)) for n in range(count)])


def paired(own, other):
    return jnp.concatenate([own, other], 1)


def step(sends, work=None, given=(), join=()):
    n = len(sends)
    arrays = lax.optimization_barrier((*(array for _, array in sends), *given))
    moved = [mover(array) for (mover, _), array in zip(sends, arrays)]
    made = tuple(work(*arrays[n:])) if work else ()
    done = lax.optimization_barrier((*moved, *made, *join))
    return list(done[:n]), list(done[n : n + len(made)]), list(done[n + len(made) :])


def ordered(runs):
    width = runs[0].shape[1] // 2
    return (
        jnp.concatenate([run[:, :width] for run in runs], 0),
        jnp.concatenate([run[:, width:] for run in runs], 0),
    )


def cut(array, count):
    each = -(-array.shape[0] // count)
    each = -(-each // 16) * 16
    return [array[at : at + each] for at in range(0, array.shape[0], each)]


def shards(
    tokens,
    segments,
    mix_gain,
    w_mix,
    lower_bound,
    group_gain,
    w_out,
    ffn_gain,
    w_ffn_in,
    w_down,
    cotangent,
):
    row = lax.axis_index("row")
    core = row % 2
    y = row // 2
    z = lax.axis_index("col")
    count = lax.axis_size("col")
    pairs = lax.axis_size("dp") == 2
    half = tokens.shape[0] // 2
    width = tokens.shape[1]
    hc = w_mix.shape[2] // 2
    units_col = w_down.shape[0]
    here = count * half
    hb = here // 2

    def mine(x, at, size, axis):
        return lax.dynamic_slice_in_dim(x, at * size, size, axis)

    def rows(x, at):
        return mine(x, at, hb, 0)

    def joined(first_if_zero, second_if_zero, flag, axis):
        return jnp.where(
            flag == 0,
            jnp.concatenate([first_if_zero, second_if_zero], axis),
            jnp.concatenate([second_if_zero, first_if_zero], axis),
        )

    def blocks(array):
        return [array[k * half : (k + 1) * half] for k in range(count)]

    tok_own = mine(tokens, y, half, 0)
    (tok_other,), _, _ = step([(swap_chip, mine(tokens, 1 - y, half, 0))])
    cot_own, cot_send = mine(cotangent, y, half, 0), mine(cotangent, 1 - y, half, 0)
    wm_parts = cut(w_mix, 4)
    first = swap_chip(tie(wm_parts[0], tok_other))
    gains_other = swap_chip(tie(jnp.stack([mix_gain, ffn_gain]), tok_other))
    x_own, x_other = tok_own.astype(f32), tok_other.astype(f32)
    squares = jnp.sum(x_own * x_own, axis=1) + jnp.sum(x_other * x_other, axis=1)
    squares = squares + swap_core(squares)
    mix_scale = lax.rsqrt(squares / D + norm_eps)[:, None]
    m = [
        paired(x_own * mix_scale * mix_gain, x_other * mix_scale * gains_other[0]).astype(bf16)
    ]
    wm = [first]
    for k in range(1, count):
        sends = [(up, m[-1]), (swap_chip, cot_send if k == 1 else wm_parts[k - 1])]
        (a, got), _, late = step(sends, join=wm if k == 1 else [])
        if k == 1:
            wm, cot_other = late, got
        else:
            wm.append(got)
        m.append(a)
    c = [paired(cot_own, cot_other)]
    (a, got, m[-1]), _, _ = step(
        [(up, c[0]), (swap_chip, wm_parts[3]), (lambda v: v, m[-1])]
    )
    c.append(a)
    wm_other = jnp.concatenate([*wm, got], 0)
    m_own, m_other = ordered(m)

    def columns(w, at):
        return mine(w, at, hc, 2).reshape(width, 4 * hc)

    wm_keep, wm_send = columns(w_mix, core), columns(w_mix, 1 - core)
    wm_keep_o, wm_send_o = columns(wm_other, core), columns(wm_other, 1 - core)

    names = segments.astype(f32)
    before = jnp.concatenate([jnp.full((1,), -1.0, f32), names[:-1]])

    def runs_of(array):
        array = lax.dynamic_index_in_dim(array.reshape(count, 2, half), y, 1, keepdims=False)
        places = [folded((folded(z) - k + count) % count) for k in range(count)]
        return jnp.stack(
            [lax.dynamic_index_in_dim(array, at, 0, keepdims=False) for at in places]
        )

    names, before = runs_of(names), runs_of(before)
    ids = (names.reshape(here, 1), names.reshape(count, 1, half), before.reshape(here, 1))
    bound = mine(lower_bound, core, hc, 0).reshape(1, hc)
    gain_row = group_gain.reshape(1, HD)
    place = jnp.stack([z, y]).astype(jnp.int32)

    send = (mm(m_own, wm_send) + mm(m_other, wm_send_o)).astype(bf16)
    recv = swap_core(send)
    keep = mm(m_own, wm_keep) + mm(m_other, wm_keep_o)
    wf = w_ffn_in.reshape(width, 2 * units_col)
    pieces = cut(w_down, 2) + cut(wf, 5)
    (a, wo_o), local, _ = step(
        [(up, c[-1]), (swap_chip, w_out)],
        lambda keep, recv: recurrence_local(keep, recv, bound, ids),
        (keep, recv),
    )
    c.append(a)
    *local, seg, low, decay = local
    (peer, peer_decay), _, _ = step([(swap_chip, low), (swap_chip, decay)])

    def finish(seg, decay, peer, peer_decay):
        enter = recurrence_enter(place, seg, decay, peer, peer_decay, False)
        return recurrence_finish(local, enter, keep, recv, gain_row)

    (a, got), (gated, rec, states), _ = step(
        [(up, c[-1]), (swap_chip, pieces[0])],
        finish,
        (seg, decay, peer, peer_decay),
    )
    c.append(a)
    weights = [got]
    c_own, c_other = ordered(c)
    gated = joined(gated, swap_core(gated), core, 1)

    def scatter(own, other, beside):
        sent = paired(own[1], other[1]).astype(bf16)
        for k in range(1, count):
            sends, work, given, take = beside(k)
            moved, made, _ = step([(up, sent), *sends], work, given)
            at = (k + 1) % count
            a = moved[0][:, :width].astype(f32) + own[at].astype(f32)
            b = moved[0][:, width:].astype(f32) + other[at].astype(f32)
            sent = paired(a, b).astype(bf16)
            take(moved[1:], made)
        return a, b

    def gather(own, other, beside):
        runs = [paired(own, other)]
        for k in range(1, count):
            sends, work, given, take = beside(k)
            moved, made, _ = step([(up, runs[-1]), *sends], work, given)
            runs.append(moved[0])
            take(moved[1:], made)
        return ordered(runs)

    def weights_step(k):
        return [(swap_chip, pieces[len(weights)])], None, (), lambda moved, made: weights.extend(moved)

    h_own, h_other = scatter(
        blocks(mm(gated, w_out).astype(bf16)), blocks(mm(gated, wo_o).astype(bf16)), weights_step
    )
    h_own, h_other = x_own + h_own, x_other + h_other

    squares = jnp.sum(h_own * h_own, axis=1) + jnp.sum(h_other * h_other, axis=1)
    squares = squares + swap_core(squares)
    ffn_scale = lax.rsqrt(squares / D + norm_eps)[:, None]
    n_own = (h_own * ffn_scale * ffn_gain).astype(bf16)
    n_other = (h_other * ffn_scale * gains_other[1]).astype(bf16)

    wd_o = jnp.concatenate(weights[:2], 0)
    gu_recv = swap_core(
        (mm_nt(rows(c_own, 1 - core), w_down) + mm_nt(rows(c_other, 1 - core), wd_o)).astype(bf16)
    )
    gu = mm_nt(rows(c_own, core), w_down) + mm_nt(rows(c_other, core), wd_o) + gu_recv.astype(f32)
    f_own, f_other = gather(n_own, n_other, weights_step)
    wf_o = jnp.concatenate(weights[2:], 0)
    f_own, gu = lax.optimization_barrier((f_own, gu))
    fk_own, fs_own = rows(f_own, core), rows(f_own, 1 - core)
    fk_other, fs_other = rows(f_other, core), rows(f_other, 1 - core)
    b_recv = swap_core((mm(fs_own, wf) + mm(fs_other, wf_o)).astype(bf16))
    both = mm(fk_own, wf) + mm(fk_other, wf_o) + b_recv.astype(f32)
    gate, up_part = both[:, :units_col], both[:, units_col:]
    sigma = jax.nn.sigmoid(gate)
    act = gate * sigma
    units = (act * up_part).astype(bf16)
    gb = jnp.concatenate(
        [(gu * up_part * silu_slope(gate, sigma)).astype(bf16), (gu * act).astype(bf16)], 1
    )
    gb_p = swap_core(gb)
    units_p = swap_core(tie(units, gb))
    df_kept = [mm_nt(gb, wf).astype(bf16), mm_nt(gb, wf_o).astype(bf16)]
    df_sent = [mm_nt(gb_p, wf).astype(bf16), mm_nt(gb_p, wf_o).astype(bf16)]
    ck_own, cs_own = rows(c_own, core), rows(c_own, 1 - core)
    ck_other, cs_other = rows(c_other, core), rows(c_other, 1 - core)
    wide = width // 2
    down_sent = [
        (mm_tn(units, ck_other[:, at : at + wide]) + mm_tn(units_p, cs_other[:, at : at + wide]))
        .astype(bf16)
        for at in (0, wide)
    ]

    def by_core(kept, sent):
        each = count // 2
        parts = []
        for k in range(count):
            s = slice(k % each * half, (k % each + 1) * half)
            parts.append(jnp.where(core == k // each, kept[s], sent[s]))
        return parts

    y_queue, x_queue, landed, found = [], [], {}, {}

    def background(work=None, given=(), takes=None, y_pieces=1, x_pieces=1):
        sends, keys, moving = [], [], []
        for _ in range(min(y_pieces, len(y_queue))):
            key, array = y_queue.pop(0)
            keys.append(key)
            sends.append((swap_chip, array))
        n = len(sends)
        for _ in range(min(x_pieces, len(x_queue))):
            moving.append(x_queue.pop(0))
        if pairs:
            sends += [(swap_group, array) for _, array in moving]

        def take(moved, made):
            if takes is not None:
                takes(made)
            landed.update(zip(keys, moved[:n]))
            for at, (key, array) in enumerate(moving):
                if pairs:
                    found[key] = (array, moved[n + at])
                else:
                    found[key] = (array,)

        return sends, work, given, take

    def total(key, *after):
        parts = found[key]
        if after:
            parts = lax.optimization_barrier((*parts, *after))[: len(parts)]
        if pairs:
            return parts[0].astype(f32) + parts[1].astype(f32)
        return lax.psum(parts[0], "dp").astype(f32)

    def queue(name, parts):
        y_queue.extend((f"{name}{n}", part) for n, part in enumerate(parts))

    feed_own = []

    def down_gradient(n):
        def work(u, v, c, d, got):
            return [weight_gradients([u, v], [c, d], [got], columns=(n, wide))]

        return work, (units, units_p, ck_own, cs_own, landed[f"d{n}"])

    def ready_for_group(*keys):
        return lambda made: x_queue.extend(zip(keys, made))

    queue("d", down_sent)

    def ffn_step(k):
        if k == 1:

            def work(f, h, g, p):
                return weight_gradient_pieces([f, h], [g, p], bf16, 4)

            return background(
                work, (fk_other, fs_other, gb, gb_p), lambda made: queue("f", made)
            )
        own, given = down_gradient(k - 2)
        if k == 3:
            return background(own, given, ready_for_group("d1"))

        def work(f, h, g, p, *given):
            return [*own(*given), *weight_gradient_pieces([f, h], [g, p], f32, 4)]

        def takes(made):
            x_queue.append(("d0", made[0]))
            feed_own.extend(made[1:])

        return background(work, (fk_own, fs_own, gb, gb_p, *given), takes)

    kept = []
    df_own, df_other = scatter(
        by_core(df_kept[0], df_sent[0]), by_core(df_kept[1], df_sent[1]), ffn_step
    )

    gain_fo = gains_other[1]
    w_o, w_p = df_own * ffn_gain, df_other * gain_fo
    along = jnp.sum(w_o * h_own, axis=1) + jnp.sum(w_p * h_other, axis=1)
    along = along + swap_core(along)
    factor = ffn_scale**3 * along[:, None] / D
    gh_own = cot_own.astype(f32) + ffn_scale * w_o - h_own * factor
    gh_other = cot_other.astype(f32) + ffn_scale * w_p - h_other * factor
    ffn_part = jnp.sum(df_own * h_own * ffn_scale, axis=0)
    ffn_part_o = jnp.sum(df_other * h_other * ffn_scale, axis=0)

    def back_step(k):
        given = (feed_own[k - 1], landed[f"f{k - 1}"])
        if k == 3:
            return background(lambda a, b: [rounded_sum(a, b)], given, ready_for_group("f2"))

        def work(u, v, w, a, b):
            return [*products([u, v], w), rounded_sum(a, b)]

        def takes(made):
            kept.extend(made[:2])
            x_queue.append((f"f{k - 1}", made[2]))

        return background(work, (units, units_p, w_down if k == 1 else wd_o, *given), takes)

    g_own, g_other = gather(gh_own.astype(bf16), gh_other.astype(bf16), back_step)
    un_own, un_other = by_core(*kept[:2]), by_core(*kept[2:])

    gg_recv = swap_core(
        (mm_nt(g_own, mine(w_out, 1 - core, hc, 0)) + mm_nt(g_other, mine(wo_o, 1 - core, hc, 0)))
        .astype(bf16)
    )
    gg_keep = mm_nt(g_own, mine(w_out, core, hc, 0)) + mm_nt(g_other, mine(wo_o, core, hc, 0))
    do, d_gate, group_part, seg, low = recurrence_back_local(
        gg_keep, gg_recv, rec, keep, recv, gain_row, local[1], local[4]
    )
    core_here = core.astype(jnp.int32).reshape(1)

    def gate_gradients(gate, left, grad, right):
        gate_p = swap_core(gate)
        sent = weight_gradients([left], [grad])
        return [gate_p, sent, head_gradients(core_here, right, gate, gate_p, 0, hc, bf16)]

    (peer,), (d_gate_p, out_sent, gate_sent), _ = step(
        [(swap_chip, low)], gate_gradients, (d_gate, gated, g_other, m_other)
    )

    def finish_back(seg, peer, own, got):
        enter = recurrence_enter(place, seg, decay, peer, peer_decay, True)
        return [
            *recurrence_back_finish(keep, recv, bound, ids, local, states, do, enter),
            rounded_sum(own, got),
        ]

    queue("o", [out_sent])
    queue("g", [gate_sent])
    out_run = paired(un_own[1], un_other[1])
    sends, _, _, take = background(y_pieces=2)
    moved, (d_three, bound_part, feed_last), _ = step(
        [(up, out_run), *sends], finish_back, (seg, peer, feed_own[3], landed["f3"])
    )
    x_queue.append(("f3", feed_last))
    d_gate, d_gate_p = lax.optimization_barrier((d_gate, d_gate_p, d_three))[:2]

    def out_sum(moved, at):
        a = moved[:, :width].astype(f32) + un_own[at].astype(f32)
        return a, moved[:, width:].astype(f32) + un_other[at].astype(f32)

    out_run = paired(*out_sum(moved[0], 2)).astype(bf16)
    take(moved[1:], [])

    d_three_p = swap_core(d_three)

    dp_keep = jnp.concatenate([d_three, d_gate], 1)
    sums_own, sums_other = mm_nt(dp_keep, wm_keep), mm_nt(dp_keep, wm_keep_o)
    dp_send = jnp.concatenate([d_three_p, d_gate_p], 1)
    sums_own, sums_other = sums_own + mm_nt(dp_send, wm_send), sums_other + mm_nt(dp_send, wm_send_o)
    own, other = blocks(sums_own.astype(bf16)), blocks(sums_other.astype(bf16))
    mix_part = jnp.sum(sums_own * m_own.astype(f32), axis=0) / mix_gain
    mix_part_o = jnp.sum(sums_other * m_other.astype(f32), axis=0) / gains_other[0]
    tail = jnp.concatenate([bound_part[0], group_part[0]])
    small = jnp.concatenate([mix_part, ffn_part, tail])
    small_o = jnp.concatenate([mix_part_o, ffn_part_o, tail])

    def heads_of(left, three, three_p, part, kind):
        return head_gradients(core_here, left, three, three_p, part, hc, kind)

    def first_gradients(three, three_p, right, heads, grad, left, gate, gate_p, o_got, g_got):
        sent = [heads_of(right, three, three_p, p, bf16) for p in range(3)]
        out = weight_gradients([heads], [grad], [o_got])
        gates = head_gradients(core_here, left, gate, gate_p, 0, hc, bf16, [g_got])
        return [*sent, out, gates]

    sends, _, _, take = background()
    dx_run = paired(own[1], other[1])
    moved, made, _ = step(
        [(up, dx_run), (up, out_run), (swap_chip, small_o), *sends],
        first_gradients,
        (d_three, d_three_p, m_other, gated, g_own, m_own, d_gate, d_gate_p)
        + (landed["o0"], landed["g0"]),
    )
    small = small + moved[2]
    take(moved[3:], [])
    x_queue.extend(zip(("o0", "g0"), made[3:]))
    for name, value in zip("qkv", made):
        queue(name, [value])

    def dx_sum(moved, at):
        a = moved[:, :width].astype(f32) + own[at].astype(f32)
        return a, moved[:, width:].astype(f32) + other[at].astype(f32)

    dx_run = paired(*dx_sum(moved[0], 2)).astype(bf16)
    out_run = paired(*out_sum(moved[1], 3)).astype(bf16)
    sends, work, given, take = background(
        lambda three, three_p, left: [heads_of(left, three, three_p, p, f32) for p in range(3)],
        (d_three, d_three_p, m_own),
        y_pieces=2,
        x_pieces=2,
    )
    if pairs:
        sends.append((swap_group, small))
    moved, made, _ = step([(up, dx_run), (up, out_run), *sends], work, given)
    small = small + moved[-1] if pairs else lax.psum(small, "dp")
    take(moved[2:-1] if pairs else moved[2:], made)
    of_parts = dict(zip(("q0", "k0", "v0"), made))

    def reduced(key):
        x_queue.append((key, (of_parts[key] + landed[key].astype(f32)).astype(bf16)))

    reduced("q0")
    reduced("k0")
    dx_run = paired(*dx_sum(moved[0], 3)).astype(bf16)
    out_own, out_other = out_sum(moved[1], 0)
    out_own, out_other = (h_own + out_own).astype(bf16), (h_other + out_other).astype(bf16)
    edge = 2 * width
    bound_sum = small[edge : edge + hc]
    wide = jnp.concatenate([small[:edge], small[edge + hc :]])
    near = lambda a: lax.ppermute(a, "col", [(i, i ^ 1) for i in range(count)])
    far = lambda a: lax.ppermute(a, "col", [(i, i ^ 2) for i in range(count)])
    ffn_pieces = [found[f"f{n}"] if pairs else (total(f"f{n}"),) for n in range(4)]
    each = len(ffn_pieces[0])

    def whole_ffn(*given):
        return [
            halves_of_rows([given[n * each : (n + 1) * each] for n in range(4)], 2)
        ]

    sends, _, _, take = background(x_pieces=2)
    moved, (ffn_whole,), _ = step(
        [(up, dx_run), (near, wide), (swap_chip, out_other), *sends],
        whole_ffn,
        [array for found_piece in ffn_pieces for array in found_piece],
    )
    wide = wide + moved[1]
    out_other = moved[2]
    take(moved[3:], [])
    reduced("v0")
    dx_own, dx_other = dx_sum(moved[0], 0)

    w_o, w_p = dx_own * mix_gain, dx_other * gains_other[0]
    along = jnp.sum(w_o * x_own, axis=1) + jnp.sum(w_p * x_other, axis=1)
    along = along + swap_core(along)
    factor = mix_scale**3 * along[:, None] / D
    gt_own = gh_own + mix_scale * w_o - x_own * factor
    gt_other = gh_other + mix_scale * w_p - x_other * factor
    sends, _, _, take = background(x_pieces=2)
    moved, _, _ = step([(swap_chip, gt_other.astype(bf16)), (far, wide), *sends])
    grad_other = moved[0].astype(f32)
    wide = wide + moved[1]
    take(moved[2:], [])
    while y_queue or x_queue:
        sends, _, _, take = background(x_pieces=2)
        moved, _, _ = step(sends) if sends else ([], [], [])
        take(moved, [])
    turned = swap_core(jnp.concatenate([bound_sum, wide[edge:]]))
    grad_bound = joined(bound_sum, turned[:hc], core, 0)

    return (
        joined(out_own, out_other, y, 0),
        joined(gt_own, grad_other, y, 0),
        wide[:width],
        stacked([found[key] if pairs else (total(key),) for key in ("q0", "k0", "v0", "g0")]),
        grad_bound,
        wide[edge:] + turned[hc:],
        total("o0"),
        wide[width:edge],
        ffn_whole,
        jnp.concatenate([total("d0"), total("d1")], 1),
    )


def solution(mesh):
    return jax.shard_map(
        shards,
        mesh=mesh,
        in_specs=(
            P(("dp", "col"), "row"),
            P("dp"),
            P("row"),
            P("row", None, "col"),
            P("col"),
            P(),
            P("col", "row"),
            P("row"),
            P("row", None, "col"),
            P("col", "row"),
            P(("dp", "col"), "row"),
        ),
        out_specs=(
            P(("dp", "col"), "row"),
            P(("dp", "col"), "row"),
            P("row"),
            P("row", None, "col"),
            P("col"),
            P(),
            P("col", "row"),
            P("row"),
            P("row", None, "col"),
            P("col", "row"),
        ),
        check_vma=False,
    )
```

```python
from functools import partial

import jax
import jax.numpy as jnp
from jax import lax
from jax.experimental import pallas as pl
from jax.experimental.pallas import tpu as pltpu
from jax.sharding import PartitionSpec as P

D = 2048
HD = 128
BLOCK = 64
norm_eps = 1e-06
bf16 = jnp.bfloat16
f32 = jnp.float32

CORE = [(0, 1), (1, 0), (2, 3), (3, 2)]
CHIP = [(0, 2), (2, 0), (1, 3), (3, 1)]


def swap_core(x):
    return lax.ppermute(x, "row", CORE)


def swap_chip(x):
    return lax.ppermute(x, "row", CHIP)


def tie(x, *others):
    return lax.optimization_barrier((x, *others))[0]


def mm(left, right):
    return lax.dot_general(left, right, (((1,), (0,)), ((), ())), preferred_element_type=f32)


def mm_nt(left, right):
    return lax.dot_general(left, right, (((1,), (1,)), ((), ())), preferred_element_type=f32)


def mm_tn(left, right):
    return lax.dot_general(left, right, (((0,), (0,)), ((), ())), preferred_element_type=f32)


def silu_slope(value, sigma):
    return sigma * (1.0 + value * (1.0 - sigma))


def split_mm(left, value):
    high = value.astype(bf16)
    low = (value - high.astype(f32)).astype(bf16)
    return mm(left, high) + mm(left, low)


def run_masks(i, idc_ref, idr_ref, prev_ref):
    s = slice(i * BLOCK, (i + 1) * BLOCK)
    idc = idc_ref[s, :]
    idr = idr_ref[0, :, s]
    prev = prev_ref[s, :]
    before = prev[0:1, :]
    last = idc[BLOCK - 1 : BLOCK, :]
    t = lax.broadcasted_iota(jnp.int32, (BLOCK, BLOCK), 0)
    u = lax.broadcasted_iota(jnp.int32, (BLOCK, BLOCK), 1)
    same = idc == idr
    heads = (idc == before).astype(f32)
    tails = (idc == last).astype(f32)
    through = (last == before).astype(f32)
    old = (idc == prev).astype(f32)
    return t, u, same, heads, tails, through, old


def run_decays(f_raw, lb, t, u):
    closed = jax.nn.sigmoid(-f_raw)
    keys = (1.0 - lb) * closed
    total = split_mm((t >= u).astype(bf16), jnp.log1p(-keys))
    middle = total[BLOCK // 2 - 1 : BLOCK // 2, :]
    final = total[BLOCK - 1 : BLOCK, :]
    return closed, keys, total, middle, final


def col(h, part=0, heads=1):
    start = (part * heads + h) * HD
    return slice(start, start + HD)


def local_kernel(
    keep_ref, recv_ref, lb_ref, idc_ref, idr_ref, prev_ref,
    inner_ref, qh_ref, kh_ref, vb_ref, decay_ref, seg_ref, low_ref, segd_ref,
):
    heads = lb_ref.shape[1] // HD
    state = [jnp.zeros((HD, HD), f32)] * heads
    passing = [jnp.ones((1, HD), f32)] * heads
    for i in range(keep_ref.shape[0] // BLOCK):
        s = slice(i * BLOCK, (i + 1) * BLOCK)
        t, u, same, head, tails, through, _ = run_masks(i, idc_ref, idr_ref, prev_ref)
        for h in range(heads):
            c = col(h)

            def raw(part):
                p = col(h, part, heads)
                return keep_ref[s, p] + recv_ref[s, p].astype(f32)

            q_raw = raw(0)
            vb = raw(2).astype(bf16)
            q = q_raw * jax.nn.sigmoid(q_raw)
            _, keys, total, middle, final = run_decays(raw(1), lb_ref[:, c], t, u)
            qt = (q * jnp.exp(total - middle)).astype(bf16)
            kt = (keys * jnp.exp(middle - total)).astype(bf16)
            scores = jnp.where(same & (t >= u), mm_nt(qt, kt), 0.0).astype(bf16)
            inner_ref[s, c] = mm(scores, vb)
            qh_ref[s, c] = (q * jnp.exp(total) * head).astype(bf16)
            kh = (keys * jnp.exp(final - total) * tails).astype(bf16)
            kh_ref[s, c] = kh
            vb_ref[s, c] = vb
            keep = jnp.exp(final) * through
            decay_ref[0, i : i + 1, c] = keep
            state[h] = keep * state[h] + mm_tn(vb, kh)
            passing[h] = passing[h] * keep
    for h in range(heads):
        seg_ref[0, h] = state[h]
        low_ref[0, h] = state[h].astype(bf16)
        segd_ref[0, :, col(h)] = passing[h]


def enter_kernel(reverse, place_ref, seg_ref, segd_ref, peer_ref, peerd_ref, out_ref):
    z, y = place_ref[0], place_ref[1]
    count, heads = seg_ref.shape[:2]
    peer_first = (y == 0) if reverse else (y == 1)
    state = [jnp.zeros((HD, HD), f32)] * heads
    for place in reversed(range(count)) if reverse else range(count):
        k = lax.rem((z ^ (z >> 1)) - (place ^ (place >> 1)) + count, count)
        for h in range(heads):
            add = peer_ref[k, h].astype(f32)
            scale = peerd_ref[k, :, col(h)]
            s = jnp.where(peer_first, scale, 1.0) * state[h] + jnp.where(peer_first, add, 0.0)
            out_ref[k, h] = s
            s = segd_ref[k, :, col(h)] * s + seg_ref[k, h]
            state[h] = jnp.where(peer_first, 1.0, scale) * s + jnp.where(peer_first, 0.0, add)


def finish_kernel(
    inner_ref, qh_ref, kh_ref, vb_ref, decay_ref, enter_ref, keep_ref, recv_ref, gain_ref,
    gated_ref, rec_ref, st_ref,
):
    heads = enter_ref.shape[1]
    state = [enter_ref[0, h] for h in range(heads)]
    for i in range(qh_ref.shape[0] // BLOCK):
        s = slice(i * BLOCK, (i + 1) * BLOCK)
        for h in range(heads):
            c = col(h)
            low = state[h].astype(bf16)
            st_ref[0, i, h] = low
            rec = inner_ref[s, c] + mm_nt(qh_ref[s, c], low)
            rec_ref[s, c] = rec
            scale = lax.rsqrt(jnp.mean(rec * rec, axis=1, keepdims=True) + norm_eps)
            g_raw = keep_ref[s, c] + recv_ref[s, c].astype(f32)
            gate = g_raw * jax.nn.sigmoid(g_raw)
            gated_ref[s, c] = (rec * scale * gain_ref[...] * gate).astype(bf16)
            state[h] = decay_ref[0, i : i + 1, c] * state[h] + mm_tn(vb_ref[s, c], kh_ref[s, c])


def back_local_kernel(
    kd, rd, rec_ref, keep_ref, recv_ref, gain_ref, qh_ref, decay_ref,
    do_ref, dg_ref, group_ref, seg_ref, low_ref,
):
    @pl.when(pl.program_id(0) == 0)
    def _():
        group_ref[...] = jnp.zeros_like(group_ref)

    gain = gain_ref[...]
    heads = seg_ref.shape[1]
    adjoint = [jnp.zeros((HD, HD), f32)] * heads
    group = jnp.zeros((1, HD), f32)
    for i in reversed(range(qh_ref.shape[0] // BLOCK)):
        s = slice(i * BLOCK, (i + 1) * BLOCK)
        for h in range(heads):
            c = col(h)
            grad = kd[s, c] + rd[s, c].astype(f32)
            rec = rec_ref[s, c]
            scale = lax.rsqrt(jnp.mean(rec * rec, axis=1, keepdims=True) + norm_eps)
            normed = rec * scale
            g_raw = keep_ref[s, c] + recv_ref[s, c].astype(f32)
            sigma = jax.nn.sigmoid(g_raw)
            act = g_raw * sigma
            both = grad * normed
            group = group + jnp.sum(both * act, axis=0, keepdims=True)
            dg_ref[s, c] = (both * gain * silu_slope(g_raw, sigma)).astype(bf16)
            dn = grad * gain * act
            do = (scale * (dn - normed * jnp.mean(dn * normed, axis=1, keepdims=True))).astype(bf16)
            do_ref[s, c] = do
            adjoint[h] = decay_ref[0, i : i + 1, c] * adjoint[h] + mm_tn(do, qh_ref[s, c])
    group_ref[...] += group
    for h in range(heads):
        seg_ref[0, h] = adjoint[h]
        low_ref[0, h] = adjoint[h].astype(bf16)


def back_finish_kernel(
    keep_ref, recv_ref, lb_ref, idc_ref, idr_ref, prev_ref,
    qh_ref, kh_ref, vb_ref, decay_ref, st_ref, do_ref, enter_ref, gate_ref,
    grad_ref, bound_ref,
):
    @pl.when(pl.program_id(0) == 0)
    def _():
        bound_ref[...] = jnp.zeros_like(bound_ref)

    heads = enter_ref.shape[1]
    grad_ref[:, 3 * gate_ref.shape[1] :] = gate_ref[...]
    adjoint = [enter_ref[0, h] for h in range(heads)]
    bound = [jnp.zeros((1, HD), f32)] * heads
    for i in reversed(range(keep_ref.shape[0] // BLOCK)):
        s = slice(i * BLOCK, (i + 1) * BLOCK)
        t, u, same, head, tails, through, old = run_masks(i, idc_ref, idr_ref, prev_ref)
        causal = same & (t >= u)
        later = (same & (u >= t)).astype(bf16)
        for h in range(heads):
            c = col(h)

            def raw(part):
                p = col(h, part, heads)
                return keep_ref[s, p] + recv_ref[s, p].astype(f32)

            q_raw = raw(0)
            sigma = jax.nn.sigmoid(q_raw)
            q = q_raw * sigma
            closed, keys, total, middle, final = run_decays(raw(1), lb_ref[:, c], t, u)
            out = jnp.exp(total - middle)
            back = jnp.exp(middle - total)
            qt = (q * out).astype(bf16)
            kt = (keys * back).astype(bf16)
            scores = jnp.where(causal, mm_nt(qt, kt), 0.0).astype(bf16)
            vb = vb_ref[s, c]
            kh = kh_ref[s, c]
            do = do_ref[s, c]
            st = st_ref[0, i, h]
            low = adjoint[h].astype(bf16)
            keep = decay_ref[0, i : i + 1, c]
            ds = jnp.where(causal, mm_nt(do, vb), 0.0).astype(bf16)
            dq = mm(ds, kt) * out + mm(do, st) * (jnp.exp(total) * head)
            dkh = mm(vb, low)
            dk = mm_tn(ds, qt) * back + dkh * (jnp.exp(final - total) * tails)
            grad_ref[s, col(h, 2, heads)] = (mm_tn(scores, do) + mm_nt(kh, low)).astype(bf16)
            ends = keep * jnp.sum(adjoint[h] * st.astype(f32), axis=0, keepdims=True) + jnp.sum(
                kh.astype(f32) * dkh, axis=0, keepdims=True
            )
            dlog = split_mm(later, q * dq - keys * dk) + tails * ends
            key_total = dk - old * dlog / (1.0 - keys)
            bound[h] = bound[h] - jnp.sum(key_total * closed, axis=0, keepdims=True)
            grad_ref[s, col(h, 1, heads)] = (-key_total * keys * (1.0 - closed)).astype(bf16)
            grad_ref[s, col(h, 0, heads)] = (dq * silu_slope(q_raw, sigma)).astype(bf16)
            adjoint[h] = keep * adjoint[h] + mm_tn(do, qh_ref[s, c])
    for h in range(heads):
        bound_ref[:, col(h)] += bound[h]


def shape(dims, kind):
    return jax.ShapeDtypeStruct(dims, kind)


COST = pl.CostEstimate(flops=0, bytes_accessed=0, transcendentals=0)
SMEM = pl.BlockSpec(memory_space=pltpu.SMEM)
VMEM = pl.BlockSpec(memory_space=pltpu.VMEM)


def run_block(*dims, at=0):
    return pl.BlockSpec(dims, lambda j: (j, *([0] * (len(dims) - 2)), at))


def whole(*dims):
    return pl.BlockSpec(dims, lambda j: (0,) * len(dims))


def recurrence_local(keep, recv, bound, ids):
    runs, _, run = ids[1].shape
    width = bound.shape[1]
    heads = width // HD
    chunks = run // BLOCK
    tokens = runs * run
    return pl.pallas_call(
        local_kernel,
        grid=(runs,),
        in_specs=[
            run_block(run, 4 * width), run_block(run, 4 * width), whole(1, width),
            run_block(run, 1), run_block(1, 1, run), run_block(run, 1),
        ],
        out_specs=[run_block(run, width)] * 4
        + [run_block(1, chunks, width)]
        + [run_block(1, heads, HD, HD)] * 2
        + [run_block(1, 1, width)],
        out_shape=[
            shape((tokens, width), f32),
            shape((tokens, width), bf16),
            shape((tokens, width), bf16),
            shape((tokens, width), bf16),
            shape((runs, chunks, width), f32),
            shape((runs, heads, HD, HD), f32),
            shape((runs, heads, HD, HD), bf16),
            shape((runs, 1, width), f32),
        ],
        cost_estimate=COST,
        name="recurrence_local",
    )(keep, recv, bound, *ids)


def recurrence_enter(place, seg, segd, peer, peerd, reverse):
    return pl.pallas_call(
        partial(enter_kernel, reverse),
        in_specs=[SMEM] + [VMEM] * 4,
        out_specs=VMEM,
        out_shape=shape(seg.shape, f32),
        cost_estimate=COST,
        name="recurrence_enter_back" if reverse else "recurrence_enter",
    )(place, seg, segd, peer, peerd)


def recurrence_finish(local, enter, keep, recv, gain):
    inner, qh, kh, vb, decay = local
    runs, chunks, width = decay.shape
    heads = width // HD
    run = chunks * BLOCK
    tokens = runs * run
    cols = run_block(run, width)
    gate = run_block(run, width, at=3)
    return pl.pallas_call(
        finish_kernel,
        grid=(runs,),
        in_specs=[
            cols, cols, cols, cols, run_block(1, chunks, width), run_block(1, heads, HD, HD),
            gate, gate, whole(1, HD),
        ],
        out_specs=[cols, cols, run_block(1, chunks, heads, HD, HD)],
        out_shape=[
            shape((tokens, width), bf16),
            shape((tokens, width), f32),
            shape((runs, chunks, heads, HD, HD), bf16),
        ],
        cost_estimate=COST,
        name="recurrence_finish",
    )(inner, qh, kh, vb, decay, enter, keep, recv, gain)


def recurrence_back_local(kd, rd, rec, keep, recv, gain, qh, decay):
    runs, chunks, width = decay.shape
    heads = width // HD
    run = chunks * BLOCK
    tokens = runs * run
    cols = run_block(run, width)
    gate = run_block(run, width, at=3)
    return pl.pallas_call(
        back_local_kernel,
        grid=(runs,),
        in_specs=[
            cols, cols, cols, gate, gate, whole(1, HD), cols, run_block(1, chunks, width),
        ],
        out_specs=[cols, cols, whole(1, HD)] + [run_block(1, heads, HD, HD)] * 2,
        out_shape=[
            shape((tokens, width), bf16),
            shape((tokens, width), bf16),
            shape((1, HD), f32),
            shape((runs, heads, HD, HD), f32),
            shape((runs, heads, HD, HD), bf16),
        ],
        cost_estimate=COST,
        name="recurrence_back_local",
    )(kd, rd, rec, keep, recv, gain, qh, decay)


def recurrence_back_finish(keep, recv, bound, ids, local, states, do, enter, gate):
    _, qh, kh, vb, decay = local
    runs, chunks, width = decay.shape
    heads = width // HD
    run = chunks * BLOCK
    tokens = runs * run
    cols = run_block(run, width)
    return pl.pallas_call(
        back_finish_kernel,
        grid=(runs,),
        in_specs=[
            run_block(run, 4 * width), run_block(run, 4 * width), whole(1, width),
            run_block(run, 1), run_block(1, 1, run), run_block(run, 1),
            cols, cols, cols, run_block(1, chunks, width),
            run_block(1, chunks, heads, HD, HD), cols, run_block(1, heads, HD, HD), cols,
        ],
        out_specs=[run_block(run, 4 * width), whole(1, width)],
        out_shape=[shape((tokens, 4 * width), bf16), shape((1, width), f32)],
        cost_estimate=COST,
        name="recurrence_back_finish",
    )(keep, recv, bound, *ids, qh, kh, vb, decay, states, do, enter, gate)


def weight_kernel(pairs, *refs):
    lefts, rights = refs[:pairs], refs[pairs : 2 * pairs]
    *plus, out = refs[2 * pairs :]
    total = sum(mm_tn(left[...], right[...]) for left, right in zip(lefts, rights))
    out[...] = (total + sum(part[...].astype(f32) for part in plus)).astype(out.dtype)


def weight_gradients(lefts, rights, plus=(), rows=None, columns=None, tile=256):
    at, tall = rows or (0, lefts[0].shape[1])
    first, wide = columns or (0, rights[0].shape[1])
    tiles = wide // tile
    out = pl.BlockSpec((tall, tile), lambda j: (0, j))
    return pl.pallas_call(
        partial(weight_kernel, len(lefts)),
        grid=(tiles,),
        in_specs=[pl.BlockSpec((left.shape[0], tall), lambda j: (0, at)) for left in lefts]
        + [pl.BlockSpec((r.shape[0], tile), lambda j: (0, first * tiles + j)) for r in rights]
        + [out] * len(plus),
        out_specs=out,
        out_shape=shape((tall, wide), bf16),
        cost_estimate=COST,
        name="weight_gradients",
    )(*lefts, *rights, *plus)


def pieces_kernel(pairs, *refs):
    lefts, rights, outs = refs[:pairs], refs[pairs : 2 * pairs], refs[2 * pairs :]
    total = sum(mm_tn(left[...], right[...]) for left, right in zip(lefts, rights))
    each = outs[0].shape[0]
    for n, out in enumerate(outs):
        out[...] = total[n * each : (n + 1) * each].astype(out.dtype)


def weight_gradient_pieces(lefts, rights, kind, pieces, tile=256):
    tall, wide = lefts[0].shape[1] // pieces, rights[0].shape[1]
    return pl.pallas_call(
        partial(pieces_kernel, len(lefts)),
        grid=(wide // tile,),
        in_specs=[whole(*left.shape) for left in lefts]
        + [pl.BlockSpec((right.shape[0], tile), lambda j: (0, j)) for right in rights],
        out_specs=[pl.BlockSpec((tall, tile), lambda j: (0, j))] * pieces,
        out_shape=[shape((tall, wide), kind)] * pieces,
        cost_estimate=COST,
        name="weight_gradient_pieces",
    )(*lefts, *rights)


def sum_kernel(own_ref, got_ref, out_ref):
    out_ref[...] = (own_ref[...] + got_ref[...].astype(f32)).astype(bf16)


def rounded_sum(own, got):
    return pl.pallas_call(
        sum_kernel,
        in_specs=[VMEM] * 2,
        out_specs=VMEM,
        out_shape=shape(own.shape, bf16),
        cost_estimate=COST,
        name="rounded_sum",
    )(own, got)


def halves_kernel(pieces, *refs):
    *given, out_ref = refs
    each = len(given) // pieces
    wide = out_ref.shape[2]
    rows = out_ref.shape[0]
    for n in range(pieces):

        @pl.when(pl.program_id(0) == n)
        def _():
            at = pl.ds(pl.multiple_of(pl.program_id(1) * rows, rows), rows)
            for part in range(out_ref.shape[1]):
                cols = slice(part * wide, (part + 1) * wide)
                value = sum(ref[at, cols].astype(f32) for ref in given[n * each : (n + 1) * each])
                out_ref[:, part, :] = value


def halves_of_rows(pieces, parts, rows=32):
    tall, wide = pieces[0][0].shape
    steps = tall // rows
    given = [array for piece in pieces for array in piece]
    return pl.pallas_call(
        partial(halves_kernel, len(pieces)),
        grid=(len(pieces), steps),
        in_specs=[pl.BlockSpec(a.shape, lambda n, j: (0, 0)) for a in given],
        out_specs=pl.BlockSpec((rows, parts, wide // parts), lambda n, j: (n * steps + j, 0, 0)),
        out_shape=shape((len(pieces) * tall, parts, wide // parts), f32),
        cost_estimate=COST,
        compiler_params=pltpu.CompilerParams(vmem_limit_bytes=40 * 2**20),
        name="halves_of_rows",
    )(*given)


def stack_kernel(counts, *refs):
    *given, out_ref = refs
    for part, count in enumerate(counts):
        refs_here, given = given[:count], given[count:]
        if count:
            out_ref[:, part, :] = sum(ref[...].astype(f32) for ref in refs_here)
        else:
            out_ref[:, part, :] = jnp.zeros((out_ref.shape[0], out_ref.shape[2]), f32)


def stacked(parts, rows=64):
    tall, wide = parts[0][0].shape
    given = [array for part in parts for array in part]
    return pl.pallas_call(
        partial(stack_kernel, [len(part) for part in parts]),
        grid=(tall // rows,),
        in_specs=[pl.BlockSpec((rows, wide), lambda j: (j, 0))] * len(given),
        out_specs=pl.BlockSpec((rows, len(parts), wide), lambda j: (j, 0, 0)),
        out_shape=shape((tall, len(parts), wide), f32),
        cost_estimate=COST,
        name="stacked",
    )(*given)


def product_kernel(right_ref, *refs):
    lefts, outs = refs[: len(refs) // 2], refs[len(refs) // 2 :]
    for left, out in zip(lefts, outs):
        out[...] = mm(left[...], right_ref[...]).astype(out.dtype)


def products(lefts, right, tile=256):
    wide = right.shape[1]
    return pl.pallas_call(
        product_kernel,
        grid=(wide // tile,),
        in_specs=[pl.BlockSpec((right.shape[0], tile), lambda j: (0, j))]
        + [whole(*left.shape) for left in lefts],
        out_specs=[pl.BlockSpec((left.shape[0], tile), lambda j: (0, j)) for left in lefts],
        out_shape=[shape((left.shape[0], wide), bf16) for left in lefts],
        cost_estimate=COST,
        name="products",
    )(right, *lefts)


def heads_kernel(first, half, core_ref, left_ref, own_ref, peer_ref, *refs):
    *plus, out_ref = refs
    core = core_ref[0]
    tall = left_ref.shape[1]
    for part in range(out_ref.shape[0] // tall):
        rows = slice(part * tall, (part + 1) * tall)
        given = slice((first + part) * half, (first + part + 1) * half)
        for right_ref, at in ((own_ref, core), (peer_ref, 1 - core)):
            cols = pl.ds(pl.multiple_of(at * half, half), half)
            total = mm_tn(left_ref[...], right_ref[:, given])
            for more in plus:
                total = total + more[rows, cols].astype(f32)
            out_ref[rows, cols] = total.astype(out_ref.dtype)


def head_gradients(core, left, own, peer, first, half, kind, plus=(), parts=1):
    return pl.pallas_call(
        partial(heads_kernel, first, half),
        in_specs=[SMEM] + [VMEM] * (3 + len(plus)),
        out_specs=VMEM,
        out_shape=shape((parts * left.shape[1], 2 * half), kind),
        cost_estimate=COST,
        name="head_gradients",
    )(core, left, own, peer, *plus)


def fill_kernel(part, *refs):
    base_ref, *given, out_ref = refs
    out_ref[...] = base_ref[...]
    out_ref[:, part, :] = sum(ref[...].astype(f32) for ref in given)


def filled(base, part, given, rows=64):
    tall, parts, wide = base.shape
    block = pl.BlockSpec((rows, parts, wide), lambda j: (j, 0, 0))
    return pl.pallas_call(
        partial(fill_kernel, part),
        grid=(tall // rows,),
        in_specs=[block] + [pl.BlockSpec((rows, wide), lambda j: (j, 0))] * len(given),
        out_specs=block,
        out_shape=shape(base.shape, f32),
        input_output_aliases={0: 0},
        cost_estimate=COST,
        name="filled",
    )(base, *given)


def swap_group(x):
    return lax.ppermute(x, "dp", [(0, 1), (1, 0)])


def folded(place):
    return place ^ (place >> 1)


def up(x):
    count = lax.axis_size("col")
    return lax.ppermute(x, "col", [(folded(n), folded((n + 1) % count)) for n in range(count)])


def paired(own, other):
    return jnp.concatenate([own, other], 1)


def step(sends, work=None, given=(), join=()):
    n = len(sends)
    arrays = lax.optimization_barrier((*(array for _, array in sends), *given))
    moved = [mover(array) for (mover, _), array in zip(sends, arrays)]
    made = tuple(work(*arrays[n:])) if work else ()
    done = lax.optimization_barrier((*moved, *made, *join))
    return list(done[:n]), list(done[n : n + len(made)]), list(done[n + len(made) :])


def ordered(runs):
    width = runs[0].shape[1] // 2
    return (
        jnp.concatenate([run[:, :width] for run in runs], 0),
        jnp.concatenate([run[:, width:] for run in runs], 0),
    )


def cut(array, count):
    each = -(-array.shape[0] // count)
    each = -(-each // 16) * 16
    return [array[at : at + each] for at in range(0, array.shape[0], each)]


def shards(
    tokens,
    segments,
    mix_gain,
    w_mix,
    lower_bound,
    group_gain,
    w_out,
    ffn_gain,
    w_ffn_in,
    w_down,
    cotangent,
):
    row = lax.axis_index("row")
    core = row % 2
    y = row // 2
    z = lax.axis_index("col")
    count = lax.axis_size("col")
    pairs = lax.axis_size("dp") == 2
    half = tokens.shape[0] // 2
    width = tokens.shape[1]
    hc = w_mix.shape[2] // 2
    units_col = w_down.shape[0]
    here = count * half
    hb = here // 2

    def mine(x, at, size, axis):
        return lax.dynamic_slice_in_dim(x, at * size, size, axis)

    def rows(x, at):
        return mine(x, at, hb, 0)

    def joined(first_if_zero, second_if_zero, flag, axis):
        return jnp.where(
            flag == 0,
            jnp.concatenate([first_if_zero, second_if_zero], axis),
            jnp.concatenate([second_if_zero, first_if_zero], axis),
        )

    def blocks(array):
        return [array[k * half : (k + 1) * half] for k in range(count)]

    tok_own = mine(tokens, y, half, 0)
    (tok_other,), _, _ = step([(swap_chip, mine(tokens, 1 - y, half, 0))])
    cot_own, cot_send = mine(cotangent, y, half, 0), mine(cotangent, 1 - y, half, 0)
    wm_parts = cut(w_mix, 4)
    first = swap_chip(tie(wm_parts[0], tok_other))
    gains_other = swap_chip(tie(jnp.stack([mix_gain, ffn_gain]), tok_other))
    x_own, x_other = tok_own.astype(f32), tok_other.astype(f32)
    squares = jnp.sum(x_own * x_own, axis=1) + jnp.sum(x_other * x_other, axis=1)
    squares = squares + swap_core(squares)
    mix_scale = lax.rsqrt(squares / D + norm_eps)[:, None]
    m = [
        paired(x_own * mix_scale * mix_gain, x_other * mix_scale * gains_other[0]).astype(bf16)
    ]
    wm = [first]
    for k in range(1, count):
        sends = [(up, m[-1]), (swap_chip, cot_send if k == 1 else wm_parts[k - 1])]
        (a, got), _, late = step(sends, join=wm if k == 1 else [])
        if k == 1:
            wm, cot_other = late, got
        else:
            wm.append(got)
        m.append(a)
    c = [paired(cot_own, cot_other)]
    (a, got, m[-1]), _, _ = step(
        [(up, c[0]), (swap_chip, wm_parts[3]), (lambda v: v, m[-1])]
    )
    c.append(a)
    wm_other = jnp.concatenate([*wm, got], 0)
    m_own, m_other = ordered(m)

    def columns(w, at):
        return mine(w, at, hc, 2).reshape(width, 4 * hc)

    wm_keep, wm_send = columns(w_mix, core), columns(w_mix, 1 - core)
    wm_keep_o, wm_send_o = columns(wm_other, core), columns(wm_other, 1 - core)

    names = segments.astype(f32)
    before = jnp.concatenate([jnp.full((1,), -1.0, f32), names[:-1]])

    def runs_of(array):
        array = lax.dynamic_index_in_dim(array.reshape(count, 2, half), y, 1, keepdims=False)
        places = [folded((folded(z) - k + count) % count) for k in range(count)]
        return jnp.stack(
            [lax.dynamic_index_in_dim(array, at, 0, keepdims=False) for at in places]
        )

    names, before = runs_of(names), runs_of(before)
    ids = (names.reshape(here, 1), names.reshape(count, 1, half), before.reshape(here, 1))
    bound = mine(lower_bound, core, hc, 0).reshape(1, hc)
    gain_row = group_gain.reshape(1, HD)
    place = jnp.stack([z, y]).astype(jnp.int32)

    send = (mm(m_own, wm_send) + mm(m_other, wm_send_o)).astype(bf16)
    recv = swap_core(send)
    keep = mm(m_own, wm_keep) + mm(m_other, wm_keep_o)
    wf = w_ffn_in.reshape(width, 2 * units_col)
    pieces = cut(w_down, 2) + cut(wf, 5)
    (a, wo_o), local, _ = step(
        [(up, c[-1]), (swap_chip, w_out)],
        lambda keep, recv: recurrence_local(keep, recv, bound, ids),
        (keep, recv),
    )
    c.append(a)
    *local, seg, low, decay = local
    (peer, peer_decay), _, _ = step([(swap_chip, low), (swap_chip, decay)])

    def finish(seg, decay, peer, peer_decay):
        enter = recurrence_enter(place, seg, decay, peer, peer_decay, False)
        return recurrence_finish(local, enter, keep, recv, gain_row)

    (a, got), (gated, rec, states), _ = step(
        [(up, c[-1]), (swap_chip, pieces[0])],
        finish,
        (seg, decay, peer, peer_decay),
    )
    c.append(a)
    weights = [got]
    c_own, c_other = ordered(c)
    gated = joined(gated, swap_core(gated), core, 1)

    def scatter(own, other, beside):
        sent = paired(own[1], other[1]).astype(bf16)
        for k in range(1, count):
            sends, work, given, take = beside(k)
            moved, made, _ = step([(up, sent), *sends], work, given)
            at = (k + 1) % count
            a = moved[0][:, :width].astype(f32) + own[at].astype(f32)
            b = moved[0][:, width:].astype(f32) + other[at].astype(f32)
            sent = paired(a, b).astype(bf16)
            take(moved[1:], made)
        return a, b

    def gather(own, other, beside):
        runs = [paired(own, other)]
        for k in range(1, count):
            sends, work, given, take = beside(k)
            moved, made, _ = step([(up, runs[-1]), *sends], work, given)
            runs.append(moved[0])
            take(moved[1:], made)
        return ordered(runs)

    def weights_step(k):
        return [(swap_chip, pieces[len(weights)])], None, (), lambda moved, made: weights.extend(moved)

    h_own, h_other = scatter(
        blocks(mm(gated, w_out).astype(bf16)), blocks(mm(gated, wo_o).astype(bf16)), weights_step
    )
    h_own, h_other = x_own + h_own, x_other + h_other

    squares = jnp.sum(h_own * h_own, axis=1) + jnp.sum(h_other * h_other, axis=1)
    squares = squares + swap_core(squares)
    ffn_scale = lax.rsqrt(squares / D + norm_eps)[:, None]
    n_own = (h_own * ffn_scale * ffn_gain).astype(bf16)
    n_other = (h_other * ffn_scale * gains_other[1]).astype(bf16)

    wd_o = jnp.concatenate(weights[:2], 0)
    gu_recv = swap_core(
        (mm_nt(rows(c_own, 1 - core), w_down) + mm_nt(rows(c_other, 1 - core), wd_o)).astype(bf16)
    )
    gu = mm_nt(rows(c_own, core), w_down) + mm_nt(rows(c_other, core), wd_o) + gu_recv.astype(f32)
    f_own, f_other = gather(n_own, n_other, weights_step)
    wf_o = jnp.concatenate(weights[2:], 0)
    f_own, gu = lax.optimization_barrier((f_own, gu))
    fk_own, fs_own = rows(f_own, core), rows(f_own, 1 - core)
    fk_other, fs_other = rows(f_other, core), rows(f_other, 1 - core)
    b_recv = swap_core((mm(fs_own, wf) + mm(fs_other, wf_o)).astype(bf16))
    both = mm(fk_own, wf) + mm(fk_other, wf_o) + b_recv.astype(f32)
    gate, up_part = both[:, :units_col], both[:, units_col:]
    sigma = jax.nn.sigmoid(gate)
    act = gate * sigma
    units = (act * up_part).astype(bf16)
    gb = jnp.concatenate(
        [(gu * up_part * silu_slope(gate, sigma)).astype(bf16), (gu * act).astype(bf16)], 1
    )
    gb_p = swap_core(gb)
    units_p = swap_core(tie(units, gb))
    df_kept = [mm_nt(gb, wf).astype(bf16), mm_nt(gb, wf_o).astype(bf16)]
    df_sent = [mm_nt(gb_p, wf).astype(bf16), mm_nt(gb_p, wf_o).astype(bf16)]
    ck_own, cs_own = rows(c_own, core), rows(c_own, 1 - core)
    ck_other, cs_other = rows(c_other, core), rows(c_other, 1 - core)
    wide = width // 2
    down_sent = [
        (mm_tn(units, ck_other[:, at : at + wide]) + mm_tn(units_p, cs_other[:, at : at + wide]))
        .astype(bf16)
        for at in (0, wide)
    ]

    def by_core(kept, sent):
        each = count // 2
        parts = []
        for k in range(count):
            s = slice(k % each * half, (k % each + 1) * half)
            parts.append(jnp.where(core == k // each, kept[s], sent[s]))
        return parts

    y_queue, x_queue, landed, found = [], [], {}, {}

    def background(work=None, given=(), takes=None, y_pieces=1, x_pieces=1):
        sends, keys, moving = [], [], []
        for _ in range(min(y_pieces, len(y_queue))):
            key, array = y_queue.pop(0)
            keys.append(key)
            sends.append((swap_chip, array))
        n = len(sends)
        for _ in range(min(x_pieces, len(x_queue))):
            moving.append(x_queue.pop(0))
        if pairs:
            sends += [(swap_group, array) for _, array in moving]

        def take(moved, made):
            if takes is not None:
                takes(made)
            landed.update(zip(keys, moved[:n]))
            for at, (key, array) in enumerate(moving):
                if pairs:
                    found[key] = (array, moved[n + at])
                else:
                    found[key] = (array,)

        return sends, work, given, take

    def total(key, *after):
        parts = found[key]
        if after:
            parts = lax.optimization_barrier((*parts, *after))[: len(parts)]
        if pairs:
            return parts[0].astype(f32) + parts[1].astype(f32)
        return lax.psum(parts[0], "dp").astype(f32)

    def queue(name, parts):
        y_queue.extend((f"{name}{n}", part) for n, part in enumerate(parts))

    feed_own = []

    def down_gradient(n):
        def work(u, v, c, d, got):
            return [weight_gradients([u, v], [c, d], [got], columns=(n, wide))]

        return work, (units, units_p, ck_own, cs_own, landed[f"d{n}"])

    def ready_for_group(*keys):
        return lambda made: x_queue.extend(zip(keys, made))

    queue("d", down_sent)

    def ffn_step(k):
        if k == 1:

            def work(f, h, g, p):
                return weight_gradient_pieces([f, h], [g, p], bf16, 4)

            return background(
                work, (fk_other, fs_other, gb, gb_p), lambda made: queue("f", made)
            )
        own, given = down_gradient(k - 2)
        if k == 3:
            return background(own, given, ready_for_group("d1"))

        def work(f, h, g, p, *given):
            return [*own(*given), *weight_gradient_pieces([f, h], [g, p], f32, 4)]

        def takes(made):
            x_queue.append(("d0", made[0]))
            feed_own.extend(made[1:])

        return background(work, (fk_own, fs_own, gb, gb_p, *given), takes)

    kept = []
    df_own, df_other = scatter(
        by_core(df_kept[0], df_sent[0]), by_core(df_kept[1], df_sent[1]), ffn_step
    )

    gain_fo = gains_other[1]
    w_o, w_p = df_own * ffn_gain, df_other * gain_fo
    along = jnp.sum(w_o * h_own, axis=1) + jnp.sum(w_p * h_other, axis=1)
    along = along + swap_core(along)
    factor = ffn_scale**3 * along[:, None] / D
    gh_own = cot_own.astype(f32) + ffn_scale * w_o - h_own * factor
    gh_other = cot_other.astype(f32) + ffn_scale * w_p - h_other * factor
    ffn_part = jnp.sum(df_own * h_own * ffn_scale, axis=0)
    ffn_part_o = jnp.sum(df_other * h_other * ffn_scale, axis=0)

    def back_step(k):
        given = (feed_own[k - 1], landed[f"f{k - 1}"])
        if k == 3:
            return background(lambda a, b: [rounded_sum(a, b)], given, ready_for_group("f2"))

        def work(u, v, w, a, b):
            return [*products([u, v], w), rounded_sum(a, b)]

        def takes(made):
            kept.extend(made[:2])
            x_queue.append((f"f{k - 1}", made[2]))

        return background(work, (units, units_p, w_down if k == 1 else wd_o, *given), takes)

    g_own, g_other = gather(gh_own.astype(bf16), gh_other.astype(bf16), back_step)
    un_own, un_other = by_core(*kept[:2]), by_core(*kept[2:])

    gg_recv = swap_core(
        (mm_nt(g_own, mine(w_out, 1 - core, hc, 0)) + mm_nt(g_other, mine(wo_o, 1 - core, hc, 0)))
        .astype(bf16)
    )
    gg_keep = mm_nt(g_own, mine(w_out, core, hc, 0)) + mm_nt(g_other, mine(wo_o, core, hc, 0))
    do, d_gate, group_part, seg, low = recurrence_back_local(
        gg_keep, gg_recv, rec, keep, recv, gain_row, local[1], local[4]
    )
    core_here = core.astype(jnp.int32).reshape(1)

    def gate_gradients(gate, left, grad, right):
        gate_p = swap_core(gate)
        sent = weight_gradients([left], [grad])
        return [gate_p, sent, head_gradients(core_here, right, gate, gate_p, 0, hc, bf16)]

    (peer,), (d_gate_p, out_sent, gate_sent), _ = step(
        [(swap_chip, low)], gate_gradients, (d_gate, gated, g_other, m_other)
    )

    def finish_back(seg, peer, gate, own, got):
        enter = recurrence_enter(place, seg, decay, peer, peer_decay, True)
        return [
            *recurrence_back_finish(keep, recv, bound, ids, local, states, do, enter, gate),
            rounded_sum(own, got),
        ]

    queue("o", [out_sent])
    queue("g", [gate_sent])
    out_run = paired(un_own[1], un_other[1])
    sends, _, _, take = background(y_pieces=2)
    moved, (dp_keep, bound_part, feed_last), _ = step(
        [(up, out_run), *sends], finish_back, (seg, peer, d_gate, feed_own[3], landed["f3"])
    )
    x_queue.append(("f3", feed_last))

    def out_sum(moved, at):
        a = moved[:, :width].astype(f32) + un_own[at].astype(f32)
        return a, moved[:, width:].astype(f32) + un_other[at].astype(f32)

    out_run = paired(*out_sum(moved[0], 2)).astype(bf16)
    take(moved[1:], [])

    dp_send = swap_core(dp_keep)
    sums_own, sums_other = mm_nt(dp_keep, wm_keep), mm_nt(dp_keep, wm_keep_o)
    sums_own, sums_other = sums_own + mm_nt(dp_send, wm_send), sums_other + mm_nt(dp_send, wm_send_o)
    own, other = blocks(sums_own.astype(bf16)), blocks(sums_other.astype(bf16))
    mix_part = jnp.sum(sums_own * m_own.astype(f32), axis=0) / mix_gain
    mix_part_o = jnp.sum(sums_other * m_other.astype(f32), axis=0) / gains_other[0]
    tail = jnp.concatenate([bound_part[0], group_part[0]])
    small = jnp.concatenate([mix_part, ffn_part, tail])
    small_o = jnp.concatenate([mix_part_o, ffn_part_o, tail])

    def heads_of(left, keep, send, first, parts, kind, plus=()):
        return head_gradients(core_here, left, keep, send, first, hc, kind, plus, parts)

    def first_gradients(keep, send, right, heads, grad, left, o_got, g_got):
        sent = [heads_of(right, keep, send, 0, 2, bf16), heads_of(right, keep, send, 2, 1, bf16)]
        out = weight_gradients([heads], [grad], [o_got])
        return [*sent, out, heads_of(left, keep, send, 3, 1, bf16, [g_got])]

    sends, _, _, take = background()
    dx_run = paired(own[1], other[1])
    moved, made, _ = step(
        [(up, dx_run), (up, out_run), (swap_chip, small_o), *sends],
        first_gradients,
        (dp_keep, dp_send, m_other, gated, g_own, m_own, landed["o0"], landed["g0"]),
    )
    small = small + moved[2]
    take(moved[3:], [])
    x_queue.extend(zip(("o0", "g0"), made[2:]))
    queue("qk", [made[0]])
    queue("v", [made[1]])

    def dx_sum(moved, at):
        a = moved[:, :width].astype(f32) + own[at].astype(f32)
        return a, moved[:, width:].astype(f32) + other[at].astype(f32)

    dx_run = paired(*dx_sum(moved[0], 2)).astype(bf16)
    out_run = paired(*out_sum(moved[1], 3)).astype(bf16)
    def own_gradients(keep, send, left):
        return [
            heads_of(left, keep, send, 0, 2, f32), heads_of(left, keep, send, 2, 1, f32)
        ]

    sends, work, given, take = background(
        own_gradients, (dp_keep, dp_send, m_own), x_pieces=2
    )
    if pairs:
        sends.append((swap_group, small))
    moved, made, _ = step([(up, dx_run), (up, out_run), *sends], work, given)
    small = small + moved[-1] if pairs else lax.psum(small, "dp")
    take(moved[2:-1] if pairs else moved[2:], made)
    of_parts = dict(zip(("qk0", "v0"), made))

    def reduced(key):
        x_queue.append((key, (of_parts[key] + landed[key].astype(f32)).astype(bf16)))

    reduced("qk0")
    dx_run = paired(*dx_sum(moved[0], 3)).astype(bf16)
    out_own, out_other = out_sum(moved[1], 0)
    out_own, out_other = (h_own + out_own).astype(bf16), (h_other + out_other).astype(bf16)
    edge = 2 * width
    bound_sum = small[edge : edge + hc]
    wide = jnp.concatenate([small[:edge], small[edge + hc :]])
    near = lambda a: lax.ppermute(a, "col", [(i, i ^ 1) for i in range(count)])
    far = lambda a: lax.ppermute(a, "col", [(i, i ^ 2) for i in range(count)])
    ffn_pieces = [found[f"f{n}"] if pairs else (total(f"f{n}"),) for n in range(4)]
    each = len(ffn_pieces[0])

    def whole_ffn(*given):
        return [
            halves_of_rows([given[n * each : (n + 1) * each] for n in range(4)], 2)
        ]

    sends, _, _, take = background(x_pieces=2)
    moved, (ffn_whole,), _ = step(
        [(up, dx_run), (near, wide), (swap_chip, out_other), *sends],
        whole_ffn,
        [array for found_piece in ffn_pieces for array in found_piece],
    )
    wide = wide + moved[1]
    out_other = moved[2]
    take(moved[3:], [])
    reduced("v0")
    dx_own, dx_other = dx_sum(moved[0], 0)

    w_o, w_p = dx_own * mix_gain, dx_other * gains_other[0]
    along = jnp.sum(w_o * x_own, axis=1) + jnp.sum(w_p * x_other, axis=1)
    along = along + swap_core(along)
    factor = mix_scale**3 * along[:, None] / D
    gt_own = gh_own + mix_scale * w_o - x_own * factor
    gt_other = gh_other + mix_scale * w_p - x_other * factor
    def two_parts(key):
        arrays = found[key] if pairs else (total(key),)
        return [[array[at : at + width] for array in arrays] for at in (0, width)]

    def one_part(key):
        return list(found[key]) if pairs else [total(key)]

    query, forget = two_parts("qk0")
    most = [query, forget, one_part("g0")]
    counts = [len(part) for part in most]

    def most_of(*given):
        parts = [given[sum(counts[:n]) : sum(counts[: n + 1])] for n in range(3)]
        return [stacked([parts[0], parts[1], (), parts[2]])]

    sends, _, _, take = background(x_pieces=2)
    moved, (mix_whole,), _ = step(
        [(swap_chip, gt_other.astype(bf16)), (far, wide), *sends],
        most_of,
        [array for part in most for array in part],
    )
    grad_other = moved[0].astype(f32)
    wide = wide + moved[1]
    take(moved[2:], [])
    mix_whole = filled(mix_whole, 2, one_part("v0"))
    turned = swap_core(jnp.concatenate([bound_sum, wide[edge:]]))
    grad_bound = joined(bound_sum, turned[:hc], core, 0)

    return (
        joined(out_own, out_other, y, 0),
        joined(gt_own, grad_other, y, 0),
        wide[:width],
        mix_whole,
        grad_bound,
        wide[edge:] + turned[hc:],
        total("o0"),
        wide[width:edge],
        ffn_whole,
        jnp.concatenate([total("d0"), total("d1")], 1),
    )


def solution(mesh):
    return jax.shard_map(
        shards,
        mesh=mesh,
        in_specs=(
            P(("dp", "col"), "row"),
            P("dp"),
            P("row"),
            P("row", None, "col"),
            P("col"),
            P(),
            P("col", "row"),
            P("row"),
            P("row", None, "col"),
            P("col", "row"),
            P(("dp", "col"), "row"),
        ),
        out_specs=(
            P(("dp", "col"), "row"),
            P(("dp", "col"), "row"),
            P("row"),
            P("row", None, "col"),
            P("col"),
            P(),
            P("col", "row"),
            P("row"),
            P("row", None, "col"),
            P("col", "row"),
        ),
        check_vma=False,
    )
```

```python
from functools import partial

import jax
import jax.numpy as jnp
from jax import lax
from jax.experimental import pallas as pl
from jax.experimental.pallas import tpu as pltpu
from jax.sharding import PartitionSpec as P

D = 2048
HD = 128
BLOCK = 64
norm_eps = 1e-06
bf16 = jnp.bfloat16
f32 = jnp.float32

CORE = [(0, 1), (1, 0), (2, 3), (3, 2)]
CHIP = [(0, 2), (2, 0), (1, 3), (3, 1)]


def swap_core(x):
    return lax.ppermute(x, "row", CORE)


def swap_chip(x):
    return lax.ppermute(x, "row", CHIP)


def tie(x, *others):
    return lax.optimization_barrier((x, *others))[0]


def mm(left, right):
    return lax.dot_general(left, right, (((1,), (0,)), ((), ())), preferred_element_type=f32)


def mm_nt(left, right):
    return lax.dot_general(left, right, (((1,), (1,)), ((), ())), preferred_element_type=f32)


def mm_tn(left, right):
    return lax.dot_general(left, right, (((0,), (0,)), ((), ())), preferred_element_type=f32)


def silu_slope(value, sigma):
    return sigma * (1.0 + value * (1.0 - sigma))


def split_mm(left, value):
    high = value.astype(bf16)
    low = (value - high.astype(f32)).astype(bf16)
    return mm(left, high) + mm(left, low)


def run_masks(i, idc_ref, idr_ref, prev_ref):
    s = slice(i * BLOCK, (i + 1) * BLOCK)
    idc = idc_ref[s, :]
    idr = idr_ref[0, :, s]
    prev = prev_ref[s, :]
    before = prev[0:1, :]
    last = idc[BLOCK - 1 : BLOCK, :]
    t = lax.broadcasted_iota(jnp.int32, (BLOCK, BLOCK), 0)
    u = lax.broadcasted_iota(jnp.int32, (BLOCK, BLOCK), 1)
    same = idc == idr
    heads = (idc == before).astype(f32)
    tails = (idc == last).astype(f32)
    through = (last == before).astype(f32)
    old = (idc == prev).astype(f32)
    return t, u, same, heads, tails, through, old


def run_decays(f_raw, lb, t, u):
    closed = jax.nn.sigmoid(-f_raw)
    keys = (1.0 - lb) * closed
    total = split_mm((t >= u).astype(bf16), jnp.log1p(-keys))
    middle = total[BLOCK // 2 - 1 : BLOCK // 2, :]
    final = total[BLOCK - 1 : BLOCK, :]
    return closed, keys, total, middle, final


def col(h, part=0, heads=1):
    start = (part * heads + h) * HD
    return slice(start, start + HD)


def local_kernel(
    keep_ref, recv_ref, lb_ref, idc_ref, idr_ref, prev_ref,
    inner_ref, qh_ref, kh_ref, vb_ref, decay_ref, seg_ref, low_ref, segd_ref,
):
    heads = lb_ref.shape[1] // HD
    state = [jnp.zeros((HD, HD), f32)] * heads
    passing = [jnp.ones((1, HD), f32)] * heads
    for i in range(keep_ref.shape[0] // BLOCK):
        s = slice(i * BLOCK, (i + 1) * BLOCK)
        t, u, same, head, tails, through, _ = run_masks(i, idc_ref, idr_ref, prev_ref)
        for h in range(heads):
            c = col(h)

            def raw(part):
                p = col(h, part, heads)
                return keep_ref[s, p] + recv_ref[s, p].astype(f32)

            q_raw = raw(0)
            vb = raw(2).astype(bf16)
            q = q_raw * jax.nn.sigmoid(q_raw)
            _, keys, total, middle, final = run_decays(raw(1), lb_ref[:, c], t, u)
            qt = (q * jnp.exp(total - middle)).astype(bf16)
            kt = (keys * jnp.exp(middle - total)).astype(bf16)
            scores = jnp.where(same & (t >= u), mm_nt(qt, kt), 0.0).astype(bf16)
            inner_ref[s, c] = mm(scores, vb)
            qh_ref[s, c] = (q * jnp.exp(total) * head).astype(bf16)
            kh = (keys * jnp.exp(final - total) * tails).astype(bf16)
            kh_ref[s, c] = kh
            vb_ref[s, c] = vb
            keep = jnp.exp(final) * through
            decay_ref[0, i : i + 1, c] = keep
            state[h] = keep * state[h] + mm_tn(vb, kh)
            passing[h] = passing[h] * keep
    for h in range(heads):
        seg_ref[0, h] = state[h]
        low_ref[0, h] = state[h].astype(bf16)
        segd_ref[0, :, col(h)] = passing[h]


def enter_kernel(reverse, place_ref, seg_ref, segd_ref, peer_ref, peerd_ref, out_ref):
    z, y = place_ref[0], place_ref[1]
    count, heads = seg_ref.shape[:2]
    peer_first = (y == 0) if reverse else (y == 1)
    state = [jnp.zeros((HD, HD), f32)] * heads
    for place in reversed(range(count)) if reverse else range(count):
        k = lax.rem((z ^ (z >> 1)) - (place ^ (place >> 1)) + count, count)
        for h in range(heads):
            add = peer_ref[k, h].astype(f32)
            scale = peerd_ref[k, :, col(h)]
            s = jnp.where(peer_first, scale, 1.0) * state[h] + jnp.where(peer_first, add, 0.0)
            out_ref[k, h] = s
            s = segd_ref[k, :, col(h)] * s + seg_ref[k, h]
            state[h] = jnp.where(peer_first, 1.0, scale) * s + jnp.where(peer_first, 0.0, add)


def finish_kernel(
    inner_ref, qh_ref, kh_ref, vb_ref, decay_ref, enter_ref, keep_ref, recv_ref, gain_ref,
    gated_ref, rec_ref, st_ref,
):
    heads = enter_ref.shape[1]
    state = [enter_ref[0, h] for h in range(heads)]
    for i in range(qh_ref.shape[0] // BLOCK):
        s = slice(i * BLOCK, (i + 1) * BLOCK)
        for h in range(heads):
            c = col(h)
            low = state[h].astype(bf16)
            st_ref[0, i, h] = low
            rec = inner_ref[s, c] + mm_nt(qh_ref[s, c], low)
            rec_ref[s, c] = rec
            scale = lax.rsqrt(jnp.mean(rec * rec, axis=1, keepdims=True) + norm_eps)
            g_raw = keep_ref[s, c] + recv_ref[s, c].astype(f32)
            gate = g_raw * jax.nn.sigmoid(g_raw)
            gated_ref[s, c] = (rec * scale * gain_ref[...] * gate).astype(bf16)
            state[h] = decay_ref[0, i : i + 1, c] * state[h] + mm_tn(vb_ref[s, c], kh_ref[s, c])


def back_local_kernel(
    kd, rd, rec_ref, keep_ref, recv_ref, gain_ref, qh_ref, decay_ref,
    do_ref, dg_ref, group_ref, seg_ref, low_ref,
):
    @pl.when(pl.program_id(0) == 0)
    def _():
        group_ref[...] = jnp.zeros_like(group_ref)

    gain = gain_ref[...]
    heads = seg_ref.shape[1]
    adjoint = [jnp.zeros((HD, HD), f32)] * heads
    group = jnp.zeros((1, HD), f32)
    for i in reversed(range(qh_ref.shape[0] // BLOCK)):
        s = slice(i * BLOCK, (i + 1) * BLOCK)
        for h in range(heads):
            c = col(h)
            grad = kd[s, c] + rd[s, c].astype(f32)
            rec = rec_ref[s, c]
            scale = lax.rsqrt(jnp.mean(rec * rec, axis=1, keepdims=True) + norm_eps)
            normed = rec * scale
            g_raw = keep_ref[s, c] + recv_ref[s, c].astype(f32)
            sigma = jax.nn.sigmoid(g_raw)
            act = g_raw * sigma
            both = grad * normed
            group = group + jnp.sum(both * act, axis=0, keepdims=True)
            dg_ref[s, c] = (both * gain * silu_slope(g_raw, sigma)).astype(bf16)
            dn = grad * gain * act
            do = (scale * (dn - normed * jnp.mean(dn * normed, axis=1, keepdims=True))).astype(bf16)
            do_ref[s, c] = do
            adjoint[h] = decay_ref[0, i : i + 1, c] * adjoint[h] + mm_tn(do, qh_ref[s, c])
    group_ref[...] += group
    for h in range(heads):
        seg_ref[0, h] = adjoint[h]
        low_ref[0, h] = adjoint[h].astype(bf16)


def back_finish_kernel(
    keep_ref, recv_ref, lb_ref, idc_ref, idr_ref, prev_ref,
    qh_ref, kh_ref, vb_ref, decay_ref, st_ref, do_ref, enter_ref, gate_ref,
    grad_ref, bound_ref,
):
    @pl.when(pl.program_id(0) == 0)
    def _():
        bound_ref[...] = jnp.zeros_like(bound_ref)

    heads = enter_ref.shape[1]
    grad_ref[:, 3 * gate_ref.shape[1] :] = gate_ref[...]
    adjoint = [enter_ref[0, h] for h in range(heads)]
    bound = [jnp.zeros((1, HD), f32)] * heads
    for i in reversed(range(keep_ref.shape[0] // BLOCK)):
        s = slice(i * BLOCK, (i + 1) * BLOCK)
        t, u, same, head, tails, through, old = run_masks(i, idc_ref, idr_ref, prev_ref)
        causal = same & (t >= u)
        later = (same & (u >= t)).astype(bf16)
        for h in range(heads):
            c = col(h)

            def raw(part):
                p = col(h, part, heads)
                return keep_ref[s, p] + recv_ref[s, p].astype(f32)

            q_raw = raw(0)
            sigma = jax.nn.sigmoid(q_raw)
            q = q_raw * sigma
            closed, keys, total, middle, final = run_decays(raw(1), lb_ref[:, c], t, u)
            out = jnp.exp(total - middle)
            back = jnp.exp(middle - total)
            qt = (q * out).astype(bf16)
            kt = (keys * back).astype(bf16)
            scores = jnp.where(causal, mm_nt(qt, kt), 0.0).astype(bf16)
            vb = vb_ref[s, c]
            kh = kh_ref[s, c]
            do = do_ref[s, c]
            st = st_ref[0, i, h]
            low = adjoint[h].astype(bf16)
            keep = decay_ref[0, i : i + 1, c]
            ds = jnp.where(causal, mm_nt(do, vb), 0.0).astype(bf16)
            dq = mm(ds, kt) * out + mm(do, st) * (jnp.exp(total) * head)
            dkh = mm(vb, low)
            dk = mm_tn(ds, qt) * back + dkh * (jnp.exp(final - total) * tails)
            grad_ref[s, col(h, 2, heads)] = (mm_tn(scores, do) + mm_nt(kh, low)).astype(bf16)
            ends = keep * jnp.sum(adjoint[h] * st.astype(f32), axis=0, keepdims=True) + jnp.sum(
                kh.astype(f32) * dkh, axis=0, keepdims=True
            )
            dlog = split_mm(later, q * dq - keys * dk) + tails * ends
            key_total = dk - old * dlog / (1.0 - keys)
            bound[h] = bound[h] - jnp.sum(key_total * closed, axis=0, keepdims=True)
            grad_ref[s, col(h, 1, heads)] = (-key_total * keys * (1.0 - closed)).astype(bf16)
            grad_ref[s, col(h, 0, heads)] = (dq * silu_slope(q_raw, sigma)).astype(bf16)
            adjoint[h] = keep * adjoint[h] + mm_tn(do, qh_ref[s, c])
    for h in range(heads):
        bound_ref[:, col(h)] += bound[h]


def shape(dims, kind):
    return jax.ShapeDtypeStruct(dims, kind)


COST = pl.CostEstimate(flops=0, bytes_accessed=0, transcendentals=0)
SMEM = pl.BlockSpec(memory_space=pltpu.SMEM)
VMEM = pl.BlockSpec(memory_space=pltpu.VMEM)


def run_block(*dims, at=0):
    return pl.BlockSpec(dims, lambda j: (j, *([0] * (len(dims) - 2)), at))


def whole(*dims):
    return pl.BlockSpec(dims, lambda j: (0,) * len(dims))


def recurrence_local(keep, recv, bound, ids):
    runs, _, run = ids[1].shape
    width = bound.shape[1]
    heads = width // HD
    chunks = run // BLOCK
    tokens = runs * run
    return pl.pallas_call(
        local_kernel,
        grid=(runs,),
        in_specs=[
            run_block(run, 4 * width), run_block(run, 4 * width), whole(1, width),
            run_block(run, 1), run_block(1, 1, run), run_block(run, 1),
        ],
        out_specs=[run_block(run, width)] * 4
        + [run_block(1, chunks, width)]
        + [run_block(1, heads, HD, HD)] * 2
        + [run_block(1, 1, width)],
        out_shape=[
            shape((tokens, width), f32),
            shape((tokens, width), bf16),
            shape((tokens, width), bf16),
            shape((tokens, width), bf16),
            shape((runs, chunks, width), f32),
            shape((runs, heads, HD, HD), f32),
            shape((runs, heads, HD, HD), bf16),
            shape((runs, 1, width), f32),
        ],
        cost_estimate=COST,
        name="recurrence_local",
    )(keep, recv, bound, *ids)


def recurrence_enter(place, seg, segd, peer, peerd, reverse):
    return pl.pallas_call(
        partial(enter_kernel, reverse),
        in_specs=[SMEM] + [VMEM] * 4,
        out_specs=VMEM,
        out_shape=shape(seg.shape, f32),
        cost_estimate=COST,
        name="recurrence_enter_back" if reverse else "recurrence_enter",
    )(place, seg, segd, peer, peerd)


def recurrence_finish(local, enter, keep, recv, gain):
    inner, qh, kh, vb, decay = local
    runs, chunks, width = decay.shape
    heads = width // HD
    run = chunks * BLOCK
    tokens = runs * run
    cols = run_block(run, width)
    gate = run_block(run, width, at=3)
    return pl.pallas_call(
        finish_kernel,
        grid=(runs,),
        in_specs=[
            cols, cols, cols, cols, run_block(1, chunks, width), run_block(1, heads, HD, HD),
            gate, gate, whole(1, HD),
        ],
        out_specs=[cols, cols, run_block(1, chunks, heads, HD, HD)],
        out_shape=[
            shape((tokens, width), bf16),
            shape((tokens, width), f32),
            shape((runs, chunks, heads, HD, HD), bf16),
        ],
        cost_estimate=COST,
        name="recurrence_finish",
    )(inner, qh, kh, vb, decay, enter, keep, recv, gain)


def recurrence_back_local(kd, rd, rec, keep, recv, gain, qh, decay):
    runs, chunks, width = decay.shape
    heads = width // HD
    run = chunks * BLOCK
    tokens = runs * run
    cols = run_block(run, width)
    gate = run_block(run, width, at=3)
    return pl.pallas_call(
        back_local_kernel,
        grid=(runs,),
        in_specs=[
            cols, cols, cols, gate, gate, whole(1, HD), cols, run_block(1, chunks, width),
        ],
        out_specs=[cols, cols, whole(1, HD)] + [run_block(1, heads, HD, HD)] * 2,
        out_shape=[
            shape((tokens, width), bf16),
            shape((tokens, width), bf16),
            shape((1, HD), f32),
            shape((runs, heads, HD, HD), f32),
            shape((runs, heads, HD, HD), bf16),
        ],
        cost_estimate=COST,
        name="recurrence_back_local",
    )(kd, rd, rec, keep, recv, gain, qh, decay)


def recurrence_back_finish(keep, recv, bound, ids, local, states, do, enter, gate):
    _, qh, kh, vb, decay = local
    runs, chunks, width = decay.shape
    heads = width // HD
    run = chunks * BLOCK
    tokens = runs * run
    cols = run_block(run, width)
    return pl.pallas_call(
        back_finish_kernel,
        grid=(runs,),
        in_specs=[
            run_block(run, 4 * width), run_block(run, 4 * width), whole(1, width),
            run_block(run, 1), run_block(1, 1, run), run_block(run, 1),
            cols, cols, cols, run_block(1, chunks, width),
            run_block(1, chunks, heads, HD, HD), cols, run_block(1, heads, HD, HD), cols,
        ],
        out_specs=[run_block(run, 4 * width), whole(1, width)],
        out_shape=[shape((tokens, 4 * width), bf16), shape((1, width), f32)],
        cost_estimate=COST,
        name="recurrence_back_finish",
    )(keep, recv, bound, *ids, qh, kh, vb, decay, states, do, enter, gate)


def weight_kernel(pairs, *refs):
    lefts, rights = refs[:pairs], refs[pairs : 2 * pairs]
    *plus, out = refs[2 * pairs :]
    total = sum(mm_tn(left[...], right[...]) for left, right in zip(lefts, rights))
    out[...] = (total + sum(part[...].astype(f32) for part in plus)).astype(out.dtype)


def weight_gradients(lefts, rights, plus=(), rows=None, columns=None, tile=256):
    at, tall = rows or (0, lefts[0].shape[1])
    first, wide = columns or (0, rights[0].shape[1])
    tiles = wide // tile
    out = pl.BlockSpec((tall, tile), lambda j: (0, j))
    return pl.pallas_call(
        partial(weight_kernel, len(lefts)),
        grid=(tiles,),
        in_specs=[pl.BlockSpec((left.shape[0], tall), lambda j: (0, at)) for left in lefts]
        + [pl.BlockSpec((r.shape[0], tile), lambda j: (0, first * tiles + j)) for r in rights]
        + [out] * len(plus),
        out_specs=out,
        out_shape=shape((tall, wide), bf16),
        cost_estimate=COST,
        name="weight_gradients",
    )(*lefts, *rights, *plus)


def pieces_kernel(pairs, *refs):
    lefts, rights, outs = refs[:pairs], refs[pairs : 2 * pairs], refs[2 * pairs :]
    total = sum(mm_tn(left[...], right[...]) for left, right in zip(lefts, rights))
    each = outs[0].shape[0]
    for n, out in enumerate(outs):
        out[...] = total[n * each : (n + 1) * each].astype(out.dtype)


def weight_gradient_pieces(lefts, rights, kind, pieces, tile=256):
    tall, wide = lefts[0].shape[1] // pieces, rights[0].shape[1]
    return pl.pallas_call(
        partial(pieces_kernel, len(lefts)),
        grid=(wide // tile,),
        in_specs=[whole(*left.shape) for left in lefts]
        + [pl.BlockSpec((right.shape[0], tile), lambda j: (0, j)) for right in rights],
        out_specs=[pl.BlockSpec((tall, tile), lambda j: (0, j))] * pieces,
        out_shape=[shape((tall, wide), kind)] * pieces,
        cost_estimate=COST,
        name="weight_gradient_pieces",
    )(*lefts, *rights)


def sum_kernel(own_ref, got_ref, out_ref):
    out_ref[...] = (own_ref[...] + got_ref[...].astype(f32)).astype(bf16)


def rounded_sum(own, got):
    return pl.pallas_call(
        sum_kernel,
        in_specs=[VMEM] * 2,
        out_specs=VMEM,
        out_shape=shape(own.shape, bf16),
        cost_estimate=COST,
        name="rounded_sum",
    )(own, got)


def halves_kernel(pieces, *refs):
    *given, out_ref = refs
    each = len(given) // pieces
    wide = out_ref.shape[2]
    rows = out_ref.shape[0]
    for n in range(pieces):

        @pl.when(pl.program_id(0) == n)
        def _():
            at = pl.ds(pl.multiple_of(pl.program_id(1) * rows, rows), rows)
            for part in range(out_ref.shape[1]):
                cols = slice(part * wide, (part + 1) * wide)
                value = sum(ref[at, cols].astype(f32) for ref in given[n * each : (n + 1) * each])
                out_ref[:, part, :] = value


def halves_of_rows(pieces, parts, rows=32):
    tall, wide = pieces[0][0].shape
    steps = tall // rows
    given = [array for piece in pieces for array in piece]
    return pl.pallas_call(
        partial(halves_kernel, len(pieces)),
        grid=(len(pieces), steps),
        in_specs=[pl.BlockSpec(a.shape, lambda n, j: (0, 0)) for a in given],
        out_specs=pl.BlockSpec((rows, parts, wide // parts), lambda n, j: (n * steps + j, 0, 0)),
        out_shape=shape((len(pieces) * tall, parts, wide // parts), f32),
        cost_estimate=COST,
        compiler_params=pltpu.CompilerParams(vmem_limit_bytes=40 * 2**20),
        name="halves_of_rows",
    )(*given)


def stack_kernel(counts, *refs):
    *given, out_ref = refs
    for part, count in enumerate(counts):
        refs_here, given = given[:count], given[count:]
        if count:
            out_ref[:, part, :] = sum(ref[...].astype(f32) for ref in refs_here)
        else:
            out_ref[:, part, :] = jnp.zeros((out_ref.shape[0], out_ref.shape[2]), f32)


def stacked(parts, rows=128):
    tall, wide = parts[0][0].shape
    given = [array for part in parts for array in part]
    return pl.pallas_call(
        partial(stack_kernel, [len(part) for part in parts]),
        grid=(tall // rows,),
        in_specs=[pl.BlockSpec((rows, wide), lambda j: (j, 0))] * len(given),
        out_specs=pl.BlockSpec((rows, len(parts), wide), lambda j: (j, 0, 0)),
        out_shape=shape((tall, len(parts), wide), f32),
        cost_estimate=COST,
        name="stacked",
    )(*given)


def product_kernel(right_ref, *refs):
    lefts, outs = refs[: len(refs) // 2], refs[len(refs) // 2 :]
    for left, out in zip(lefts, outs):
        out[...] = mm(left[...], right_ref[...]).astype(out.dtype)


def products(lefts, right, tile=256):
    wide = right.shape[1]
    return pl.pallas_call(
        product_kernel,
        grid=(wide // tile,),
        in_specs=[pl.BlockSpec((right.shape[0], tile), lambda j: (0, j))]
        + [whole(*left.shape) for left in lefts],
        out_specs=[pl.BlockSpec((left.shape[0], tile), lambda j: (0, j)) for left in lefts],
        out_shape=[shape((left.shape[0], wide), bf16) for left in lefts],
        cost_estimate=COST,
        name="products",
    )(right, *lefts)


def heads_kernel(first, half, core_ref, left_ref, own_ref, peer_ref, *refs):
    *plus, out_ref = refs
    core = core_ref[0]
    tall = left_ref.shape[1]
    for part in range(out_ref.shape[0] // tall):
        rows = slice(part * tall, (part + 1) * tall)
        given = slice((first + part) * half, (first + part + 1) * half)
        for right_ref, at in ((own_ref, core), (peer_ref, 1 - core)):
            cols = pl.ds(pl.multiple_of(at * half, half), half)
            total = mm_tn(left_ref[...], right_ref[:, given])
            for more in plus:
                total = total + more[rows, cols].astype(f32)
            out_ref[rows, cols] = total.astype(out_ref.dtype)


def head_gradients(core, left, own, peer, first, half, kind, plus=(), parts=1):
    return pl.pallas_call(
        partial(heads_kernel, first, half),
        in_specs=[SMEM] + [VMEM] * (3 + len(plus)),
        out_specs=VMEM,
        out_shape=shape((parts * left.shape[1], 2 * half), kind),
        cost_estimate=COST,
        name="head_gradients",
    )(core, left, own, peer, *plus)


def fill_kernel(part, *refs):
    base_ref, *given, out_ref = refs
    out_ref[...] = base_ref[...]
    out_ref[:, part, :] = sum(ref[...].astype(f32) for ref in given)


def filled(base, part, given, rows=128):
    tall, parts, wide = base.shape
    block = pl.BlockSpec((rows, parts, wide), lambda j: (j, 0, 0))
    return pl.pallas_call(
        partial(fill_kernel, part),
        grid=(tall // rows,),
        in_specs=[block] + [pl.BlockSpec((rows, wide), lambda j: (j, 0))] * len(given),
        out_specs=block,
        out_shape=shape(base.shape, f32),
        input_output_aliases={0: 0},
        cost_estimate=COST,
        name="filled",
    )(base, *given)


def swap_group(x):
    return lax.ppermute(x, "dp", [(0, 1), (1, 0)])


def folded(place):
    return place ^ (place >> 1)


def up(x):
    count = lax.axis_size("col")
    return lax.ppermute(x, "col", [(folded(n), folded((n + 1) % count)) for n in range(count)])


def paired(own, other):
    return jnp.concatenate([own, other], 1)


def step(sends, work=None, given=(), join=()):
    n = len(sends)
    arrays = lax.optimization_barrier((*(array for _, array in sends), *given))
    moved = [mover(array) for (mover, _), array in zip(sends, arrays)]
    made = tuple(work(*arrays[n:])) if work else ()
    done = lax.optimization_barrier((*moved, *made, *join))
    return list(done[:n]), list(done[n : n + len(made)]), list(done[n + len(made) :])


def ordered(runs):
    width = runs[0].shape[1] // 2
    return (
        jnp.concatenate([run[:, :width] for run in runs], 0),
        jnp.concatenate([run[:, width:] for run in runs], 0),
    )


def cut(array, count):
    each = -(-array.shape[0] // count)
    each = -(-each // 16) * 16
    return [array[at : at + each] for at in range(0, array.shape[0], each)]


def shards(
    tokens,
    segments,
    mix_gain,
    w_mix,
    lower_bound,
    group_gain,
    w_out,
    ffn_gain,
    w_ffn_in,
    w_down,
    cotangent,
):
    row = lax.axis_index("row")
    core = row % 2
    y = row // 2
    z = lax.axis_index("col")
    count = lax.axis_size("col")
    pairs = lax.axis_size("dp") == 2
    half = tokens.shape[0] // 2
    width = tokens.shape[1]
    hc = w_mix.shape[2] // 2
    units_col = w_down.shape[0]
    here = count * half
    hb = here // 2

    def mine(x, at, size, axis):
        return lax.dynamic_slice_in_dim(x, at * size, size, axis)

    def rows(x, at):
        return mine(x, at, hb, 0)

    def joined(first_if_zero, second_if_zero, flag, axis):
        return jnp.where(
            flag == 0,
            jnp.concatenate([first_if_zero, second_if_zero], axis),
            jnp.concatenate([second_if_zero, first_if_zero], axis),
        )

    def blocks(array):
        return [array[k * half : (k + 1) * half] for k in range(count)]

    tok_own = mine(tokens, y, half, 0)
    (tok_other,), _, _ = step([(swap_chip, mine(tokens, 1 - y, half, 0))])
    cot_own, cot_send = mine(cotangent, y, half, 0), mine(cotangent, 1 - y, half, 0)
    group = lax.axis_index("dp")

    def half_of(array):
        return mine(array, group, array.shape[0] // 2, 0) if pairs else array

    def over_group(array):
        return [(swap_group, array)] if pairs else []

    def assembled(parts, parts_x):
        if not pairs:
            return jnp.concatenate(parts, 0)
        rows_half = sum(part.shape[0] for part in parts)
        both = jnp.zeros((2 * rows_half, *parts[0].shape[1:]), parts[0].dtype)
        for which, given in ((group, parts), (1 - group, parts_x)):
            at = which * rows_half
            for part in given:
                both = lax.dynamic_update_slice(both, part, (at, *[0] * (part.ndim - 1)))
                at += part.shape[0]
        return both

    wm_parts = cut(half_of(w_mix), 2)
    first = swap_chip(tie(wm_parts[0], tok_other))
    gains_other = swap_chip(tie(jnp.stack([mix_gain, ffn_gain]), tok_other))
    x_own, x_other = tok_own.astype(f32), tok_other.astype(f32)
    squares = jnp.sum(x_own * x_own, axis=1) + jnp.sum(x_other * x_other, axis=1)
    squares = squares + swap_core(squares)
    mix_scale = lax.rsqrt(squares / D + norm_eps)[:, None]
    m = [
        paired(x_own * mix_scale * mix_gain, x_other * mix_scale * gains_other[0]).astype(bf16)
    ]
    (a, cot_other), _, (first,) = step([(up, m[0]), (swap_chip, cot_send)], join=[first])
    m.append(a)
    (a, second, *first_x), _, _ = step(
        [(up, m[1]), (swap_chip, wm_parts[1]), *over_group(first)]
    )
    m.append(a)
    wf = w_ffn_in.reshape(width, 2 * units_col)
    pieces = [half_of(w_down), *cut(half_of(wf), 3)]
    moved, _, _ = step(
        [(lambda v: v, piece) for piece in pieces]
        + [(up, m[2]), (swap_chip, w_out), *over_group(second)]
    )
    pieces, (a, wo_o, *second_x) = moved[: len(pieces)], moved[len(pieces) :]
    m.append(a)
    c = [paired(cot_own, cot_other)]
    wm_other = assembled([first, second], [*first_x, *second_x])
    m_own, m_other = ordered(m)

    def columns(w, at):
        return mine(w, at, hc, 2).reshape(width, 4 * hc)

    wm_keep, wm_send = columns(w_mix, core), columns(w_mix, 1 - core)
    wm_keep_o, wm_send_o = columns(wm_other, core), columns(wm_other, 1 - core)

    names = segments.astype(f32)
    before = jnp.concatenate([jnp.full((1,), -1.0, f32), names[:-1]])

    def runs_of(array):
        array = lax.dynamic_index_in_dim(array.reshape(count, 2, half), y, 1, keepdims=False)
        places = [folded((folded(z) - k + count) % count) for k in range(count)]
        return jnp.stack(
            [lax.dynamic_index_in_dim(array, at, 0, keepdims=False) for at in places]
        )

    names, before = runs_of(names), runs_of(before)
    ids = (names.reshape(here, 1), names.reshape(count, 1, half), before.reshape(here, 1))
    bound = mine(lower_bound, core, hc, 0).reshape(1, hc)
    gain_row = group_gain.reshape(1, HD)
    place = jnp.stack([z, y]).astype(jnp.int32)

    weights, weights_x = [], []

    def weights_step(k=0):
        sends = [(swap_chip, pieces[len(weights)])] if len(weights) < len(pieces) else []
        n = len(sends)
        if pairs and len(weights_x) < len(weights):
            sends.append((swap_group, weights[len(weights_x)]))

        def take(moved, made):
            weights.extend(moved[:n])
            weights_x.extend(moved[n:])

        return sends, None, (), take

    send = (mm(m_own, wm_send) + mm(m_other, wm_send_o)).astype(bf16)
    recv = swap_core(send)
    keep = mm(m_own, wm_keep) + mm(m_other, wm_keep_o)
    sends, _, _, take = weights_step()
    (a, *moved), local, _ = step(
        [(up, c[-1]), *sends],
        lambda keep, recv: recurrence_local(keep, recv, bound, ids),
        (keep, recv),
    )
    take(moved, [])
    c.append(a)
    *local, seg, low, decay = local
    more = [(swap_group, weights[0])] if pairs else []
    (a, peer, peer_decay, *moved), _, _ = step(
        [(up, c[-1]), (swap_chip, low), (swap_chip, decay), *more]
    )
    c.append(a)
    weights_x.extend(moved)

    def finish(seg, decay, peer, peer_decay):
        enter = recurrence_enter(place, seg, decay, peer, peer_decay, False)
        return recurrence_finish(local, enter, keep, recv, gain_row)

    sends, _, _, take = weights_step()
    (a, *moved), (gated, rec, states), _ = step(
        [(up, c[-1]), *sends],
        finish,
        (seg, decay, peer, peer_decay),
    )
    c.append(a)
    take(moved, [])
    c_own, c_other = ordered(c)
    gated = joined(gated, swap_core(gated), core, 1)

    def scatter(own, other, beside):
        sent = paired(own[1], other[1]).astype(bf16)
        for k in range(1, count):
            sends, work, given, take = beside(k)
            moved, made, _ = step([(up, sent), *sends], work, given)
            at = (k + 1) % count
            a = moved[0][:, :width].astype(f32) + own[at].astype(f32)
            b = moved[0][:, width:].astype(f32) + other[at].astype(f32)
            sent = paired(a, b).astype(bf16)
            take(moved[1:], made)
        return a, b

    def gather(own, other, beside):
        runs = [paired(own, other)]
        for k in range(1, count):
            sends, work, given, take = beside(k)
            moved, made, _ = step([(up, runs[-1]), *sends], work, given)
            runs.append(moved[0])
            take(moved[1:], made)
        return ordered(runs)

    h_own, h_other = scatter(
        blocks(mm(gated, w_out).astype(bf16)), blocks(mm(gated, wo_o).astype(bf16)), weights_step
    )
    h_own, h_other = x_own + h_own, x_other + h_other

    squares = jnp.sum(h_own * h_own, axis=1) + jnp.sum(h_other * h_other, axis=1)
    squares = squares + swap_core(squares)
    ffn_scale = lax.rsqrt(squares / D + norm_eps)[:, None]
    n_own = (h_own * ffn_scale * ffn_gain).astype(bf16)
    n_other = (h_other * ffn_scale * gains_other[1]).astype(bf16)

    wd_o = assembled(weights[:1], weights_x[:1])
    gu_recv = swap_core(
        (mm_nt(rows(c_own, 1 - core), w_down) + mm_nt(rows(c_other, 1 - core), wd_o)).astype(bf16)
    )
    gu = mm_nt(rows(c_own, core), w_down) + mm_nt(rows(c_other, core), wd_o) + gu_recv.astype(f32)
    f_own, f_other = gather(n_own, n_other, lambda k: ([], None, (), lambda moved, made: None))
    wf_o = assembled(weights[1:], weights_x[1:])
    f_own, gu = lax.optimization_barrier((f_own, gu))
    fk_own, fs_own = rows(f_own, core), rows(f_own, 1 - core)
    fk_other, fs_other = rows(f_other, core), rows(f_other, 1 - core)
    b_recv = swap_core((mm(fs_own, wf) + mm(fs_other, wf_o)).astype(bf16))
    both = mm(fk_own, wf) + mm(fk_other, wf_o) + b_recv.astype(f32)
    gate, up_part = both[:, :units_col], both[:, units_col:]
    sigma = jax.nn.sigmoid(gate)
    act = gate * sigma
    units = (act * up_part).astype(bf16)
    gb = jnp.concatenate(
        [(gu * up_part * silu_slope(gate, sigma)).astype(bf16), (gu * act).astype(bf16)], 1
    )
    gb_p = swap_core(gb)
    units_p = swap_core(tie(units, gb))
    df_kept = [mm_nt(gb, wf).astype(bf16), mm_nt(gb, wf_o).astype(bf16)]
    df_sent = [mm_nt(gb_p, wf).astype(bf16), mm_nt(gb_p, wf_o).astype(bf16)]
    ck_own, cs_own = rows(c_own, core), rows(c_own, 1 - core)
    ck_other, cs_other = rows(c_other, core), rows(c_other, 1 - core)
    wide = width // 2
    down_sent = [
        (mm_tn(units, ck_other[:, at : at + wide]) + mm_tn(units_p, cs_other[:, at : at + wide]))
        .astype(bf16)
        for at in (0, wide)
    ]

    def by_core(kept, sent):
        each = count // 2
        parts = []
        for k in range(count):
            s = slice(k % each * half, (k % each + 1) * half)
            parts.append(jnp.where(core == k // each, kept[s], sent[s]))
        return parts

    y_queue, x_queue, landed, found = [], [], {}, {}

    def background(work=None, given=(), takes=None, y_pieces=1, x_pieces=1):
        sends, keys, moving = [], [], []
        for _ in range(min(y_pieces, len(y_queue))):
            key, array = y_queue.pop(0)
            keys.append(key)
            sends.append((swap_chip, array))
        n = len(sends)
        for _ in range(min(x_pieces, len(x_queue))):
            moving.append(x_queue.pop(0))
        if pairs:
            sends += [(swap_group, array) for _, array in moving]

        def take(moved, made):
            if takes is not None:
                takes(made)
            landed.update(zip(keys, moved[:n]))
            for at, (key, array) in enumerate(moving):
                if pairs:
                    found[key] = (array, moved[n + at])
                else:
                    found[key] = (array,)

        return sends, work, given, take

    def total(key, *after):
        parts = found[key]
        if after:
            parts = lax.optimization_barrier((*parts, *after))[: len(parts)]
        if pairs:
            return parts[0].astype(f32) + parts[1].astype(f32)
        return lax.psum(parts[0], "dp").astype(f32)

    def queue(name, parts):
        y_queue.extend((f"{name}{n}", part) for n, part in enumerate(parts))

    feed_own = []

    def down_gradient(n):
        def work(u, v, c, d, got):
            return [weight_gradients([u, v], [c, d], [got], columns=(n, wide))]

        return work, (units, units_p, ck_own, cs_own, landed[f"d{n}"])

    def ready_for_group(*keys):
        return lambda made: x_queue.extend(zip(keys, made))

    queue("d", down_sent)

    def ffn_step(k):
        if k == 1:

            def work(f, h, g, p):
                return weight_gradient_pieces([f, h], [g, p], bf16, 4)

            return background(
                work, (fk_other, fs_other, gb, gb_p), lambda made: queue("f", made)
            )
        own, given = down_gradient(k - 2)
        if k == 3:
            return background(own, given, ready_for_group("d1"))

        def work(f, h, g, p, *given):
            return [*own(*given), *weight_gradient_pieces([f, h], [g, p], f32, 4)]

        def takes(made):
            x_queue.append(("d0", made[0]))
            feed_own.extend(made[1:])

        return background(work, (fk_own, fs_own, gb, gb_p, *given), takes)

    kept = []
    df_own, df_other = scatter(
        by_core(df_kept[0], df_sent[0]), by_core(df_kept[1], df_sent[1]), ffn_step
    )

    gain_fo = gains_other[1]
    w_o, w_p = df_own * ffn_gain, df_other * gain_fo
    along = jnp.sum(w_o * h_own, axis=1) + jnp.sum(w_p * h_other, axis=1)
    along = along + swap_core(along)
    factor = ffn_scale**3 * along[:, None] / D
    gh_own = cot_own.astype(f32) + ffn_scale * w_o - h_own * factor
    gh_other = cot_other.astype(f32) + ffn_scale * w_p - h_other * factor
    ffn_part = jnp.sum(df_own * h_own * ffn_scale, axis=0)
    ffn_part_o = jnp.sum(df_other * h_other * ffn_scale, axis=0)

    def back_step(k):
        given = (feed_own[k - 1], landed[f"f{k - 1}"])
        if k == 3:
            return background(lambda a, b: [rounded_sum(a, b)], given, ready_for_group("f2"))

        def work(u, v, w, a, b):
            return [*products([u, v], w), rounded_sum(a, b)]

        def takes(made):
            kept.extend(made[:2])
            x_queue.append((f"f{k - 1}", made[2]))

        return background(work, (units, units_p, w_down if k == 1 else wd_o, *given), takes)

    g_own, g_other = gather(gh_own.astype(bf16), gh_other.astype(bf16), back_step)
    un_own, un_other = by_core(*kept[:2]), by_core(*kept[2:])

    gg_recv = swap_core(
        (mm_nt(g_own, mine(w_out, 1 - core, hc, 0)) + mm_nt(g_other, mine(wo_o, 1 - core, hc, 0)))
        .astype(bf16)
    )
    gg_keep = mm_nt(g_own, mine(w_out, core, hc, 0)) + mm_nt(g_other, mine(wo_o, core, hc, 0))
    do, d_gate, group_part, seg, low = recurrence_back_local(
        gg_keep, gg_recv, rec, keep, recv, gain_row, local[1], local[4]
    )
    core_here = core.astype(jnp.int32).reshape(1)

    def gate_gradients(gate, left, grad, right):
        gate_p = swap_core(gate)
        sent = weight_gradients([left], [grad])
        return [gate_p, sent, head_gradients(core_here, right, gate, gate_p, 0, hc, bf16)]

    (peer,), (d_gate_p, out_sent, gate_sent), _ = step(
        [(swap_chip, low)], gate_gradients, (d_gate, gated, g_other, m_other)
    )

    def finish_back(seg, peer, gate, own, got):
        enter = recurrence_enter(place, seg, decay, peer, peer_decay, True)
        return [
            *recurrence_back_finish(keep, recv, bound, ids, local, states, do, enter, gate),
            rounded_sum(own, got),
        ]

    queue("o", [out_sent])
    queue("g", [gate_sent])
    out_run = paired(un_own[1], un_other[1])
    sends, _, _, take = background(y_pieces=2)
    moved, (dp_keep, bound_part, feed_last), _ = step(
        [(up, out_run), *sends], finish_back, (seg, peer, d_gate, feed_own[3], landed["f3"])
    )
    x_queue.append(("f3", feed_last))

    def out_sum(moved, at):
        a = moved[:, :width].astype(f32) + un_own[at].astype(f32)
        return a, moved[:, width:].astype(f32) + un_other[at].astype(f32)

    out_run = paired(*out_sum(moved[0], 2)).astype(bf16)
    take(moved[1:], [])

    dp_send = swap_core(dp_keep)
    sums_own, sums_other = mm_nt(dp_keep, wm_keep), mm_nt(dp_keep, wm_keep_o)
    sums_own, sums_other = sums_own + mm_nt(dp_send, wm_send), sums_other + mm_nt(dp_send, wm_send_o)
    own, other = blocks(sums_own.astype(bf16)), blocks(sums_other.astype(bf16))
    mix_part = jnp.sum(sums_own * m_own.astype(f32), axis=0) / mix_gain
    mix_part_o = jnp.sum(sums_other * m_other.astype(f32), axis=0) / gains_other[0]
    tail = jnp.concatenate([bound_part[0], group_part[0]])
    small = jnp.concatenate([mix_part, ffn_part, tail])
    small_o = jnp.concatenate([mix_part_o, ffn_part_o, tail])

    def heads_of(left, keep, send, first, parts, kind, plus=()):
        return head_gradients(core_here, left, keep, send, first, hc, kind, plus, parts)

    def first_gradients(keep, send, right, heads, grad, left, o_got, g_got):
        sent = [heads_of(right, keep, send, 0, 2, bf16), heads_of(right, keep, send, 2, 1, bf16)]
        out = weight_gradients([heads], [grad], [o_got])
        return [*sent, out, heads_of(left, keep, send, 3, 1, bf16, [g_got])]

    sends, _, _, take = background()
    dx_run = paired(own[1], other[1])
    moved, made, _ = step(
        [(up, dx_run), (up, out_run), (swap_chip, small_o), *sends],
        first_gradients,
        (dp_keep, dp_send, m_other, gated, g_own, m_own, landed["o0"], landed["g0"]),
    )
    small = small + moved[2]
    take(moved[3:], [])
    x_queue.extend(zip(("o0", "g0"), made[2:]))
    queue("qk", [made[0]])
    queue("v", [made[1]])

    def dx_sum(moved, at):
        a = moved[:, :width].astype(f32) + own[at].astype(f32)
        return a, moved[:, width:].astype(f32) + other[at].astype(f32)

    dx_run = paired(*dx_sum(moved[0], 2)).astype(bf16)
    out_run = paired(*out_sum(moved[1], 3)).astype(bf16)
    def own_gradients(keep, send, left):
        return [
            heads_of(left, keep, send, 0, 2, f32), heads_of(left, keep, send, 2, 1, f32)
        ]

    sends, work, given, take = background(
        own_gradients, (dp_keep, dp_send, m_own), x_pieces=2
    )
    if pairs:
        sends.append((swap_group, small))
    moved, made, _ = step([(up, dx_run), (up, out_run), *sends], work, given)
    small = small + moved[-1] if pairs else lax.psum(small, "dp")
    take(moved[2:-1] if pairs else moved[2:], made)
    of_parts = dict(zip(("qk0", "v0"), made))

    def reduced(key):
        x_queue.append((key, (of_parts[key] + landed[key].astype(f32)).astype(bf16)))

    reduced("qk0")
    dx_run = paired(*dx_sum(moved[0], 3)).astype(bf16)
    out_own, out_other = out_sum(moved[1], 0)
    out_own, out_other = (h_own + out_own).astype(bf16), (h_other + out_other).astype(bf16)
    edge = 2 * width
    bound_sum = small[edge : edge + hc]
    wide = jnp.concatenate([small[:edge], small[edge + hc :]])
    near = lambda a: lax.ppermute(a, "col", [(i, i ^ 1) for i in range(count)])
    far = lambda a: lax.ppermute(a, "col", [(i, i ^ 2) for i in range(count)])
    ffn_pieces = [found[f"f{n}"] if pairs else (total(f"f{n}"),) for n in range(4)]
    each = len(ffn_pieces[0])

    def whole_ffn(*given):
        return [
            halves_of_rows([given[n * each : (n + 1) * each] for n in range(4)], 2)
        ]

    sends, _, _, take = background(x_pieces=2)
    moved, (ffn_whole,), _ = step(
        [(up, dx_run), (near, wide), (swap_chip, out_other), *sends],
        whole_ffn,
        [array for found_piece in ffn_pieces for array in found_piece],
    )
    wide = wide + moved[1]
    out_other = moved[2]
    take(moved[3:], [])
    reduced("v0")
    dx_own, dx_other = dx_sum(moved[0], 0)

    w_o, w_p = dx_own * mix_gain, dx_other * gains_other[0]
    along = jnp.sum(w_o * x_own, axis=1) + jnp.sum(w_p * x_other, axis=1)
    along = along + swap_core(along)
    factor = mix_scale**3 * along[:, None] / D
    gt_own = gh_own + mix_scale * w_o - x_own * factor
    gt_other = gh_other + mix_scale * w_p - x_other * factor
    def two_parts(key):
        arrays = found[key] if pairs else (total(key),)
        return [[array[at : at + width] for array in arrays] for at in (0, width)]

    def one_part(key):
        return list(found[key]) if pairs else [total(key)]

    query, forget = two_parts("qk0")
    most = [query, forget, one_part("g0")]
    counts = [len(part) for part in most]

    def most_of(*given):
        parts = [given[sum(counts[:n]) : sum(counts[: n + 1])] for n in range(3)]
        return [stacked([parts[0], parts[1], (), parts[2]])]

    sends, _, _, take = background(x_pieces=2)
    moved, (mix_whole,), _ = step(
        [(swap_chip, gt_other.astype(bf16)), (far, wide), *sends],
        most_of,
        [array for part in most for array in part],
    )
    grad_other = moved[0].astype(f32)
    wide = wide + moved[1]
    take(moved[2:], [])
    mix_whole = filled(mix_whole, 2, one_part("v0"))
    turned = swap_core(jnp.concatenate([bound_sum, wide[edge:]]))
    grad_bound = joined(bound_sum, turned[:hc], core, 0)

    return (
        joined(out_own, out_other, y, 0),
        joined(gt_own, grad_other, y, 0),
        wide[:width],
        mix_whole,
        grad_bound,
        wide[edge:] + turned[hc:],
        total("o0"),
        wide[width:edge],
        ffn_whole,
        jnp.concatenate([total("d0"), total("d1")], 1),
    )


def solution(mesh):
    return jax.shard_map(
        shards,
        mesh=mesh,
        in_specs=(
            P(("dp", "col"), "row"),
            P("dp"),
            P("row"),
            P("row", None, "col"),
            P("col"),
            P(),
            P("col", "row"),
            P("row"),
            P("row", None, "col"),
            P("col", "row"),
            P(("dp", "col"), "row"),
        ),
        out_specs=(
            P(("dp", "col"), "row"),
            P(("dp", "col"), "row"),
            P("row"),
            P("row", None, "col"),
            P("col"),
            P(),
            P("col", "row"),
            P("row"),
            P("row", None, "col"),
            P("col", "row"),
        ),
        check_vma=False,
    )
```

```python
from functools import partial

import jax
import jax.numpy as jnp
from jax import lax
from jax.experimental import pallas as pl
from jax.experimental.pallas import tpu as pltpu
from jax.sharding import PartitionSpec as P

D = 2048
HD = 128
BLOCK = 64
norm_eps = 1e-06
bf16 = jnp.bfloat16
f32 = jnp.float32

CORE = [(0, 1), (1, 0), (2, 3), (3, 2)]
CHIP = [(0, 2), (2, 0), (1, 3), (3, 1)]


def swap_core(x):
    return lax.ppermute(x, "row", CORE)


def swap_chip(x):
    return lax.ppermute(x, "row", CHIP)


def tie(x, *others):
    return lax.optimization_barrier((x, *others))[0]


def mm(left, right):
    return lax.dot_general(left, right, (((1,), (0,)), ((), ())), preferred_element_type=f32)


def mm_nt(left, right):
    return lax.dot_general(left, right, (((1,), (1,)), ((), ())), preferred_element_type=f32)


def mm_tn(left, right):
    return lax.dot_general(left, right, (((0,), (0,)), ((), ())), preferred_element_type=f32)


def silu_slope(value, sigma):
    return sigma * (1.0 + value * (1.0 - sigma))


def split_mm(left, value):
    high = value.astype(bf16)
    low = (value - high.astype(f32)).astype(bf16)
    return mm(left, high) + mm(left, low)


def run_masks(i, idc_ref, idr_ref, prev_ref):
    s = slice(i * BLOCK, (i + 1) * BLOCK)
    idc = idc_ref[s, :]
    idr = idr_ref[0, :, s]
    prev = prev_ref[s, :]
    before = prev[0:1, :]
    last = idc[BLOCK - 1 : BLOCK, :]
    t = lax.broadcasted_iota(jnp.int32, (BLOCK, BLOCK), 0)
    u = lax.broadcasted_iota(jnp.int32, (BLOCK, BLOCK), 1)
    same = idc == idr
    heads = (idc == before).astype(f32)
    tails = (idc == last).astype(f32)
    through = (last == before).astype(f32)
    old = (idc == prev).astype(f32)
    return t, u, same, heads, tails, through, old


def run_decays(f_raw, lb, t, u):
    closed = jax.nn.sigmoid(-f_raw)
    keys = (1.0 - lb) * closed
    total = split_mm((t >= u).astype(bf16), jnp.log1p(-keys))
    middle = total[BLOCK // 2 - 1 : BLOCK // 2, :]
    final = total[BLOCK - 1 : BLOCK, :]
    return closed, keys, total, middle, final


def col(h, part=0, heads=1):
    start = (part * heads + h) * HD
    return slice(start, start + HD)


def local_kernel(
    keep_ref, recv_ref, lb_ref, idc_ref, idr_ref, prev_ref,
    inner_ref, qh_ref, kh_ref, vb_ref, decay_ref, seg_ref, low_ref, segd_ref,
):
    heads = lb_ref.shape[1] // HD
    state = [jnp.zeros((HD, HD), f32)] * heads
    passing = [jnp.ones((1, HD), f32)] * heads
    for i in range(keep_ref.shape[0] // BLOCK):
        s = slice(i * BLOCK, (i + 1) * BLOCK)
        t, u, same, head, tails, through, _ = run_masks(i, idc_ref, idr_ref, prev_ref)
        for h in range(heads):
            c = col(h)

            def raw(part):
                p = col(h, part, heads)
                return keep_ref[s, p] + recv_ref[s, p].astype(f32)

            q_raw = raw(0)
            vb = raw(2).astype(bf16)
            q = q_raw * jax.nn.sigmoid(q_raw)
            _, keys, total, middle, final = run_decays(raw(1), lb_ref[:, c], t, u)
            qt = (q * jnp.exp(total - middle)).astype(bf16)
            kt = (keys * jnp.exp(middle - total)).astype(bf16)
            scores = jnp.where(same & (t >= u), mm_nt(qt, kt), 0.0).astype(bf16)
            inner_ref[s, c] = mm(scores, vb)
            qh_ref[s, c] = (q * jnp.exp(total) * head).astype(bf16)
            kh = (keys * jnp.exp(final - total) * tails).astype(bf16)
            kh_ref[s, c] = kh
            vb_ref[s, c] = vb
            keep = jnp.exp(final) * through
            decay_ref[0, i : i + 1, c] = keep
            state[h] = keep * state[h] + mm_tn(vb, kh)
            passing[h] = passing[h] * keep
    for h in range(heads):
        seg_ref[0, h] = state[h]
        low_ref[0, h] = state[h].astype(bf16)
        segd_ref[0, :, col(h)] = passing[h]


def enter_kernel(reverse, place_ref, seg_ref, segd_ref, peer_ref, peerd_ref, out_ref):
    z, y = place_ref[0], place_ref[1]
    count, heads = seg_ref.shape[:2]
    peer_first = (y == 0) if reverse else (y == 1)
    state = [jnp.zeros((HD, HD), f32)] * heads
    for place in reversed(range(count)) if reverse else range(count):
        k = lax.rem((z ^ (z >> 1)) - (place ^ (place >> 1)) + count, count)
        for h in range(heads):
            add = peer_ref[k, h].astype(f32)
            scale = peerd_ref[k, :, col(h)]
            s = jnp.where(peer_first, scale, 1.0) * state[h] + jnp.where(peer_first, add, 0.0)
            out_ref[k, h] = s
            s = segd_ref[k, :, col(h)] * s + seg_ref[k, h]
            state[h] = jnp.where(peer_first, 1.0, scale) * s + jnp.where(peer_first, 0.0, add)


def finish_kernel(
    inner_ref, qh_ref, kh_ref, vb_ref, decay_ref, enter_ref, keep_ref, recv_ref, gain_ref,
    gated_ref, rec_ref, st_ref,
):
    heads = enter_ref.shape[1]
    state = [enter_ref[0, h] for h in range(heads)]
    for i in range(qh_ref.shape[0] // BLOCK):
        s = slice(i * BLOCK, (i + 1) * BLOCK)
        for h in range(heads):
            c = col(h)
            low = state[h].astype(bf16)
            st_ref[0, i, h] = low
            rec = inner_ref[s, c] + mm_nt(qh_ref[s, c], low)
            rec_ref[s, c] = rec
            scale = lax.rsqrt(jnp.mean(rec * rec, axis=1, keepdims=True) + norm_eps)
            g_raw = keep_ref[s, c] + recv_ref[s, c].astype(f32)
            gate = g_raw * jax.nn.sigmoid(g_raw)
            gated_ref[s, c] = (rec * scale * gain_ref[...] * gate).astype(bf16)
            state[h] = decay_ref[0, i : i + 1, c] * state[h] + mm_tn(vb_ref[s, c], kh_ref[s, c])


def back_local_kernel(
    kd, rd, rec_ref, keep_ref, recv_ref, gain_ref, qh_ref, decay_ref,
    do_ref, dg_ref, group_ref, seg_ref, low_ref,
):
    @pl.when(pl.program_id(0) == 0)
    def _():
        group_ref[...] = jnp.zeros_like(group_ref)

    gain = gain_ref[...]
    heads = seg_ref.shape[1]
    adjoint = [jnp.zeros((HD, HD), f32)] * heads
    group = jnp.zeros((1, HD), f32)
    for i in reversed(range(qh_ref.shape[0] // BLOCK)):
        s = slice(i * BLOCK, (i + 1) * BLOCK)
        for h in range(heads):
            c = col(h)
            grad = kd[s, c] + rd[s, c].astype(f32)
            rec = rec_ref[s, c]
            scale = lax.rsqrt(jnp.mean(rec * rec, axis=1, keepdims=True) + norm_eps)
            normed = rec * scale
            g_raw = keep_ref[s, c] + recv_ref[s, c].astype(f32)
            sigma = jax.nn.sigmoid(g_raw)
            act = g_raw * sigma
            both = grad * normed
            group = group + jnp.sum(both * act, axis=0, keepdims=True)
            dg_ref[s, c] = (both * gain * silu_slope(g_raw, sigma)).astype(bf16)
            dn = grad * gain * act
            do = (scale * (dn - normed * jnp.mean(dn * normed, axis=1, keepdims=True))).astype(bf16)
            do_ref[s, c] = do
            adjoint[h] = decay_ref[0, i : i + 1, c] * adjoint[h] + mm_tn(do, qh_ref[s, c])
    group_ref[...] += group
    for h in range(heads):
        seg_ref[0, h] = adjoint[h]
        low_ref[0, h] = adjoint[h].astype(bf16)


def back_finish_kernel(
    keep_ref, recv_ref, lb_ref, idc_ref, idr_ref, prev_ref,
    qh_ref, kh_ref, vb_ref, decay_ref, st_ref, do_ref, enter_ref, gate_ref,
    grad_ref, bound_ref,
):
    @pl.when(pl.program_id(0) == 0)
    def _():
        bound_ref[...] = jnp.zeros_like(bound_ref)

    heads = enter_ref.shape[1]
    grad_ref[:, 3 * gate_ref.shape[1] :] = gate_ref[...]
    adjoint = [enter_ref[0, h] for h in range(heads)]
    bound = [jnp.zeros((1, HD), f32)] * heads
    for i in reversed(range(keep_ref.shape[0] // BLOCK)):
        s = slice(i * BLOCK, (i + 1) * BLOCK)
        t, u, same, head, tails, through, old = run_masks(i, idc_ref, idr_ref, prev_ref)
        causal = same & (t >= u)
        later = (same & (u >= t)).astype(bf16)
        for h in range(heads):
            c = col(h)

            def raw(part):
                p = col(h, part, heads)
                return keep_ref[s, p] + recv_ref[s, p].astype(f32)

            q_raw = raw(0)
            sigma = jax.nn.sigmoid(q_raw)
            q = q_raw * sigma
            closed, keys, total, middle, final = run_decays(raw(1), lb_ref[:, c], t, u)
            out = jnp.exp(total - middle)
            back = jnp.exp(middle - total)
            qt = (q * out).astype(bf16)
            kt = (keys * back).astype(bf16)
            scores = jnp.where(causal, mm_nt(qt, kt), 0.0).astype(bf16)
            vb = vb_ref[s, c]
            kh = kh_ref[s, c]
            do = do_ref[s, c]
            st = st_ref[0, i, h]
            low = adjoint[h].astype(bf16)
            keep = decay_ref[0, i : i + 1, c]
            ds = jnp.where(causal, mm_nt(do, vb), 0.0).astype(bf16)
            dq = mm(ds, kt) * out + mm(do, st) * (jnp.exp(total) * head)
            dkh = mm(vb, low)
            dk = mm_tn(ds, qt) * back + dkh * (jnp.exp(final - total) * tails)
            grad_ref[s, col(h, 2, heads)] = (mm_tn(scores, do) + mm_nt(kh, low)).astype(bf16)
            ends = keep * jnp.sum(adjoint[h] * st.astype(f32), axis=0, keepdims=True) + jnp.sum(
                kh.astype(f32) * dkh, axis=0, keepdims=True
            )
            dlog = split_mm(later, q * dq - keys * dk) + tails * ends
            key_total = dk - old * dlog / (1.0 - keys)
            bound[h] = bound[h] - jnp.sum(key_total * closed, axis=0, keepdims=True)
            grad_ref[s, col(h, 1, heads)] = (-key_total * keys * (1.0 - closed)).astype(bf16)
            grad_ref[s, col(h, 0, heads)] = (dq * silu_slope(q_raw, sigma)).astype(bf16)
            adjoint[h] = keep * adjoint[h] + mm_tn(do, qh_ref[s, c])
    for h in range(heads):
        bound_ref[:, col(h)] += bound[h]


def shape(dims, kind):
    return jax.ShapeDtypeStruct(dims, kind)


COST = pl.CostEstimate(flops=0, bytes_accessed=0, transcendentals=0)
SMEM = pl.BlockSpec(memory_space=pltpu.SMEM)
VMEM = pl.BlockSpec(memory_space=pltpu.VMEM)


def run_block(*dims, at=0):
    return pl.BlockSpec(dims, lambda j: (j, *([0] * (len(dims) - 2)), at))


def whole(*dims):
    return pl.BlockSpec(dims, lambda j: (0,) * len(dims))


def recurrence_local(keep, recv, bound, ids):
    runs, _, run = ids[1].shape
    width = bound.shape[1]
    heads = width // HD
    chunks = run // BLOCK
    tokens = runs * run
    return pl.pallas_call(
        local_kernel,
        grid=(runs,),
        in_specs=[
            run_block(run, 4 * width), run_block(run, 4 * width), whole(1, width),
            run_block(run, 1), run_block(1, 1, run), run_block(run, 1),
        ],
        out_specs=[run_block(run, width)] * 4
        + [run_block(1, chunks, width)]
        + [run_block(1, heads, HD, HD)] * 2
        + [run_block(1, 1, width)],
        out_shape=[
            shape((tokens, width), f32),
            shape((tokens, width), bf16),
            shape((tokens, width), bf16),
            shape((tokens, width), bf16),
            shape((runs, chunks, width), f32),
            shape((runs, heads, HD, HD), f32),
            shape((runs, heads, HD, HD), bf16),
            shape((runs, 1, width), f32),
        ],
        cost_estimate=COST,
        name="recurrence_local",
    )(keep, recv, bound, *ids)


def recurrence_enter(place, seg, segd, peer, peerd, reverse):
    return pl.pallas_call(
        partial(enter_kernel, reverse),
        in_specs=[SMEM] + [VMEM] * 4,
        out_specs=VMEM,
        out_shape=shape(seg.shape, f32),
        cost_estimate=COST,
        name="recurrence_enter_back" if reverse else "recurrence_enter",
    )(place, seg, segd, peer, peerd)


def recurrence_finish(local, enter, keep, recv, gain):
    inner, qh, kh, vb, decay = local
    runs, chunks, width = decay.shape
    heads = width // HD
    run = chunks * BLOCK
    tokens = runs * run
    cols = run_block(run, width)
    gate = run_block(run, width, at=3)
    return pl.pallas_call(
        finish_kernel,
        grid=(runs,),
        in_specs=[
            cols, cols, cols, cols, run_block(1, chunks, width), run_block(1, heads, HD, HD),
            gate, gate, whole(1, HD),
        ],
        out_specs=[cols, cols, run_block(1, chunks, heads, HD, HD)],
        out_shape=[
            shape((tokens, width), bf16),
            shape((tokens, width), f32),
            shape((runs, chunks, heads, HD, HD), bf16),
        ],
        cost_estimate=COST,
        name="recurrence_finish",
    )(inner, qh, kh, vb, decay, enter, keep, recv, gain)


def recurrence_back_local(kd, rd, rec, keep, recv, gain, qh, decay):
    runs, chunks, width = decay.shape
    heads = width // HD
    run = chunks * BLOCK
    tokens = runs * run
    cols = run_block(run, width)
    gate = run_block(run, width, at=3)
    return pl.pallas_call(
        back_local_kernel,
        grid=(runs,),
        in_specs=[
            cols, cols, cols, gate, gate, whole(1, HD), cols, run_block(1, chunks, width),
        ],
        out_specs=[cols, cols, whole(1, HD)] + [run_block(1, heads, HD, HD)] * 2,
        out_shape=[
            shape((tokens, width), bf16),
            shape((tokens, width), bf16),
            shape((1, HD), f32),
            shape((runs, heads, HD, HD), f32),
            shape((runs, heads, HD, HD), bf16),
        ],
        cost_estimate=COST,
        name="recurrence_back_local",
    )(kd, rd, rec, keep, recv, gain, qh, decay)


def recurrence_back_finish(keep, recv, bound, ids, local, states, do, enter, gate):
    _, qh, kh, vb, decay = local
    runs, chunks, width = decay.shape
    heads = width // HD
    run = chunks * BLOCK
    tokens = runs * run
    cols = run_block(run, width)
    return pl.pallas_call(
        back_finish_kernel,
        grid=(runs,),
        in_specs=[
            run_block(run, 4 * width), run_block(run, 4 * width), whole(1, width),
            run_block(run, 1), run_block(1, 1, run), run_block(run, 1),
            cols, cols, cols, run_block(1, chunks, width),
            run_block(1, chunks, heads, HD, HD), cols, run_block(1, heads, HD, HD), cols,
        ],
        out_specs=[run_block(run, 4 * width), whole(1, width)],
        out_shape=[shape((tokens, 4 * width), bf16), shape((1, width), f32)],
        cost_estimate=COST,
        name="recurrence_back_finish",
    )(keep, recv, bound, *ids, qh, kh, vb, decay, states, do, enter, gate)


def weight_kernel(pairs, *refs):
    lefts, rights = refs[:pairs], refs[pairs : 2 * pairs]
    *plus, out = refs[2 * pairs :]
    total = sum(mm_tn(left[...], right[...]) for left, right in zip(lefts, rights))
    out[...] = (total + sum(part[...].astype(f32) for part in plus)).astype(out.dtype)


def weight_gradients(lefts, rights, plus=(), rows=None, columns=None, tile=256):
    at, tall = rows or (0, lefts[0].shape[1])
    first, wide = columns or (0, rights[0].shape[1])
    tiles = wide // tile
    out = pl.BlockSpec((tall, tile), lambda j: (0, j))
    return pl.pallas_call(
        partial(weight_kernel, len(lefts)),
        grid=(tiles,),
        in_specs=[pl.BlockSpec((left.shape[0], tall), lambda j: (0, at)) for left in lefts]
        + [pl.BlockSpec((r.shape[0], tile), lambda j: (0, first * tiles + j)) for r in rights]
        + [out] * len(plus),
        out_specs=out,
        out_shape=shape((tall, wide), bf16),
        cost_estimate=COST,
        name="weight_gradients",
    )(*lefts, *rights, *plus)


def pieces_kernel(pairs, *refs):
    lefts, rights, outs = refs[:pairs], refs[pairs : 2 * pairs], refs[2 * pairs :]
    total = sum(mm_tn(left[...], right[...]) for left, right in zip(lefts, rights))
    each = outs[0].shape[0]
    for n, out in enumerate(outs):
        out[...] = total[n * each : (n + 1) * each].astype(out.dtype)


def weight_gradient_pieces(lefts, rights, kind, pieces, tile=256):
    tall, wide = lefts[0].shape[1] // pieces, rights[0].shape[1]
    return pl.pallas_call(
        partial(pieces_kernel, len(lefts)),
        grid=(wide // tile,),
        in_specs=[whole(*left.shape) for left in lefts]
        + [pl.BlockSpec((right.shape[0], tile), lambda j: (0, j)) for right in rights],
        out_specs=[pl.BlockSpec((tall, tile), lambda j: (0, j))] * pieces,
        out_shape=[shape((tall, wide), kind)] * pieces,
        cost_estimate=COST,
        name="weight_gradient_pieces",
    )(*lefts, *rights)


def sum_kernel(own_ref, got_ref, out_ref):
    out_ref[...] = (own_ref[...] + got_ref[...].astype(f32)).astype(bf16)


def rounded_sum(own, got):
    return pl.pallas_call(
        sum_kernel,
        in_specs=[VMEM] * 2,
        out_specs=VMEM,
        out_shape=shape(own.shape, bf16),
        cost_estimate=COST,
        name="rounded_sum",
    )(own, got)


def halves_kernel(pieces, *refs):
    *given, out_ref = refs
    each = len(given) // pieces
    wide = out_ref.shape[2]
    rows = out_ref.shape[0]
    for n in range(pieces):

        @pl.when(pl.program_id(0) == n)
        def _():
            at = pl.ds(pl.multiple_of(pl.program_id(1) * rows, rows), rows)
            for part in range(out_ref.shape[1]):
                cols = slice(part * wide, (part + 1) * wide)
                value = sum(ref[at, cols].astype(f32) for ref in given[n * each : (n + 1) * each])
                out_ref[:, part, :] = value


def halves_of_rows(pieces, parts, rows=32):
    tall, wide = pieces[0][0].shape
    steps = tall // rows
    given = [array for piece in pieces for array in piece]
    return pl.pallas_call(
        partial(halves_kernel, len(pieces)),
        grid=(len(pieces), steps),
        in_specs=[pl.BlockSpec(a.shape, lambda n, j: (0, 0)) for a in given],
        out_specs=pl.BlockSpec((rows, parts, wide // parts), lambda n, j: (n * steps + j, 0, 0)),
        out_shape=shape((len(pieces) * tall, parts, wide // parts), f32),
        cost_estimate=COST,
        compiler_params=pltpu.CompilerParams(vmem_limit_bytes=40 * 2**20),
        name="halves_of_rows",
    )(*given)


def stack_kernel(counts, *refs):
    *given, out_ref = refs
    for part, count in enumerate(counts):
        refs_here, given = given[:count], given[count:]
        if count:
            out_ref[:, part, :] = sum(ref[...].astype(f32) for ref in refs_here)
        else:
            out_ref[:, part, :] = jnp.zeros((out_ref.shape[0], out_ref.shape[2]), f32)


def stacked(parts, rows=128):
    tall, wide = parts[0][0].shape
    given = [array for part in parts for array in part]
    return pl.pallas_call(
        partial(stack_kernel, [len(part) for part in parts]),
        grid=(tall // rows,),
        in_specs=[pl.BlockSpec((rows, wide), lambda j: (j, 0))] * len(given),
        out_specs=pl.BlockSpec((rows, len(parts), wide), lambda j: (j, 0, 0)),
        out_shape=shape((tall, len(parts), wide), f32),
        cost_estimate=COST,
        name="stacked",
    )(*given)


def product_kernel(right_ref, *refs):
    lefts, outs = refs[: len(refs) // 2], refs[len(refs) // 2 :]
    for left, out in zip(lefts, outs):
        out[...] = mm(left[...], right_ref[...]).astype(out.dtype)


def products(lefts, right, tile=256):
    wide = right.shape[1]
    return pl.pallas_call(
        product_kernel,
        grid=(wide // tile,),
        in_specs=[pl.BlockSpec((right.shape[0], tile), lambda j: (0, j))]
        + [whole(*left.shape) for left in lefts],
        out_specs=[pl.BlockSpec((left.shape[0], tile), lambda j: (0, j)) for left in lefts],
        out_shape=[shape((left.shape[0], wide), bf16) for left in lefts],
        cost_estimate=COST,
        name="products",
    )(right, *lefts)


def heads_kernel(first, half, core_ref, left_ref, own_ref, peer_ref, *refs):
    *plus, out_ref = refs
    core = core_ref[0]
    tall = left_ref.shape[1]
    for part in range(out_ref.shape[0] // tall):
        rows = slice(part * tall, (part + 1) * tall)
        given = slice((first + part) * half, (first + part + 1) * half)
        for right_ref, at in ((own_ref, core), (peer_ref, 1 - core)):
            cols = pl.ds(pl.multiple_of(at * half, half), half)
            total = mm_tn(left_ref[...], right_ref[:, given])
            for more in plus:
                total = total + more[rows, cols].astype(f32)
            out_ref[rows, cols] = total.astype(out_ref.dtype)


def head_gradients(core, left, own, peer, first, half, kind, plus=(), parts=1):
    return pl.pallas_call(
        partial(heads_kernel, first, half),
        in_specs=[SMEM] + [VMEM] * (3 + len(plus)),
        out_specs=VMEM,
        out_shape=shape((parts * left.shape[1], 2 * half), kind),
        cost_estimate=COST,
        name="head_gradients",
    )(core, left, own, peer, *plus)


def fill_kernel(part, *refs):
    base_ref, *given, out_ref = refs
    out_ref[...] = base_ref[...]
    out_ref[:, part, :] = sum(ref[...].astype(f32) for ref in given)


def filled(base, part, given, rows=128):
    tall, parts, wide = base.shape
    block = pl.BlockSpec((rows, parts, wide), lambda j: (j, 0, 0))
    return pl.pallas_call(
        partial(fill_kernel, part),
        grid=(tall // rows,),
        in_specs=[block] + [pl.BlockSpec((rows, wide), lambda j: (j, 0))] * len(given),
        out_specs=block,
        out_shape=shape(base.shape, f32),
        input_output_aliases={0: 0},
        cost_estimate=COST,
        name="filled",
    )(base, *given)


def swap_group(x):
    return lax.ppermute(x, "dp", [(0, 1), (1, 0)])


def folded(place):
    return place ^ (place >> 1)


def up(x):
    count = lax.axis_size("col")
    return lax.ppermute(x, "col", [(folded(n), folded((n + 1) % count)) for n in range(count)])


def paired(own, other):
    return jnp.concatenate([own, other], 1)


def step(sends, work=None, given=(), join=()):
    n = len(sends)
    arrays = lax.optimization_barrier((*(array for _, array in sends), *given))
    moved = [mover(array) for (mover, _), array in zip(sends, arrays)]
    made = tuple(work(*arrays[n:])) if work else ()
    done = lax.optimization_barrier((*moved, *made, *join))
    return list(done[:n]), list(done[n : n + len(made)]), list(done[n + len(made) :])


def ordered(runs):
    width = runs[0].shape[1] // 2
    return (
        jnp.concatenate([run[:, :width] for run in runs], 0),
        jnp.concatenate([run[:, width:] for run in runs], 0),
    )


def cut(array, count):
    each = -(-array.shape[0] // count)
    each = -(-each // 16) * 16
    return [array[at : at + each] for at in range(0, array.shape[0], each)]


def shards(
    tokens,
    segments,
    mix_gain,
    w_mix,
    lower_bound,
    group_gain,
    w_out,
    ffn_gain,
    w_ffn_in,
    w_down,
    cotangent,
):
    row = lax.axis_index("row")
    core = row % 2
    y = row // 2
    z = lax.axis_index("col")
    count = lax.axis_size("col")
    pairs = lax.axis_size("dp") == 2
    half = tokens.shape[0] // 2
    width = tokens.shape[1]
    hc = w_mix.shape[2] // 2
    units_col = w_down.shape[0]
    here = count * half
    hb = here // 2

    def mine(x, at, size, axis):
        return lax.dynamic_slice_in_dim(x, at * size, size, axis)

    def rows(x, at):
        return mine(x, at, hb, 0)

    def joined(first_if_zero, second_if_zero, flag, axis):
        return jnp.where(
            flag == 0,
            jnp.concatenate([first_if_zero, second_if_zero], axis),
            jnp.concatenate([second_if_zero, first_if_zero], axis),
        )

    def blocks(array):
        return [array[k * half : (k + 1) * half] for k in range(count)]

    tok_own = mine(tokens, y, half, 0)
    (tok_other,), _, _ = step([(swap_chip, mine(tokens, 1 - y, half, 0))])
    cot_own, cot_send = mine(cotangent, y, half, 0), mine(cotangent, 1 - y, half, 0)
    group = lax.axis_index("dp")

    def half_of(array):
        return mine(array, group, array.shape[0] // 2, 0) if pairs else array

    def over_group(array):
        return [(swap_group, array)] if pairs else []

    def assembled(parts, parts_x):
        if not pairs:
            return jnp.concatenate(parts, 0)
        rows_half = sum(part.shape[0] for part in parts)
        both = jnp.zeros((2 * rows_half, *parts[0].shape[1:]), parts[0].dtype)
        for which, given in ((group, parts), (1 - group, parts_x)):
            at = which * rows_half
            for part in given:
                both = lax.dynamic_update_slice(both, part, (at, *[0] * (part.ndim - 1)))
                at += part.shape[0]
        return both

    wm_parts = cut(half_of(w_mix), 2)
    first = swap_chip(tie(wm_parts[0], tok_other))
    gains_other = swap_chip(tie(jnp.stack([mix_gain, ffn_gain]), tok_other))
    x_own, x_other = tok_own.astype(f32), tok_other.astype(f32)
    squares = jnp.sum(x_own * x_own, axis=1) + jnp.sum(x_other * x_other, axis=1)
    squares = squares + swap_core(squares)
    mix_scale = lax.rsqrt(squares / D + norm_eps)[:, None]
    m = [
        paired(x_own * mix_scale * mix_gain, x_other * mix_scale * gains_other[0]).astype(bf16)
    ]
    (a, cot_other), _, (first,) = step([(up, m[0]), (swap_chip, cot_send)], join=[first])
    m.append(a)
    (a, second, *first_x), _, _ = step(
        [(up, m[1]), (swap_chip, wm_parts[1]), *over_group(first)]
    )
    m.append(a)
    wf = w_ffn_in.reshape(width, 2 * units_col)
    pieces = [half_of(w_down), *cut(half_of(wf), 3)]
    moved, _, _ = step(
        [(lambda v: v, piece) for piece in pieces]
        + [(up, m[2]), (swap_chip, w_out), *over_group(second)]
    )
    pieces, (a, wo_o, *second_x) = moved[: len(pieces)], moved[len(pieces) :]
    m.append(a)
    c = [paired(cot_own, cot_other)]
    wm_other = assembled([first, second], [*first_x, *second_x])
    m_own, m_other = ordered(m)

    def columns(w, at):
        return mine(w, at, hc, 2).reshape(width, 4 * hc)

    wm_keep, wm_send = columns(w_mix, core), columns(w_mix, 1 - core)
    wm_keep_o, wm_send_o = columns(wm_other, core), columns(wm_other, 1 - core)

    names = segments.astype(f32)
    before = jnp.concatenate([jnp.full((1,), -1.0, f32), names[:-1]])

    def runs_of(array):
        array = lax.dynamic_index_in_dim(array.reshape(count, 2, half), y, 1, keepdims=False)
        places = [folded((folded(z) - k + count) % count) for k in range(count)]
        return jnp.stack(
            [lax.dynamic_index_in_dim(array, at, 0, keepdims=False) for at in places]
        )

    names, before = runs_of(names), runs_of(before)
    ids = (names.reshape(here, 1), names.reshape(count, 1, half), before.reshape(here, 1))
    bound = mine(lower_bound, core, hc, 0).reshape(1, hc)
    gain_row = group_gain.reshape(1, HD)
    place = jnp.stack([z, y]).astype(jnp.int32)

    weights, weights_x = [], []

    def weights_step(k=0):
        sends = [(swap_chip, pieces[len(weights)])] if len(weights) < len(pieces) else []
        n = len(sends)
        if pairs and len(weights_x) < len(weights):
            sends.append((swap_group, weights[len(weights_x)]))

        def take(moved, made):
            weights.extend(moved[:n])
            weights_x.extend(moved[n:])

        return sends, None, (), take

    send = (mm(m_own, wm_send) + mm(m_other, wm_send_o)).astype(bf16)
    recv = swap_core(send)
    keep = mm(m_own, wm_keep) + mm(m_other, wm_keep_o)
    sends, _, _, take = weights_step()
    (a, *moved), local, _ = step(
        [(up, c[-1]), *sends],
        lambda keep, recv: recurrence_local(keep, recv, bound, ids),
        (keep, recv),
    )
    take(moved, [])
    c.append(a)
    *local, seg, low, decay = local
    late = [swap_group(tie(weights[0], low))] if pairs else []
    (a, peer, peer_decay), _, _ = step([(up, c[-1]), (swap_chip, low), (swap_chip, decay)])
    c.append(a)

    def finish(seg, decay, peer, peer_decay):
        enter = recurrence_enter(place, seg, decay, peer, peer_decay, False)
        return recurrence_finish(local, enter, keep, recv, gain_row)

    (a, got), (gated, rec, states), late = step(
        [(up, c[-1]), (swap_chip, pieces[1])],
        finish,
        (seg, decay, peer, peer_decay),
        join=late,
    )
    c.append(a)
    weights.append(got)
    weights_x.extend(late)
    c_own, c_other = ordered(c)
    gated = joined(gated, swap_core(gated), core, 1)

    def scatter(own, other, beside):
        sent = paired(own[1], other[1]).astype(bf16)
        for k in range(1, count):
            sends, work, given, take = beside(k)
            moved, made, _ = step([(up, sent), *sends], work, given)
            at = (k + 1) % count
            a = moved[0][:, :width].astype(f32) + own[at].astype(f32)
            b = moved[0][:, width:].astype(f32) + other[at].astype(f32)
            sent = paired(a, b).astype(bf16)
            take(moved[1:], made)
        return a, b

    def gather(own, other, beside):
        runs = [paired(own, other)]
        for k in range(1, count):
            sends, work, given, take = beside(k)
            moved, made, _ = step([(up, runs[-1]), *sends], work, given)
            runs.append(moved[0])
            take(moved[1:], made)
        return ordered(runs)

    h_own, h_other = scatter(
        blocks(mm(gated, w_out).astype(bf16)), blocks(mm(gated, wo_o).astype(bf16)), weights_step
    )
    h_own, h_other = x_own + h_own, x_other + h_other

    squares = jnp.sum(h_own * h_own, axis=1) + jnp.sum(h_other * h_other, axis=1)
    squares = squares + swap_core(squares)
    ffn_scale = lax.rsqrt(squares / D + norm_eps)[:, None]
    n_own = (h_own * ffn_scale * ffn_gain).astype(bf16)
    n_other = (h_other * ffn_scale * gains_other[1]).astype(bf16)

    wd_o = assembled(weights[:1], weights_x[:1])
    gu_recv = swap_core(
        (mm_nt(rows(c_own, 1 - core), w_down) + mm_nt(rows(c_other, 1 - core), wd_o)).astype(bf16)
    )
    gu = mm_nt(rows(c_own, core), w_down) + mm_nt(rows(c_other, core), wd_o) + gu_recv.astype(f32)
    f_own, f_other = gather(n_own, n_other, lambda k: ([], None, (), lambda moved, made: None))
    wf_o = assembled(weights[1:], weights_x[1:])
    f_own, gu = lax.optimization_barrier((f_own, gu))
    fk_own, fs_own = rows(f_own, core), rows(f_own, 1 - core)
    fk_other, fs_other = rows(f_other, core), rows(f_other, 1 - core)
    b_recv = swap_core((mm(fs_own, wf) + mm(fs_other, wf_o)).astype(bf16))
    both = mm(fk_own, wf) + mm(fk_other, wf_o) + b_recv.astype(f32)
    gate, up_part = both[:, :units_col], both[:, units_col:]
    sigma = jax.nn.sigmoid(gate)
    act = gate * sigma
    units = (act * up_part).astype(bf16)
    gb = jnp.concatenate(
        [(gu * up_part * silu_slope(gate, sigma)).astype(bf16), (gu * act).astype(bf16)], 1
    )
    gb_p = swap_core(gb)
    units_p = swap_core(tie(units, gb))
    df_kept = [mm_nt(gb, wf).astype(bf16), mm_nt(gb, wf_o).astype(bf16)]
    df_sent = [mm_nt(gb_p, wf).astype(bf16), mm_nt(gb_p, wf_o).astype(bf16)]
    ck_own, cs_own = rows(c_own, core), rows(c_own, 1 - core)
    ck_other, cs_other = rows(c_other, core), rows(c_other, 1 - core)
    wide = width // 2
    down_sent = [
        (mm_tn(units, ck_other[:, at : at + wide]) + mm_tn(units_p, cs_other[:, at : at + wide]))
        .astype(bf16)
        for at in (0, wide)
    ]

    def by_core(kept, sent):
        each = count // 2
        parts = []
        for k in range(count):
            s = slice(k % each * half, (k % each + 1) * half)
            parts.append(jnp.where(core == k // each, kept[s], sent[s]))
        return parts

    y_queue, x_queue, landed, found = [], [], {}, {}

    def background(work=None, given=(), takes=None, y_pieces=1, x_pieces=1):
        sends, keys, moving = [], [], []
        for _ in range(min(y_pieces, len(y_queue))):
            key, array = y_queue.pop(0)
            keys.append(key)
            sends.append((swap_chip, array))
        n = len(sends)
        for _ in range(min(x_pieces, len(x_queue))):
            moving.append(x_queue.pop(0))
        if pairs:
            sends += [(swap_group, array) for _, array in moving]

        def take(moved, made):
            if takes is not None:
                takes(made)
            landed.update(zip(keys, moved[:n]))
            for at, (key, array) in enumerate(moving):
                if pairs:
                    found[key] = (array, moved[n + at])
                else:
                    found[key] = (array,)

        return sends, work, given, take

    def total(key, *after):
        parts = found[key]
        if after:
            parts = lax.optimization_barrier((*parts, *after))[: len(parts)]
        if pairs:
            return parts[0].astype(f32) + parts[1].astype(f32)
        return lax.psum(parts[0], "dp").astype(f32)

    def queue(name, parts):
        y_queue.extend((f"{name}{n}", part) for n, part in enumerate(parts))

    feed_own = []

    def down_gradient(n):
        def work(u, v, c, d, got):
            return [weight_gradients([u, v], [c, d], [got], columns=(n, wide))]

        return work, (units, units_p, ck_own, cs_own, landed[f"d{n}"])

    def ready_for_group(*keys):
        return lambda made: x_queue.extend(zip(keys, made))

    queue("d", down_sent)

    def ffn_step(k):
        if k == 1:

            def work(f, h, g, p):
                return weight_gradient_pieces([f, h], [g, p], bf16, 4)

            return background(
                work, (fk_other, fs_other, gb, gb_p), lambda made: queue("f", made)
            )
        own, given = down_gradient(k - 2)
        if k == 3:
            return background(own, given, ready_for_group("d1"))

        def work(f, h, g, p, *given):
            return [*own(*given), *weight_gradient_pieces([f, h], [g, p], f32, 4)]

        def takes(made):
            x_queue.append(("d0", made[0]))
            feed_own.extend(made[1:])

        return background(work, (fk_own, fs_own, gb, gb_p, *given), takes)

    kept = []
    df_own, df_other = scatter(
        by_core(df_kept[0], df_sent[0]), by_core(df_kept[1], df_sent[1]), ffn_step
    )

    gain_fo = gains_other[1]
    w_o, w_p = df_own * ffn_gain, df_other * gain_fo
    along = jnp.sum(w_o * h_own, axis=1) + jnp.sum(w_p * h_other, axis=1)
    along = along + swap_core(along)
    factor = ffn_scale**3 * along[:, None] / D
    gh_own = cot_own.astype(f32) + ffn_scale * w_o - h_own * factor
    gh_other = cot_other.astype(f32) + ffn_scale * w_p - h_other * factor
    ffn_part = jnp.sum(df_own * h_own * ffn_scale, axis=0)
    ffn_part_o = jnp.sum(df_other * h_other * ffn_scale, axis=0)

    def back_step(k):
        given = (feed_own[k - 1], landed[f"f{k - 1}"])
        if k == 3:
            return background(lambda a, b: [rounded_sum(a, b)], given, ready_for_group("f2"))

        def work(u, v, w, a, b):
            return [*products([u, v], w), rounded_sum(a, b)]

        def takes(made):
            kept.extend(made[:2])
            x_queue.append((f"f{k - 1}", made[2]))

        return background(work, (units, units_p, w_down if k == 1 else wd_o, *given), takes)

    g_own, g_other = gather(gh_own.astype(bf16), gh_other.astype(bf16), back_step)
    un_own, un_other = by_core(*kept[:2]), by_core(*kept[2:])

    gg_recv = swap_core(
        (mm_nt(g_own, mine(w_out, 1 - core, hc, 0)) + mm_nt(g_other, mine(wo_o, 1 - core, hc, 0)))
        .astype(bf16)
    )
    gg_keep = mm_nt(g_own, mine(w_out, core, hc, 0)) + mm_nt(g_other, mine(wo_o, core, hc, 0))
    do, d_gate, group_part, seg, low = recurrence_back_local(
        gg_keep, gg_recv, rec, keep, recv, gain_row, local[1], local[4]
    )
    core_here = core.astype(jnp.int32).reshape(1)

    def gate_gradients(gate, left, grad, right):
        gate_p = swap_core(gate)
        sent = weight_gradients([left], [grad])
        return [gate_p, sent, head_gradients(core_here, right, gate, gate_p, 0, hc, bf16)]

    (peer,), (d_gate_p, out_sent, gate_sent), _ = step(
        [(swap_chip, low)], gate_gradients, (d_gate, gated, g_other, m_other)
    )

    def finish_back(seg, peer, gate, own, got):
        enter = recurrence_enter(place, seg, decay, peer, peer_decay, True)
        return [
            *recurrence_back_finish(keep, recv, bound, ids, local, states, do, enter, gate),
            rounded_sum(own, got),
        ]

    queue("o", [out_sent])
    queue("g", [gate_sent])
    out_run = paired(un_own[1], un_other[1])
    sends, _, _, take = background(y_pieces=2)
    moved, (dp_keep, bound_part, feed_last), _ = step(
        [(up, out_run), *sends], finish_back, (seg, peer, d_gate, feed_own[3], landed["f3"])
    )
    x_queue.append(("f3", feed_last))

    def out_sum(moved, at):
        a = moved[:, :width].astype(f32) + un_own[at].astype(f32)
        return a, moved[:, width:].astype(f32) + un_other[at].astype(f32)

    out_run = paired(*out_sum(moved[0], 2)).astype(bf16)
    take(moved[1:], [])

    dp_send = swap_core(dp_keep)
    sums_own, sums_other = mm_nt(dp_keep, wm_keep), mm_nt(dp_keep, wm_keep_o)
    sums_own, sums_other = sums_own + mm_nt(dp_send, wm_send), sums_other + mm_nt(dp_send, wm_send_o)
    own, other = blocks(sums_own.astype(bf16)), blocks(sums_other.astype(bf16))
    mix_part = jnp.sum(sums_own * m_own.astype(f32), axis=0) / mix_gain
    mix_part_o = jnp.sum(sums_other * m_other.astype(f32), axis=0) / gains_other[0]
    tail = jnp.concatenate([bound_part[0], group_part[0]])
    small = jnp.concatenate([mix_part, ffn_part, tail])
    small_o = jnp.concatenate([mix_part_o, ffn_part_o, tail])

    def heads_of(left, keep, send, first, parts, kind, plus=()):
        return head_gradients(core_here, left, keep, send, first, hc, kind, plus, parts)

    def first_gradients(keep, send, right, heads, grad, left, o_got, g_got):
        sent = [heads_of(right, keep, send, 0, 2, bf16), heads_of(right, keep, send, 2, 1, bf16)]
        out = weight_gradients([heads], [grad], [o_got])
        return [*sent, out, heads_of(left, keep, send, 3, 1, bf16, [g_got])]

    sends, _, _, take = background()
    dx_run = paired(own[1], other[1])
    moved, made, _ = step(
        [(up, dx_run), (up, out_run), (swap_chip, small_o), *sends],
        first_gradients,
        (dp_keep, dp_send, m_other, gated, g_own, m_own, landed["o0"], landed["g0"]),
    )
    small = small + moved[2]
    take(moved[3:], [])
    x_queue.extend(zip(("o0", "g0"), made[2:]))
    queue("qk", [made[0]])
    queue("v", [made[1]])

    def dx_sum(moved, at):
        a = moved[:, :width].astype(f32) + own[at].astype(f32)
        return a, moved[:, width:].astype(f32) + other[at].astype(f32)

    dx_run = paired(*dx_sum(moved[0], 2)).astype(bf16)
    out_run = paired(*out_sum(moved[1], 3)).astype(bf16)
    def own_gradients(keep, send, left):
        return [
            heads_of(left, keep, send, 0, 2, f32), heads_of(left, keep, send, 2, 1, f32)
        ]

    sends, work, given, take = background(
        own_gradients, (dp_keep, dp_send, m_own), x_pieces=2
    )
    if pairs:
        sends.append((swap_group, small))
    moved, made, _ = step([(up, dx_run), (up, out_run), *sends], work, given)
    small = small + moved[-1] if pairs else lax.psum(small, "dp")
    take(moved[2:-1] if pairs else moved[2:], made)
    of_parts = dict(zip(("qk0", "v0"), made))

    def reduced(key):
        x_queue.append((key, (of_parts[key] + landed[key].astype(f32)).astype(bf16)))

    reduced("qk0")
    dx_run = paired(*dx_sum(moved[0], 3)).astype(bf16)
    out_own, out_other = out_sum(moved[1], 0)
    out_own, out_other = (h_own + out_own).astype(bf16), (h_other + out_other).astype(bf16)
    edge = 2 * width
    bound_sum = small[edge : edge + hc]
    wide = jnp.concatenate([small[:edge], small[edge + hc :]])
    near = lambda a: lax.ppermute(a, "col", [(i, i ^ 1) for i in range(count)])
    far = lambda a: lax.ppermute(a, "col", [(i, i ^ 2) for i in range(count)])
    ffn_pieces = [found[f"f{n}"] if pairs else (total(f"f{n}"),) for n in range(4)]
    each = len(ffn_pieces[0])

    def whole_ffn(*given):
        return [
            halves_of_rows([given[n * each : (n + 1) * each] for n in range(4)], 2)
        ]

    sends, _, _, take = background(x_pieces=2)
    moved, (ffn_whole,), _ = step(
        [(up, dx_run), (near, wide), (swap_chip, out_other), *sends],
        whole_ffn,
        [array for found_piece in ffn_pieces for array in found_piece],
    )
    wide = wide + moved[1]
    out_other = moved[2]
    take(moved[3:], [])
    reduced("v0")
    dx_own, dx_other = dx_sum(moved[0], 0)

    w_o, w_p = dx_own * mix_gain, dx_other * gains_other[0]
    along = jnp.sum(w_o * x_own, axis=1) + jnp.sum(w_p * x_other, axis=1)
    along = along + swap_core(along)
    factor = mix_scale**3 * along[:, None] / D
    gt_own = gh_own + mix_scale * w_o - x_own * factor
    gt_other = gh_other + mix_scale * w_p - x_other * factor
    def two_parts(key):
        arrays = found[key] if pairs else (total(key),)
        return [[array[at : at + width] for array in arrays] for at in (0, width)]

    def one_part(key):
        return list(found[key]) if pairs else [total(key)]

    query, forget = two_parts("qk0")
    most = [query, forget, one_part("g0")]
    counts = [len(part) for part in most]

    def most_of(*given):
        parts = [given[sum(counts[:n]) : sum(counts[: n + 1])] for n in range(3)]
        return [stacked([parts[0], parts[1], (), parts[2]])]

    sends, _, _, take = background(x_pieces=2)
    moved, (mix_whole,), _ = step(
        [(swap_chip, gt_other.astype(bf16)), (far, wide), *sends],
        most_of,
        [array for part in most for array in part],
    )
    grad_other = moved[0].astype(f32)
    wide = wide + moved[1]
    take(moved[2:], [])
    mix_whole = filled(mix_whole, 2, one_part("v0"))
    turned = swap_core(jnp.concatenate([bound_sum, wide[edge:]]))
    grad_bound = joined(bound_sum, turned[:hc], core, 0)

    return (
        joined(out_own, out_other, y, 0),
        joined(gt_own, grad_other, y, 0),
        wide[:width],
        mix_whole,
        grad_bound,
        wide[edge:] + turned[hc:],
        total("o0"),
        wide[width:edge],
        ffn_whole,
        jnp.concatenate([total("d0"), total("d1")], 1),
    )


def solution(mesh):
    return jax.shard_map(
        shards,
        mesh=mesh,
        in_specs=(
            P(("dp", "col"), "row"),
            P("dp"),
            P("row"),
            P("row", None, "col"),
            P("col"),
            P(),
            P("col", "row"),
            P("row"),
            P("row", None, "col"),
            P("col", "row"),
            P(("dp", "col"), "row"),
        ),
        out_specs=(
            P(("dp", "col"), "row"),
            P(("dp", "col"), "row"),
            P("row"),
            P("row", None, "col"),
            P("col"),
            P(),
            P("col", "row"),
            P("row"),
            P("row", None, "col"),
            P("col", "row"),
        ),
        check_vma=False,
    )
```
